32 devices in a mesh: lon: 8 (over y, x, core), lat: 4 (over z).
Axes of the slice: x: 2, y: 2, z: 4, core: 2. Of those that a mesh axis runs over, the one named last changes fastest.
Arguments:
- state: float32 [16, 256, 1024], P(None, 'lat', 'lon'), may hold values from -6 to 6
- land_mask: int32 [256, 1024], P('lat', 'lon'), may hold values from 0 to 1, as said below
- kernel_one: bfloat16 [3, 3, 16, 16], replicated, may hold values from -0.5 to 0.5
- bias_one: float32 [16], replicated, may hold values from -3 to 3
- kernel_two: bfloat16 [3, 3, 16, 16], replicated, may hold values from -0.5 to 0.5
- bias_two: float32 [16], replicated, may hold values from -3 to 3
- kernel_three: bfloat16 [3, 3, 8, 16], replicated, may hold values from -0.5 to 0.5
- bias_three: float32 [8], replicated, may hold values from -3 to 3
Outputs:
- updated: float32 [16, 256, 1024], P(None, 'lat', 'lon')
The draws below stay inside these ranges and needn't reach their ends.
Inputs may be any that keep to these rules, and one draw needn't show every extreme that they name: `land_mask`: 1 marks an ocean cell and 0 land; whole tiles of 64 x 128 cells may be land.
All inputs are finite; a program needn't handle non-finite values.
Results may differ from the reference program's by a relative error of at most 0.0003.
Values sent between devices are 32-bit elements; how exact they have to be, the bound alone decides.
No kernel may reach another device: no remote copies, remote signals or barrier semaphores. Data moves between devices by JAX's collectives and lax.ppermute only.
A program may use at most 128 MiB of HBM per device.

```python
import jax
import jax.numpy as jnp

CLAT = 64
CLON = 128
LEV = 4
HID = 16
STATE = 16
FORCE = 8
NLAT = 256
NLON = 1024


def draw_land_mask(key, part):
    key = jax.random.fold_in(key, 7)
    first, second = jax.random.split(key)
    tiles = jax.random.randint(first, (NLAT // CLAT, NLON // CLON), 0, 4)
    cells = jax.random.randint(second, (NLAT, NLON), 0, 5)
    tile_ocean = (tiles > 0).astype(jnp.int32)
    spread = jnp.repeat(jnp.repeat(tile_ocean, CLAT, axis=0), CLON, axis=1)
    return (cells > 0).astype(jnp.int32) * spread


def level_of(rng, dims, shards, low, largest):
    level = 1.0
    for axis_at, blocks in shards:
        draws = jax.random.uniform(jax.random.fold_in(jax.random.fold_in(rng, 6), axis_at), (blocks,), jnp.float32, low / len(shards), largest / len(shards))
        level = level * jnp.repeat(jnp.exp(draws), dims[axis_at] // blocks).reshape((-1,) + (1,) * (len(dims) - 1 - axis_at))
    return level


def noise(rng, dims, scale, reach, cuts=(), held_as=jnp.bfloat16):
    result = jax.random.normal(rng, dims, jnp.float32) * scale
    if len(cuts) > 0:
        result = level_of(rng, dims, cuts, -0.22, 0.18) * result
    return jnp.clip(result, min=-reach, max=reach).astype(held_as)


def setup_inputs(seed: int = 0) -> dict:
    streams_of = jax.random.split(jax.random.key(seed), 9)
    return {
        "state": noise(streams_of[0], (STATE, NLAT, NLON), 1.0, 6.0, ((1, 4), (2, 8)), jnp.float32),
        "land_mask": draw_land_mask(jax.random.fold_in(streams_of[8], 71), 0),
        "kernel_one": noise(streams_of[2], (3, 3, HID, STATE), (9 * STATE) ** -0.5, 0.5),
        "bias_one": noise(streams_of[3], (HID,), 0.5, 3.0, (), jnp.float32),
        "kernel_two": noise(streams_of[4], (3, 3, HID, HID), (9 * HID) ** -0.5, 0.5),
        "bias_two": noise(streams_of[5], (HID,), 0.5, 3.0, (), jnp.float32),
        "kernel_three": noise(streams_of[6], (3, 3, FORCE, HID), (9 * HID) ** -0.5, 0.5),
        "bias_three": noise(streams_of[7], (FORCE,), 0.5, 3.0, (), jnp.float32),
    }


def conv(x, kernel, bias):
    rows = x.shape[1] - 2
    cols = x.shape[2] - 2
    xf = x.astype(jnp.float32)
    kf = kernel.astype(jnp.float32)
    total = jnp.zeros((kernel.shape[2], rows, cols), jnp.float32) + bias[:, None, None]
    for a in range(3):
        for c in range(3):
            total = total + jnp.einsum("ok,khw->ohw", kf[a, c], xf[:, a:a + rows, c:c + cols])
    return total


def reference(state, land_mask, kernel_one, bias_one, kernel_two, bias_two, kernel_three, bias_three):
    channels = state.shape[0]
    lon_padded = jnp.concatenate([state[:, :, -3:], state, state[:, :, :3]], axis=2)
    sign = jnp.where(jnp.arange(channels) < 2 * LEV, -1.0, 1.0).astype(jnp.float32)
    fold = lon_padded[:, NLAT - 3:, :][:, ::-1, ::-1] * sign[:, None, None]
    south = jnp.zeros((channels, 3, NLON + 6), jnp.float32)
    padded = jnp.concatenate([south, lon_padded, fold], axis=1)
    layer_in = padded.astype(jnp.bfloat16)
    hidden_one = jax.nn.silu(conv(layer_in, kernel_one, bias_one)).astype(jnp.bfloat16)
    hidden_two = jax.nn.silu(conv(hidden_one, kernel_two, bias_two)).astype(jnp.bfloat16)
    forcing = conv(hidden_two, kernel_three, bias_three)
    centre = padded[:, 3:-3, 3:-3]
    east = padded[:, 3:-3, 4:-2]
    west = padded[:, 3:-3, 2:-4]
    north = padded[:, 4:-2, 3:-3]
    south_cells = padded[:, 2:-4, 3:-3]
    speed_u = jnp.tile(centre[0:LEV], (4, 1, 1))
    speed_v = jnp.tile(centre[LEV:2 * LEV], (4, 1, 1))
    tendency = -0.5 * (speed_u * (east - west) + speed_v * (north - south_cells))
    tendency = tendency + 0.2 * (east + west + north + south_cells - 4.0 * centre)
    extra = jnp.concatenate([forcing, jnp.zeros((channels - forcing.shape[0], NLAT, NLON), jnp.float32)], axis=0)
    tendency = tendency + extra
    ocean = land_mask.astype(jnp.float32)
    return state + 0.1 * ocean[None, :, :] * tendency
```

```python
import functools

import jax
import jax.numpy as jnp
from jax import lax
from jax.experimental import pallas as pl
from jax.experimental.pallas import tpu as pltpu
from jax.sharding import PartitionSpec as P

F32 = jnp.float32
BF16 = jnp.bfloat16

ROWS = 64
PITCH = 72
BLOCK = 8
DEPTH = 512
SPAN = (BLOCK + 2) * 16
VMEM = pl.BlockSpec(memory_space=pltpu.VMEM)
HBM = pl.BlockSpec(memory_space=pltpu.HBM)
LIMIT = 40 * 2**20


def lanes():
    return lax.broadcasted_iota(jnp.int32, (8, 128), 1)


def turn(x, by):
    if isinstance(by, int):
        by = by % 128
        if by == 0:
            return x
    return pltpu.roll(x, by, x.ndim - 1)


def silu(v):
    half = 0.5 * v
    return half + half * jnp.tanh(half)


def dot(weights, x):
    return jnp.dot(weights, x, preferred_element_type=F32)


def even_place(axis):
    return lax.rem(lax.axis_index(axis), 2) == 0


def sides(inner, outer):
    even = even_place("lon")
    return (
        [jnp.where(even, inner[i], outer[i]) for i in range(4)],
        [jnp.where(even, outer[i], inner[i]) for i in range(4)],
    )


def tendency(q, north, south, east, west):
    sub = lax.broadcasted_iota(jnp.int32, (8, 128), 0)
    swapped = pltpu.roll(q[0], 4, 0)
    u = jnp.where(sub < 4, q[0], swapped)
    v = jnp.where(sub < 4, swapped, q[0])
    result = []
    for e, w, n, s, x in zip(east, west, north, south, q):
        total = -0.5 * (u * (e - w) + v * (n - s))
        result.append(total + 0.2 * (e + w + n + s - 4.0 * x))
    return result


def beside(e, e_at, w, w_at):
    return jnp.where(lanes() < 64, turn(e, -e_at), turn(w, 125 - w_at))


def turn_wide(x, c):
    return pltpu.roll(x, (1 - c) % 256, 1) if c != 1 else x


def spread(rows, width):
    blank = jnp.zeros((16, 2 * width), BF16)
    result = []
    for c in range(3):
        for row in rows:
            parts = [turn_wide(row[:, at : at + 256], c)[:, 0:width] for at in (0, 256)]
            result.append(jnp.concatenate(parts, axis=1))
        result.extend([blank] * ((BLOCK + 2 if c < 2 else BLOCK + 4) - len(rows)))
    return jnp.concatenate(result, axis=0)


def prepare_kernel(state_ref, *refs):
    others, refs = refs[0:7], refs[7:]
    rows_ref, strip_ref, outer_ref, inner_ref, *held, cells_ref, sems = refs
    fetches = []
    for at in range(0, 16, 2):
        span = pl.ds(at, 2)
        target = cells_ref.at[span, pl.ds(0, ROWS), :]
        fetches.append(pltpu.make_async_copy(state_ref.at[span], target, sems.at[len(fetches)]))
    for source, target in zip(others, held):
        fetches.append(pltpu.make_async_copy(source, target, sems.at[len(fetches)]))
    for fetch in fetches:
        fetch.start()

    flat = cells_ref.reshape(16 * PITCH, 128)
    group = lanes() // 16
    part = (lanes() % 16) // 4
    even = even_place("lon")
    shifts = [
        [jnp.where(even, (4 * s - a) % 128, (4 * s - b) % 128) for s in range(4)]
        for a, b in ((6, 3), (3, 6))
    ]
    for fetch in fetches[0:8]:
        fetch.wait()
    for half in range(2):
        strip = [jnp.zeros((8, 128), F32)] * 8
        for b in range(8):
            for r in range(8):
                x = flat[pl.ds(8 * PITCH * half + 8 * b + r, 8, stride=PITCH), :]
                rows_ref[8 * b + r, half] = x
                strip[r] = jnp.where(group == b, turn(x, 6 + 16 * b), strip[r])
        for r in range(8):
            strip_ref[r, half] = strip[r]
        for target, shift in zip((outer_ref, inner_ref), shifts):
            for q in range(2):
                value = jnp.zeros((8, 128), F32)
                for s in range(4):
                    value = jnp.where(part == s, turn(strip[4 * q + s], shift[s]), value)
                target[2 * q + half] = value
    for fetch in fetches[8:]:
        fetch.wait()


def prepare(state, others):
    block = jax.ShapeDtypeStruct
    arrays = [pltpu.with_memory_space_constraint(x, pltpu.HBM) for x in (state, *others)]
    return pl.pallas_call(
        prepare_kernel,
        out_shape=[
            block((ROWS, 2, 8, 128), F32),
            block((8, 2, 8, 128), F32),
            block((4, 8, 128), F32),
            block((4, 8, 128), F32),
            *[block(x.shape, x.dtype) for x in others],
        ],
        in_specs=[HBM] * 8,
        out_specs=[VMEM] * 11,
        scratch_shapes=[pltpu.VMEM((16, PITCH, 128), F32), pltpu.SemaphoreType.DMA((15,))],
        compiler_params=pltpu.CompilerParams(vmem_limit_bytes=LIMIT),
        cost_estimate=pl.CostEstimate(flops=400000, bytes_accessed=1200000, transcendentals=0),
        name="rows_edges",
    )(*arrays)


def corners_kernel(size, rows_ref, outer_ref, inner_ref, north_ref, first_ref, second_ref):
    lat = lax.axis_index("lat")
    even = lax.rem(lat, 2) == 0
    for t in range(3):
        for half in range(2):
            at = 2 * t + half
            low = rows_ref[t, half]
            first_ref[at] = jnp.where(even, north_ref[at], low)
            second_ref[at] = jnp.where(even, low, north_ref[at])
    top = lat == size - 1
    col = lanes()
    part = col // 16
    straight = even_place("lon")
    mirrored = straight != top
    index = jnp.where(top, 112 + 4 * (3 - col // 4 % 4) + 2 - col % 4, 112 + col % 16)
    low = high = jnp.zeros((8, 128), F32)
    for i in range(4):
        half = i // 2
        pair = (inner_ref, outer_ref) if i % 2 == 0 else (outer_ref, inner_ref)
        x = jnp.where(straight, pair[0][half], pair[1][half])
        low = jnp.where(part == i, turn(x, 16 * i), low)
        x = jnp.where(mirrored, pair[0][2 + half], pair[1][2 + half])
        high = jnp.where(part == i, jnp.take_along_axis(x, index, axis=1), high)
    high = jnp.where(top & (col < 32), -high, high)
    first_ref[6] = jnp.where(even, high, low)
    second_ref[6] = jnp.where(even, low, high)


def corners(size, rows, inner, outer, north):
    return pl.pallas_call(
        functools.partial(corners_kernel, size),
        out_shape=[jax.ShapeDtypeStruct((7, 8, 128), F32)] * 2,
        in_specs=[VMEM] * 4,
        out_specs=[VMEM] * 2,
        compiler_params=pltpu.CompilerParams(vmem_limit_bytes=LIMIT),
        cost_estimate=pl.CostEstimate(flops=1000, bytes_accessed=100000, transcendentals=0),
        name="add_corners",
    )(rows, outer, inner, north)


def band(kernel_ref, wide_ref, target_ref):
    n = kernel_ref.shape[2]
    wide_ref[...] = jnp.zeros_like(wide_ref)
    tiles = [None] * (DEPTH // 128)
    for c in range(3):
        for a in range(3):
            wide_ref[3 * c + a, :, 0:16] = kernel_ref[a, c].astype(wide_ref.dtype)
            tile, off = divmod(SPAN * c + 16 * a, 128)
            x = turn(wide_ref[3 * c + a], off)
            tiles[tile] = x if tiles[tile] is None else tiles[tile] + x
    blank = jnp.zeros((n, 128), wide_ref.dtype)
    first = jnp.concatenate([blank if x is None else x for x in tiles], axis=1)
    rows = [first] + [pltpu.roll(first, 16 * r, 1) for r in range(1, BLOCK)]
    for r in range(0, BLOCK, 16 // n):
        target_ref[n * r : n * r + 16, :] = jnp.concatenate(rows[r : r + 16 // n], axis=0).astype(BF16)


def band_compact(wide_ref, target_ref, slots, outs):
    n = wide_ref.shape[1]
    tiles = [jnp.zeros((n, 128), wide_ref.dtype)] * (target_ref.shape[1] // 128)
    for c in range(3):
        for a in range(3):
            tile, off = divmod(16 * slots * c + 16 * a, 128)
            tiles[tile] = tiles[tile] + turn(wide_ref[3 * c + a], off)
    first = jnp.concatenate(tiles, axis=1)
    rows = [pltpu.roll(first, 16 * r, 1) if r else first for r in range(outs)]
    rows = rows + [jnp.zeros_like(first)] * (target_ref.shape[0] // n - outs)
    for r in range(0, len(rows), 16 // n):
        target_ref[n * r : n * r + 16, :] = jnp.concatenate(rows[r : r + 16 // n], axis=0).astype(BF16)


def main_kernel(
    size, rows_ref, mask_ref, k_one_ref, k_two_ref, k_three_ref, b_one_ref, b_two_ref, b_three_ref,
    out_ref, north_ref, ocean_ref, one_ref, two_ref, three_ref,
    late_one_ref, late_two_ref, late_three_ref, bias_ref,
    wide_ref, narrow_ref, first_ref, second_ref, third_ref,
):
    top = lax.axis_index("lat") == size - 1
    col = lanes()
    for t in range(3):
        for half in range(2):
            folded = jnp.take_along_axis(rows_ref[ROWS - 1 - t, half], 127 - col, axis=1)
            folded = -folded if half == 0 else folded
            north_ref[2 * t + half] = jnp.where(top, folded, rows_ref[ROWS - 3 + t, half])
    ocean = jnp.zeros((8, 128), F32)
    for b in range(8):
        x = 0.1 * mask_ref[8 * b : 8 * b + 8, :].astype(F32)
        ocean = jnp.where(col // 16 == b, turn(x, 6 + 16 * b), ocean)
    ocean_ref[...] = ocean

    biases = []
    at = 0
    for ref in (b_one_ref, b_two_ref, b_three_ref):
        n = ref.shape[1]
        same = lax.broadcasted_iota(jnp.int32, (n, n), 0) == lax.broadcasted_iota(jnp.int32, (n, n), 1)
        column = jnp.sum(jnp.where(same, ref[...], 0.0), axis=1, keepdims=True)
        biases.append(jnp.broadcast_to(column, (n, 128)))
        bias_ref[at : at + n, :] = biases[-1]
        at += n
    band(k_one_ref, wide_ref.at[0], one_ref)
    band(k_two_ref, wide_ref.at[1], two_ref)
    band(k_three_ref, narrow_ref, three_ref)
    band_compact(wide_ref.at[0], late_one_ref, 5, 3)
    band_compact(wide_ref.at[1], late_two_ref, 7, 5)
    band_compact(narrow_ref, late_three_ref, 5, 3)
    for ref in (first_ref, second_ref, third_ref):
        for c in range(3):
            for row in (0, ROWS + 1, ROWS + 2, ROWS + 3):
                ref[c, row] = jnp.zeros((16, 128), BF16)

    for row in range(ROWS):
        x = jnp.concatenate([rows_ref[row, 0], rows_ref[row, 1]], axis=0).astype(BF16)
        for c in range(3):
            first_ref[c, row + 1] = turn(x, 1 - c)

    def layer(source, weights, at):
        parts = []
        for start in (at, at + ROWS // 2):
            for c in range(3):
                count = BLOCK + 2 if c < 2 else BLOCK + 4
                parts.append(source[c, start : start + count].reshape(16 * count, 128))
        x = jnp.concatenate(
            [jnp.concatenate(parts[0:3], axis=0), jnp.concatenate(parts[3:6], axis=0)], axis=1
        )
        return dot(weights[...], x)

    for source, weights, bias, target in (
        (first_ref, one_ref, biases[0], second_ref),
        (second_ref, two_ref, biases[1], third_ref),
    ):
        bias = jnp.concatenate([bias, bias], axis=1)
        for at in range(0, ROWS // 2, BLOCK):
            total = layer(source, weights, at).reshape(BLOCK, 16, 256)
            value = silu(total + bias[None]).astype(BF16).reshape(16 * BLOCK, 256)
            for part in range(2):
                start = at + ROWS // 2 * part + 1
                x = value[:, 128 * part : 128 * part + 128]
                for c in range(3):
                    target[c, start : start + BLOCK] = turn(x, 1 - c).reshape(BLOCK, 16, 128)

    bias = jnp.concatenate([biases[2], biases[2]], axis=1)
    for at in range(0, ROWS // 2, BLOCK):
        forcing = layer(third_ref, three_ref, at).reshape(BLOCK, 8, 256) + bias[None]
        for part in range(2):
            for r in range(BLOCK):
                row = at + ROWS // 2 * part + r
                near = [min(max(row + d, 0), ROWS - 1) for d in (0, 1, -1)]
                q, north, south = [[rows_ref[i, half] for half in range(2)] for i in near]
                east = [turn(x, -1) for x in q]
                west = [turn(x, 1) for x in q]
                new = tendency(q, north, south, east, west)
                new[0] = new[0] + forcing[r, :, 128 * part : 128 * part + 128]
                ocean = 0.1 * mask_ref[row : row + 1, :].astype(F32)
                for half in range(2):
                    out_ref[row, half] = q[half] + ocean * new[half]


def main_pass(size, rows, mask, parameters):
    taps = pltpu.VMEM((3, ROWS + 4, 16, 128), BF16)
    block = jax.ShapeDtypeStruct
    return pl.pallas_call(
        functools.partial(main_kernel, size),
        out_shape=[
            block(rows.shape, F32),
            block((6, 8, 128), F32),
            block((8, 128), F32),
            *[block((n, DEPTH), BF16) for n in (128, 128, 64)],
            *[block(shape, BF16) for shape in ((48, 256), (80, 384), (32, 256))],
            block((40, 128), F32),
        ],
        in_specs=[VMEM] * 8,
        out_specs=[VMEM] * 10,
        scratch_shapes=[
            pltpu.VMEM((2, 9, 16, 128), BF16),
            pltpu.VMEM((9, 8, 128), F32),
            *[taps] * 3,
        ],
        compiler_params=pltpu.CompilerParams(vmem_limit_bytes=LIMIT),
        cost_estimate=pl.CostEstimate(
            flops=150000000, bytes_accessed=1500000, transcendentals=300000
        ),
        name="main_pass",
    )(rows, mask, *parameters)


def taps(rows, count):
    blank = jnp.zeros_like(rows[0])
    result = []
    for c in range(3):
        for row in rows:
            width = row.shape[1] // 128
            parts = [turn(row[:, 128 * i : 128 * i + 128], 1 - c) for i in range(width)]
            result.append(jnp.concatenate(parts, axis=1) if width > 1 else parts[0])
        result.extend([blank] * ((BLOCK + 2 if c < 2 else BLOCK + 4) - len(rows)))
    return jnp.concatenate(result, axis=0)


def strip_kernel(
    rows_ref, strip_ref, outer_ref, inner_ref, main_ref, ocean_ref, one_ref, two_ref, three_ref,
    bias_ref, cells_ref, low_ref, high_ref, side_ref, pre_ref, hidden_ref,
):
    east, west = sides(inner_ref, outer_ref)
    col = lanes()
    at = col % 16
    cells = []
    for r in range(8):
        pair = [[], []]
        for half in range(2):
            block = 2 * (r // 4) + half
            own = strip_ref[r, half]
            pair[0].append(jnp.where(at < 6, own, turn(east[block], 6 - 4 * (r % 4))))
            pair[1].append(jnp.where(at < 3, turn(west[block], -4 * (r % 4)), turn(own, -3)))
        cells.append(pair)

    def moved(pair, by):
        return [[turn(x, by) for x in part] for part in pair]

    cells = [moved(x, 16) for x in cells[5:8]] + cells + [moved(x, -16) for x in cells[0:3]]
    rows = []
    for pair in cells:
        parts = [jnp.concatenate(part, axis=0) for part in pair]
        rows.append(jnp.concatenate(parts, axis=1).astype(BF16))

    for weights, bias_at in ((one_ref, 0), (two_ref, 16)):
        count = len(rows) - 2 - BLOCK
        bias = jnp.concatenate([bias_ref[bias_at : bias_at + 16, :]] * 2, axis=1)
        low = dot(weights[...], taps(rows[0:10], 256)).reshape(BLOCK, 16, 256)
        high = dot(weights[0 : 16 * count, :], taps(rows[BLOCK:], 256)).reshape(count, 16, 256)
        low = silu(low + bias[None]).astype(BF16)
        high = silu(high + bias[None]).astype(BF16)
        rows = [low[i] for i in range(BLOCK)] + [high[i] for i in range(count)]
    forcing = dot(three_ref[...], taps(rows, 256)).reshape(BLOCK, 8, 256)
    forcing = forcing + jnp.concatenate([bias_ref[32:40, :]] * 2, axis=1)[None]

    both = []
    for r in range(8):
        new = []
        for part in range(2):
            q, north, south = [cells[i][part] for i in (r + 3, r + 4, r + 2)]
            value = tendency(
                q, north, south, [turn(x, -1) for x in q], [turn(x, 1) for x in q]
            )
            value[0] = value[0] + forcing[r, :, 128 * part : 128 * part + 128]
            new.append(value)
        ocean = ocean_ref[r : r + 1, :]
        value = [jnp.where(at < 6, new[0][half], turn(new[1][half], 3)) for half in range(2)]
        both.append([strip_ref[r, half] + ocean * value[half] for half in range(2)])

    edge = (col < 3) | (col >= 125)
    for b in range(8):
        ref, start = (low_ref, 0) if b == 0 else (high_ref, 0) if b == 7 else (cells_ref, 8 * b - 8)
        pitch = ref.shape[1]
        flat = ref.reshape(16 * pitch, 128)
        for r in range(8):
            for half in range(2):
                value = turn(both[r][half], -(16 * b + 6))
                value = jnp.where(edge, value, main_ref[8 * b + r, half])
                flat[pl.ds(8 * pitch * half + start + r, 8, stride=pitch), :] = value


    def own(row):
        start = 16 * (row // 8) + 4 * (row % 4)
        block = 2 * (row % 8 // 4)
        return [beside(east[block + h], start, west[block + h], start) for h in range(2)]

    own_rows = []
    for row in list(range(6)) + list(range(ROWS - 6, ROWS)):
        side = own(row)
        at = row if row < 3 else row - ROWS + 6
        if row < 3 or row >= ROWS - 3:
            for half in range(2):
                side_ref[at, half] = side[half]
        parts = [
            jnp.concatenate([rows_ref[row, 0], rows_ref[row, 1]], axis=0),
            jnp.concatenate(side, axis=0),
        ]
        own_rows.append(jnp.concatenate(parts, axis=1).astype(BF16))
    blank = jnp.zeros((16, 256), BF16)
    low = [blank] * 3 + own_rows[0:6]
    high = own_rows[6:12] + [blank] * 3
    rows = [jnp.concatenate(pair, axis=1) for pair in zip(low, high)]
    total = dot(one_ref[0:112, :], spread(rows, 256)).reshape(7, 16, 512)
    total = total + jnp.concatenate([bias_ref[0:16, :]] * 4, axis=1)[None]
    for r in range(3):
        pre_ref[r] = jnp.concatenate([total[r, :, 0:256], total[4 + r, :, 256:512]], axis=1)
    for r in range(4):
        for strip, x in enumerate((total[3 + r, :, 0:256], total[r, :, 256:512])):
            value = silu(x).astype(BF16)
            for c in range(3):
                hidden_ref[strip, c, r] = turn_wide(value, c)


def strip_pass(rows, strip, inner, outer, main, ocean, weights, bias):
    block = jax.ShapeDtypeStruct
    return pl.pallas_call(
        strip_kernel,
        out_shape=[
            block((16, ROWS - 8, 128), F32),
            *[block((16, 8, 128), F32)] * 2,
            block((6, 2, 8, 128), F32),
            block((3, 16, 512), F32),
            block((2, 3, 4, 16, 256), BF16),
        ],
        in_specs=[VMEM] * 10,
        out_specs=[VMEM] * 6,
        compiler_params=pltpu.CompilerParams(vmem_limit_bytes=LIMIT),
        cost_estimate=pl.CostEstimate(
            flops=150000000, bytes_accessed=2000000, transcendentals=100000
        ),
        name="strip_pass",
    )(rows, strip, outer, inner, main, ocean, *weights, bias)


def border_kernel(
    rows_ref, mask_ref, first_ref, second_ref, side_ref, pre_ref, hidden_ref, one_ref, two_ref,
    three_ref, bias_ref, cells_ref, low_in_ref, high_in_ref, out_ref, low_ref, high_ref, sems,
):
    lat = lax.axis_index("lat")
    even = lax.rem(lat, 2) == 0
    span = pl.ds(8, ROWS - 16)
    source = cells_ref.at[:, pl.ds(0, ROWS - 16), :]
    stores = [pltpu.make_async_copy(source, out_ref.at[:, span, :], sems.at[0])]
    stores[0].start()

    south, north = [], []
    low, high = [], []
    for t in range(3):
        blocks = [[], [], [], []]
        for half in range(2):
            at = 2 * t + half
            corner = jnp.where(even, second_ref[6], first_ref[6])
            x = jnp.where(even, second_ref[at], first_ref[at])
            y = beside(corner, 32 * half + 4 + 4 * t, corner, 32 * half + 20 + 4 * t)
            blocks[0].append(jnp.where(lat == 0, 0.0, x))
            blocks[1].append(jnp.where(lat == 0, 0.0, y))
            corner = jnp.where(even, first_ref[6], second_ref[6])
            blocks[2].append(jnp.where(even, first_ref[at], second_ref[at]))
            blocks[3].append(beside(corner, 32 * half + 4 * t, corner, 32 * half + 16 + 4 * t))
        south.append(blocks[0])
        north.append(blocks[2])
        wide = [jnp.concatenate(x, axis=0) for x in blocks]
        low.append(jnp.concatenate(wide[0:2], axis=1).astype(BF16))
        high.append(jnp.concatenate(wide[2:4], axis=1).astype(BF16))

    blank = jnp.zeros((16, 256), BF16)
    operand = []
    for c in range(3):
        lows = [turn_wide(x, c) for x in low] + [blank] * 2
        highs = [blank] * 2 + [turn_wide(x, c) for x in high]
        operand.extend(jnp.concatenate(pair, axis=1) for pair in zip(lows, highs))
    operand.append(jnp.zeros((16, 512), BF16))
    total = dot(one_ref[...], jnp.concatenate(operand, axis=0)).reshape(3, 16, 512)
    late = silu(total + pre_ref[...]).astype(BF16)

    operand = []
    for c in range(3):
        lows = [turn_wide(late[r, :, 0:256], c) for r in range(3)]
        lows = lows + [hidden_ref[0, c, r] for r in range(4)]
        highs = [hidden_ref[1, c, r] for r in range(4)]
        highs = highs + [turn_wide(late[r, :, 256:512], c) for r in range(3)]
        operand.extend(jnp.concatenate(pair, axis=1) for pair in zip(lows, highs))
    operand.extend([jnp.zeros((16, 512), BF16)] * 3)
    total = dot(two_ref[...], jnp.concatenate(operand, axis=0)).reshape(5, 16, 512)
    value = silu(total + jnp.concatenate([bias_ref[16:32, :]] * 4, axis=1)[None]).astype(BF16)
    operand = []
    for c in range(3):
        for r in range(5):
            parts = [turn_wide(value[r, :, at : at + 256], c)[:, 0:128] for at in (0, 256)]
            operand.append(jnp.concatenate(parts, axis=1))
    operand.append(jnp.zeros((16, 256), BF16))
    total = dot(three_ref[...], jnp.concatenate(operand, axis=0)).reshape(4, 8, 256)
    total = total + jnp.concatenate([bias_ref[32:40, :]] * 2, axis=1)[None]

    col = lanes()
    own = {row: [rows_ref[row, half] for half in range(2)] for row in (0, 1, 2, 3, 60, 61, 62, 63)}
    own[-1], own[ROWS] = south[2], north[0]
    for strip in range(2):
        ref, at = ((low_ref, 0), (high_ref, ROWS - 8))[strip]
        flat = ref.reshape(128, 128)
        for t in range(3):
            row = t if strip == 0 else ROWS - 3 + t
            q = own[row]
            side = [side_ref[3 * strip + t, half] for half in range(2)]
            ocean = 0.1 * mask_ref[row : row + 1, :].astype(F32)
            e = [turn(jnp.where(col == 0, y, x), -1) for x, y in zip(q, side)]
            w = [turn(jnp.where(col == 127, y, x), 1) for x, y in zip(q, side)]
            new = tendency(q, own[row + 1], own[row - 1], e, w)
            new[0] = new[0] + total[t, :, 128 * strip : 128 * strip + 128]
            for half in range(2):
                flat[pl.ds(64 * half + row - at, 8, stride=8), :] = q[half] + ocean * new[half]
        store = pltpu.make_async_copy(ref, out_ref.at[:, pl.ds(at, 8), :], sems.at[1 + strip])
        store.start()
        stores.append(store)
    for store in stores:
        store.wait()


def border_pass(rows, mask, first, second, side, pre, hidden, late, bias, cells, low, high):
    block = jax.ShapeDtypeStruct
    out, _, _ = pl.pallas_call(
        border_kernel,
        out_shape=[block((16, ROWS, 128), F32), block(low.shape, F32), block(high.shape, F32)],
        in_specs=[VMEM] * 14,
        out_specs=[HBM, VMEM, VMEM],
        scratch_shapes=[pltpu.SemaphoreType.DMA((3,))],
        input_output_aliases={12: 1, 13: 2},
        compiler_params=pltpu.CompilerParams(vmem_limit_bytes=LIMIT),
        cost_estimate=pl.CostEstimate(flops=60000000, bytes_accessed=1000000, transcendentals=60000),
        name="border_pass",
    )(rows, mask, first, second, side, pre, hidden, *late, bias, cells, low, high)
    return out


def shards(state, land_mask, kernel_one, bias_one, kernel_two, bias_two, kernel_three, bias_three):
    lon, lat = (lax.axis_size("lon"), lax.axis_size("lat"))
    biases = [x.reshape(1, x.shape[0]) for x in (bias_one, bias_two, bias_three)]
    rows, strip, outer, inner, mask, *parameters = prepare(
        state, (land_mask, kernel_one, kernel_two, kernel_three, *biases)
    )

    inner = lax.ppermute(inner, "lon", [(i, i + 1 - 2 * (i % 2)) for i in range(lon)])
    outer = lax.ppermute(outer, "lon", [(i, (i + 1 if i % 2 else i - 1) % lon) for i in range(lon)])
    main, north, ocean, *weights, bias = main_pass(lat, rows, mask, parameters)
    weights, late = weights[0:3], weights[3:6]

    def pairs(parity):
        result = []
        for i in range(lon):
            for j in range(parity, lat - 1, 2):
                result += [(i * lat + j, i * lat + j + 1), (i * lat + j + 1, i * lat + j)]
            if parity == 1:
                result.append((i * lat, (i + 1 - 2 * (i % 2)) * lat))
            if (lat - 1) % 2 == parity:
                result.append((i * lat + lat - 1, (lon - 1 - i) * lat + lat - 1))
        return result

    first, second = corners(lat, rows, inner, outer, north)
    first = lax.ppermute(first, ("lon", "lat"), pairs(0))
    second = lax.ppermute(second, ("lon", "lat"), pairs(1))
    cells, low, high, *own = strip_pass(
        rows, strip, inner, outer, main, ocean, weights, bias
    )
    return border_pass(rows, mask, first, second, *own, late, bias, cells, low, high)


def solution(mesh):
    return jax.shard_map(
        shards,
        mesh=mesh,
        in_specs=(P(None, "lat", "lon"), P("lat", "lon"), P(), P(), P(), P(), P(), P()),
        out_specs=P(None, "lat", "lon"),
        check_vma=False,
    )
```

```python
import functools

import jax
import jax.numpy as jnp
from jax import lax
from jax.experimental import pallas as pl
from jax.experimental.pallas import tpu as pltpu
from jax.sharding import PartitionSpec as P

F32 = jnp.float32
BF16 = jnp.bfloat16

ROWS = 64
PITCH = 72
BLOCK = 8
DEPTH = 512
SPAN = (BLOCK + 2) * 16
VMEM = pl.BlockSpec(memory_space=pltpu.VMEM)
HBM = pl.BlockSpec(memory_space=pltpu.HBM)
LIMIT = 40 * 2**20


def lanes():
    return lax.broadcasted_iota(jnp.int32, (8, 128), 1)


def turn(x, by):
    if isinstance(by, int):
        by = by % 128
        if by == 0:
            return x
    return pltpu.roll(x, by, x.ndim - 1)


def silu(v):
    half = 0.5 * v
    return half + half * jnp.tanh(half)


def dot(weights, x):
    return jnp.dot(weights, x, preferred_element_type=F32)


def even_place(axis):
    return lax.rem(lax.axis_index(axis), 2) == 0


def sides(inner, outer):
    even = even_place("lon")
    return (
        [jnp.where(even, inner[i], outer[i]) for i in range(4)],
        [jnp.where(even, outer[i], inner[i]) for i in range(4)],
    )


def tendency(q, north, south, east, west):
    sub = lax.broadcasted_iota(jnp.int32, (8, 128), 0)
    swapped = pltpu.roll(q[0], 4, 0)
    u = jnp.where(sub < 4, q[0], swapped)
    v = jnp.where(sub < 4, swapped, q[0])
    result = []
    for e, w, n, s, x in zip(east, west, north, south, q):
        total = -0.5 * (u * (e - w) + v * (n - s))
        result.append(total + 0.2 * (e + w + n + s - 4.0 * x))
    return result


def beside(e, e_at, w, w_at):
    return jnp.where(lanes() < 64, turn(e, -e_at), turn(w, 125 - w_at))


def turn_wide(x, c):
    return pltpu.roll(x, (1 - c) % 256, 1) if c != 1 else x


def spread(rows, width):
    blank = jnp.zeros((16, 2 * width), BF16)
    result = []
    for c in range(3):
        for row in rows:
            parts = [turn_wide(row[:, at : at + 256], c)[:, 0:width] for at in (0, 256)]
            result.append(jnp.concatenate(parts, axis=1))
        result.extend([blank] * ((BLOCK + 2 if c < 2 else BLOCK + 4) - len(rows)))
    return jnp.concatenate(result, axis=0)


def small_kernel(
    state_ref, b_one_ref, b_two_ref, b_three_ref,
    cells_ref, outer_ref, inner_ref, h_one_ref, h_two_ref, h_three_ref, sems,
):
    pairs = []
    for at, count in ((0, 8), (ROWS - 8, 8), (8, ROWS - 16)):
        piece = (slice(None), pl.ds(at, count), slice(None))
        pairs.append((state_ref.at[piece], cells_ref.at[piece]))
    pairs += [(b_one_ref, h_one_ref), (b_two_ref, h_two_ref), (b_three_ref, h_three_ref)]
    fetches = [
        pltpu.make_async_copy(source, target, sems.at[i]) for i, (source, target) in enumerate(pairs)
    ]
    for fetch in fetches:
        fetch.start()
    even = even_place("lon")
    for fetch in fetches[0:2]:
        fetch.wait()

    flat = cells_ref.reshape(16 * PITCH, 128)
    part = lanes() // 4
    outer = inner = jnp.zeros((8, 128), F32)
    for high in range(2):
        for half in range(2):
            for s in range(3):
                row = s + (ROWS - 3) * high
                x = flat[pl.ds(8 * PITCH * half + row, 8, stride=PITCH), :]
                at = 64 * high + 32 * half + 4 * s
                first, last = at, (at - 125) % 128
                by = jnp.where(even, first, last)
                outer = jnp.where(part == at // 4, turn(x, by), outer)
                by = jnp.where(even, last, first)
                inner = jnp.where(part == at // 4, turn(x, by), inner)
    outer_ref[...] = outer
    inner_ref[...] = inner
    for fetch in fetches[2:]:
        fetch.wait()


def small_edges(state, biases):
    block = jax.ShapeDtypeStruct
    arrays = [pltpu.with_memory_space_constraint(x, pltpu.HBM) for x in (state, *biases)]
    return pl.pallas_call(
        small_kernel,
        out_shape=[
            block((16, PITCH, 128), F32),
            block((8, 128), F32),
            block((8, 128), F32),
            *[block(x.shape, F32) for x in biases],
        ],
        in_specs=[HBM] * 4,
        out_specs=[VMEM] * 6,
        scratch_shapes=[pltpu.SemaphoreType.DMA((6,))],
        compiler_params=pltpu.CompilerParams(vmem_limit_bytes=LIMIT),
        cost_estimate=pl.CostEstimate(flops=20000, bytes_accessed=1000000, transcendentals=0),
        name="small_edges",
    )(*arrays)


def rows_kernel(size, cells_ref, rows_ref, strip_ref, outer_ref, inner_ref, north_ref):
    flat = cells_ref.reshape(16 * PITCH, 128)
    group = lanes() // 16
    part = (lanes() % 16) // 4
    even = even_place("lon")
    shifts = [
        [jnp.where(even, (4 * s - a) % 128, (4 * s - b) % 128) for s in range(4)]
        for a, b in ((6, 3), (3, 6))
    ]
    for half in range(2):
        strip = [jnp.zeros((8, 128), F32)] * 8
        for b in range(8):
            for r in range(8):
                x = flat[pl.ds(8 * PITCH * half + 8 * b + r, 8, stride=PITCH), :]
                rows_ref[8 * b + r, half] = x
                strip[r] = jnp.where(group == b, turn(x, 6 + 16 * b), strip[r])
        for r in range(8):
            strip_ref[r, half] = strip[r]
        for target, shift in zip((outer_ref, inner_ref), shifts):
            for q in range(2):
                value = jnp.zeros((8, 128), F32)
                for s in range(4):
                    value = jnp.where(part == s, turn(strip[4 * q + s], shift[s]), value)
                target[2 * q + half] = value

    top = lax.axis_index("lat") == size - 1
    order = jnp.where(top, 127 - lanes(), lanes())
    for t in range(3):
        for half in range(2):
            row = jnp.where(top, ROWS - 1 - t, ROWS - 3 + t)
            x = jnp.take_along_axis(
                flat[pl.ds(8 * PITCH * half + row, 8, stride=PITCH), :], order, axis=1
            )
            north_ref[2 * t + half] = jnp.where(top, -x, x) if half == 0 else x


def rows_edges(size, cells):
    block = jax.ShapeDtypeStruct
    return pl.pallas_call(
        functools.partial(rows_kernel, size),
        out_shape=[
            block((ROWS, 2, 8, 128), F32),
            block((8, 2, 8, 128), F32),
            block((4, 8, 128), F32),
            block((4, 8, 128), F32),
            block((6, 8, 128), F32),
        ],
        in_specs=[VMEM],
        out_specs=[VMEM] * 5,
        compiler_params=pltpu.CompilerParams(vmem_limit_bytes=LIMIT),
        cost_estimate=pl.CostEstimate(flops=400000, bytes_accessed=1200000, transcendentals=0),
        name="rows_edges",
    )(cells)


def corners_kernel(size, rows_ref, outer_ref, inner_ref, north_ref, _, first_ref, second_ref):
    lat = lax.axis_index("lat")
    even = lax.rem(lat, 2) == 0
    for t in range(3):
        for half in range(2):
            at = 2 * t + half
            low = rows_ref[t, half]
            first_ref[at] = jnp.where(even, north_ref[at], low)
            second_ref[at] = jnp.where(even, low, north_ref[at])
    top = lat == size - 1
    col = lanes()
    side = col // 16 % 2
    straight = even_place("lon")
    mirrored = straight != top
    s, j = col // 4 % 4, col % 4
    index = 64 + 32 * (col // 32 % 2) + jnp.where(top, 4 * (2 - s) + 2 - j, 4 * s + j)
    inner, outer = inner_ref[...], outer_ref[...]
    low = jnp.where(side == 0, jnp.where(straight, inner, outer), turn(jnp.where(straight, outer, inner), 16))
    high = [
        jnp.take_along_axis(jnp.where(mirrored, *pair), index, axis=1)
        for pair in ((inner, outer), (outer, inner))
    ]
    high = jnp.where(side == 0, *high)
    high = jnp.where(top & (col < 32), -high, high)
    first_ref[6] = jnp.where(even, high, low)
    second_ref[6] = jnp.where(even, low, high)


def corners(size, rows, inner, outer, north, main):
    return pl.pallas_call(
        functools.partial(corners_kernel, size),
        out_shape=[jax.ShapeDtypeStruct((7, 8, 128), F32)] * 2,
        in_specs=[VMEM] * 4 + [pl.BlockSpec(memory_space=pl.ANY)],
        out_specs=[VMEM] * 2,
        compiler_params=pltpu.CompilerParams(vmem_limit_bytes=LIMIT),
        cost_estimate=pl.CostEstimate(flops=1000, bytes_accessed=100000, transcendentals=0),
        name="add_corners",
    )(rows, outer, inner, north, main)


def band(kernel_ref, wide_ref, target_ref):
    n = kernel_ref.shape[2]
    wide_ref[...] = jnp.zeros_like(wide_ref)
    tiles = [None] * (DEPTH // 128)
    for c in range(3):
        for a in range(3):
            wide_ref[3 * c + a, :, 0:16] = kernel_ref[a, c].astype(wide_ref.dtype)
            tile, off = divmod(SPAN * c + 16 * a, 128)
            x = turn(wide_ref[3 * c + a], off)
            tiles[tile] = x if tiles[tile] is None else tiles[tile] + x
    blank = jnp.zeros((n, 128), wide_ref.dtype)
    first = jnp.concatenate([blank if x is None else x for x in tiles], axis=1)
    rows = [first] + [pltpu.roll(first, 16 * r, 1) for r in range(1, BLOCK)]
    for r in range(0, BLOCK, 16 // n):
        target_ref[n * r : n * r + 16, :] = jnp.concatenate(rows[r : r + 16 // n], axis=0).astype(BF16)


def band_compact(wide_ref, target_ref, slots, outs):
    n = wide_ref.shape[1]
    tiles = [jnp.zeros((n, 128), wide_ref.dtype)] * (target_ref.shape[1] // 128)
    for c in range(3):
        for a in range(3):
            tile, off = divmod(16 * slots * c + 16 * a, 128)
            tiles[tile] = tiles[tile] + turn(wide_ref[3 * c + a], off)
    first = jnp.concatenate(tiles, axis=1)
    rows = [pltpu.roll(first, 16 * r, 1) if r else first for r in range(outs)]
    rows = rows + [jnp.zeros_like(first)] * (target_ref.shape[0] // n - outs)
    for r in range(0, len(rows), 16 // n):
        target_ref[n * r : n * r + 16, :] = jnp.concatenate(rows[r : r + 16 // n], axis=0).astype(BF16)


def layer(source, weights, at):
    halves = []
    for start in (at, at + ROWS // 2):
        parts = []
        for c in range(3):
            count = BLOCK + 2 if c < 2 else BLOCK + 4
            parts.append(source[c, start : start + count].reshape(16 * count, 128))
        halves.append(jnp.concatenate(parts, axis=0))
    return dot(weights[...], jnp.concatenate(halves, axis=1))


def clear_ends(ref):
    for c in range(3):
        for row in (0, ROWS + 1, ROWS + 2, ROWS + 3):
            ref[c, row] = jnp.zeros((16, 128), BF16)


def hidden(source, weights, bias, target):
    clear_ends(target)
    bias = jnp.concatenate([bias, bias], axis=1)
    for at in range(0, ROWS // 2, BLOCK):
        total = layer(source, weights, at).reshape(BLOCK, 16, 256)
        value = silu(total + bias[None]).astype(BF16).reshape(16 * BLOCK, 256)
        for part in range(2):
            start = at + ROWS // 2 * part + 1
            x = value[:, 128 * part : 128 * part + 128]
            for c in range(3):
                target[c, start : start + BLOCK] = turn(x, 1 - c).reshape(BLOCK, 16, 128)


def main_first(rows_ref, mask_ref, parameters, held, wide_ref, narrow_ref, first_ref):
    k_one_ref, k_two_ref, k_three_ref, b_one_ref, b_two_ref, b_three_ref = parameters
    second_ref, ocean_ref, one_ref, two_ref, three_ref = held[0:5]
    late_one_ref, late_two_ref, late_three_ref, bias_ref, _ = held[5:10]
    col = lanes()
    ocean = jnp.zeros((8, 128), F32)
    for b in range(8):
        x = 0.1 * mask_ref[8 * b : 8 * b + 8, :].astype(F32)
        ocean = jnp.where(col // 16 == b, turn(x, 6 + 16 * b), ocean)
    ocean_ref[...] = ocean

    biases = []
    at = 0
    for ref in (b_one_ref, b_two_ref, b_three_ref):
        n = ref.shape[1]
        same = lax.broadcasted_iota(jnp.int32, (n, n), 0) == lax.broadcasted_iota(jnp.int32, (n, n), 1)
        column = jnp.sum(jnp.where(same, ref[...], 0.0), axis=1, keepdims=True)
        biases.append(jnp.broadcast_to(column, (n, 128)))
        bias_ref[at : at + n, :] = biases[-1]
        at += n
    band(k_one_ref, wide_ref.at[0], one_ref)
    band(k_two_ref, wide_ref.at[1], two_ref)
    band(k_three_ref, narrow_ref, three_ref)
    band_compact(wide_ref.at[0], late_one_ref, 5, 3)
    band_compact(wide_ref.at[1], late_two_ref, 7, 5)
    band_compact(narrow_ref, late_three_ref, 5, 3)

    clear_ends(first_ref)
    for row in range(ROWS):
        x = jnp.concatenate([rows_ref[row, 0], rows_ref[row, 1]], axis=0).astype(BF16)
        for c in range(3):
            first_ref[c, row + 1] = turn(x, 1 - c)
    hidden(first_ref, one_ref, biases[0], second_ref)


def main_rest(rows_ref, mask_ref, held, third_ref):
    second_ref, _, _, two_ref, three_ref, _, _, _, bias_ref, out_ref = held
    hidden(second_ref, two_ref, bias_ref[16:32, :], third_ref)
    bias = jnp.concatenate([bias_ref[32:40, :]] * 2, axis=1)
    for at in range(0, ROWS // 2, BLOCK):
        forcing = layer(third_ref, three_ref, at).reshape(BLOCK, 8, 256) + bias[None]
        for part in range(2):
            for r in range(BLOCK):
                row = at + ROWS // 2 * part + r
                near = [min(max(row + d, 0), ROWS - 1) for d in (0, 1, -1)]
                q, north, south = [[rows_ref[i, half] for half in range(2)] for i in near]
                east = [turn(x, -1) for x in q]
                west = [turn(x, 1) for x in q]
                new = tendency(q, north, south, east, west)
                new[0] = new[0] + forcing[r, :, 128 * part : 128 * part + 128]
                ocean = 0.1 * mask_ref[row : row + 1, :].astype(F32)
                for half in range(2):
                    out_ref[row, half] = q[half] + ocean * new[half]


TAPS = (3, ROWS + 4, 16, 128)
HELD = [
    jax.ShapeDtypeStruct(shape, kind)
    for shape, kind in (
        (TAPS, BF16),
        ((8, 128), F32),
        ((128, DEPTH), BF16),
        ((128, DEPTH), BF16),
        ((64, DEPTH), BF16),
        ((48, 256), BF16),
        ((80, 384), BF16),
        ((32, 256), BF16),
        ((40, 128), F32),
        ((ROWS, 2, 8, 128), F32),
    )
]


def main_kernel(early, *refs):
    rows_ref, mask_ref, *parameters = refs[0:8]
    *held, wide_ref, narrow_ref, first_ref, third_ref = refs[8 if early else 19 :]
    lat = lax.axis_index("lat")

    @pl.when(lat <= 1 if early else lat > 1)
    def _():
        main_first(rows_ref, mask_ref, parameters, held, wide_ref, narrow_ref, first_ref)

    @pl.when(lat == 0 if early else lat > 0)
    def _():
        main_rest(rows_ref, mask_ref, held, third_ref)


def main_pass(rows, mask, parameters, held=(), message=()):
    early = len(held) == 0
    return pl.pallas_call(
        functools.partial(main_kernel, early),
        out_shape=HELD,
        in_specs=[VMEM] * (8 + len(held)) + [pl.BlockSpec(memory_space=pl.ANY)] * len(message),
        out_specs=[VMEM] * 10,
        scratch_shapes=[
            pltpu.VMEM((2, 9, 16, 128), BF16),
            pltpu.VMEM((9, 8, 128), F32),
            pltpu.VMEM(TAPS, BF16),
            pltpu.VMEM(TAPS, BF16),
        ],
        input_output_aliases={8 + i: i for i in range(len(held))},
        compiler_params=pltpu.CompilerParams(vmem_limit_bytes=LIMIT),
        cost_estimate=pl.CostEstimate(
            flops=80000000, bytes_accessed=1500000, transcendentals=150000
        ),
        name="main_early" if early else "main_late",
    )(rows, mask, *parameters, *held, *message)


def taps(rows, count):
    blank = jnp.zeros_like(rows[0])
    result = []
    for c in range(3):
        for row in rows:
            width = row.shape[1] // 128
            parts = [turn(row[:, 128 * i : 128 * i + 128], 1 - c) for i in range(width)]
            result.append(jnp.concatenate(parts, axis=1) if width > 1 else parts[0])
        result.extend([blank] * ((BLOCK + 2 if c < 2 else BLOCK + 4) - len(rows)))
    return jnp.concatenate(result, axis=0)


def strip_kernel(
    rows_ref, strip_ref, outer_ref, inner_ref, main_ref, ocean_ref, one_ref, two_ref, three_ref,
    bias_ref, cells_ref, low_ref, high_ref, side_ref, pre_ref, hidden_ref,
):
    east, west = sides(inner_ref, outer_ref)
    col = lanes()
    at = col % 16
    cells = []
    for r in range(8):
        pair = [[], []]
        for half in range(2):
            block = 2 * (r // 4) + half
            own = strip_ref[r, half]
            pair[0].append(jnp.where(at < 6, own, turn(east[block], 6 - 4 * (r % 4))))
            pair[1].append(jnp.where(at < 3, turn(west[block], -4 * (r % 4)), turn(own, -3)))
        cells.append(pair)

    def moved(pair, by):
        return [[turn(x, by) for x in part] for part in pair]

    cells = [moved(x, 16) for x in cells[5:8]] + cells + [moved(x, -16) for x in cells[0:3]]
    rows = []
    for pair in cells:
        parts = [jnp.concatenate(part, axis=0) for part in pair]
        rows.append(jnp.concatenate(parts, axis=1).astype(BF16))

    for weights, bias_at in ((one_ref, 0), (two_ref, 16)):
        count = len(rows) - 2 - BLOCK
        bias = jnp.concatenate([bias_ref[bias_at : bias_at + 16, :]] * 2, axis=1)
        low = dot(weights[...], taps(rows[0:10], 256)).reshape(BLOCK, 16, 256)
        high = dot(weights[0 : 16 * count, :], taps(rows[BLOCK:], 256)).reshape(count, 16, 256)
        low = silu(low + bias[None]).astype(BF16)
        high = silu(high + bias[None]).astype(BF16)
        rows = [low[i] for i in range(BLOCK)] + [high[i] for i in range(count)]
    forcing = dot(three_ref[...], taps(rows, 256)).reshape(BLOCK, 8, 256)
    forcing = forcing + jnp.concatenate([bias_ref[32:40, :]] * 2, axis=1)[None]

    both = []
    for r in range(8):
        new = []
        for part in range(2):
            q, north, south = [cells[i][part] for i in (r + 3, r + 4, r + 2)]
            value = tendency(
                q, north, south, [turn(x, -1) for x in q], [turn(x, 1) for x in q]
            )
            value[0] = value[0] + forcing[r, :, 128 * part : 128 * part + 128]
            new.append(value)
        ocean = ocean_ref[r : r + 1, :]
        value = [jnp.where(at < 6, new[0][half], turn(new[1][half], 3)) for half in range(2)]
        both.append([strip_ref[r, half] + ocean * value[half] for half in range(2)])

    edge = (col < 3) | (col >= 125)
    for b in range(8):
        ref, start = (low_ref, 0) if b == 0 else (high_ref, 0) if b == 7 else (cells_ref, 8 * b - 8)
        pitch = ref.shape[1]
        flat = ref.reshape(16 * pitch, 128)
        for r in range(8):
            for half in range(2):
                value = turn(both[r][half], -(16 * b + 6))
                value = jnp.where(edge, value, main_ref[8 * b + r, half])
                flat[pl.ds(8 * pitch * half + start + r, 8, stride=pitch), :] = value


    def own(row):
        start = 16 * (row // 8) + 4 * (row % 4)
        block = 2 * (row % 8 // 4)
        return [beside(east[block + h], start, west[block + h], start) for h in range(2)]

    own_rows = []
    for row in list(range(6)) + list(range(ROWS - 6, ROWS)):
        side = own(row)
        at = row if row < 3 else row - ROWS + 6
        if row < 3 or row >= ROWS - 3:
            for half in range(2):
                side_ref[at, half] = side[half]
        parts = [
            jnp.concatenate([rows_ref[row, 0], rows_ref[row, 1]], axis=0),
            jnp.concatenate(side, axis=0),
        ]
        own_rows.append(jnp.concatenate(parts, axis=1).astype(BF16))
    blank = jnp.zeros((16, 256), BF16)
    low = [blank] * 3 + own_rows[0:6]
    high = own_rows[6:12] + [blank] * 3
    rows = [jnp.concatenate(pair, axis=1) for pair in zip(low, high)]
    total = dot(one_ref[0:112, :], spread(rows, 256)).reshape(7, 16, 512)
    total = total + jnp.concatenate([bias_ref[0:16, :]] * 4, axis=1)[None]
    for r in range(3):
        pre_ref[r] = jnp.concatenate([total[r, :, 0:256], total[4 + r, :, 256:512]], axis=1)
    for r in range(4):
        for strip, x in enumerate((total[3 + r, :, 0:256], total[r, :, 256:512])):
            value = silu(x).astype(BF16)
            for c in range(3):
                hidden_ref[strip, c, r] = turn_wide(value, c)


def strip_pass(rows, strip, inner, outer, main, ocean, weights, bias):
    block = jax.ShapeDtypeStruct
    return pl.pallas_call(
        strip_kernel,
        out_shape=[
            block((16, ROWS - 8, 128), F32),
            *[block((16, 8, 128), F32)] * 2,
            block((6, 2, 8, 128), F32),
            block((3, 16, 512), F32),
            block((2, 3, 4, 16, 256), BF16),
        ],
        in_specs=[VMEM] * 10,
        out_specs=[VMEM] * 6,
        compiler_params=pltpu.CompilerParams(vmem_limit_bytes=LIMIT),
        cost_estimate=pl.CostEstimate(
            flops=150000000, bytes_accessed=2000000, transcendentals=100000
        ),
        name="strip_pass",
    )(rows, strip, outer, inner, main, ocean, *weights, bias)


def border_kernel(
    rows_ref, mask_ref, first_ref, second_ref, side_ref, pre_ref, hidden_ref, one_ref, two_ref,
    three_ref, bias_ref, cells_ref, low_in_ref, high_in_ref, out_ref, low_ref, high_ref, sems,
):
    lat = lax.axis_index("lat")
    even = lax.rem(lat, 2) == 0
    span = pl.ds(8, ROWS - 16)
    source = cells_ref.at[:, pl.ds(0, ROWS - 16), :]
    stores = [pltpu.make_async_copy(source, out_ref.at[:, span, :], sems.at[0])]
    stores[0].start()

    south, north = [], []
    low, high = [], []
    for t in range(3):
        blocks = [[], [], [], []]
        for half in range(2):
            at = 2 * t + half
            corner = jnp.where(even, second_ref[6], first_ref[6])
            x = jnp.where(even, second_ref[at], first_ref[at])
            y = beside(corner, 32 * half + 4 * t, corner, 32 * half + 16 + 4 * t)
            blocks[0].append(jnp.where(lat == 0, 0.0, x))
            blocks[1].append(jnp.where(lat == 0, 0.0, y))
            corner = jnp.where(even, first_ref[6], second_ref[6])
            blocks[2].append(jnp.where(even, first_ref[at], second_ref[at]))
            blocks[3].append(beside(corner, 32 * half + 4 * t, corner, 32 * half + 16 + 4 * t))
        south.append(blocks[0])
        north.append(blocks[2])
        wide = [jnp.concatenate(x, axis=0) for x in blocks]
        low.append(jnp.concatenate(wide[0:2], axis=1).astype(BF16))
        high.append(jnp.concatenate(wide[2:4], axis=1).astype(BF16))

    blank = jnp.zeros((16, 256), BF16)
    operand = []
    for c in range(3):
        lows = [turn_wide(x, c) for x in low] + [blank] * 2
        highs = [blank] * 2 + [turn_wide(x, c) for x in high]
        operand.extend(jnp.concatenate(pair, axis=1) for pair in zip(lows, highs))
    operand.append(jnp.zeros((16, 512), BF16))
    total = dot(one_ref[...], jnp.concatenate(operand, axis=0)).reshape(3, 16, 512)
    late = silu(total + pre_ref[...]).astype(BF16)

    operand = []
    for c in range(3):
        lows = [turn_wide(late[r, :, 0:256], c) for r in range(3)]
        lows = lows + [hidden_ref[0, c, r] for r in range(4)]
        highs = [hidden_ref[1, c, r] for r in range(4)]
        highs = highs + [turn_wide(late[r, :, 256:512], c) for r in range(3)]
        operand.extend(jnp.concatenate(pair, axis=1) for pair in zip(lows, highs))
    operand.extend([jnp.zeros((16, 512), BF16)] * 3)
    total = dot(two_ref[...], jnp.concatenate(operand, axis=0)).reshape(5, 16, 512)
    value = silu(total + jnp.concatenate([bias_ref[16:32, :]] * 4, axis=1)[None]).astype(BF16)
    operand = []
    for c in range(3):
        for r in range(5):
            parts = [turn_wide(value[r, :, at : at + 256], c)[:, 0:128] for at in (0, 256)]
            operand.append(jnp.concatenate(parts, axis=1))
    operand.append(jnp.zeros((16, 256), BF16))
    total = dot(three_ref[...], jnp.concatenate(operand, axis=0)).reshape(4, 8, 256)
    total = total + jnp.concatenate([bias_ref[32:40, :]] * 2, axis=1)[None]

    col = lanes()
    own = {row: [rows_ref[row, half] for half in range(2)] for row in (0, 1, 2, 3, 60, 61, 62, 63)}
    own[-1], own[ROWS] = south[2], north[0]
    for strip in range(2):
        ref, at = ((low_ref, 0), (high_ref, ROWS - 8))[strip]
        flat = ref.reshape(128, 128)
        for t in range(3):
            row = t if strip == 0 else ROWS - 3 + t
            q = own[row]
            side = [side_ref[3 * strip + t, half] for half in range(2)]
            ocean = 0.1 * mask_ref[row : row + 1, :].astype(F32)
            e = [turn(jnp.where(col == 0, y, x), -1) for x, y in zip(q, side)]
            w = [turn(jnp.where(col == 127, y, x), 1) for x, y in zip(q, side)]
            new = tendency(q, own[row + 1], own[row - 1], e, w)
            new[0] = new[0] + total[t, :, 128 * strip : 128 * strip + 128]
            for half in range(2):
                flat[pl.ds(64 * half + row - at, 8, stride=8), :] = q[half] + ocean * new[half]
        store = pltpu.make_async_copy(ref, out_ref.at[:, pl.ds(at, 8), :], sems.at[1 + strip])
        store.start()
        stores.append(store)
    for store in stores:
        store.wait()


def border_pass(rows, mask, first, second, side, pre, hidden, late, bias, cells, low, high):
    block = jax.ShapeDtypeStruct
    out, _, _ = pl.pallas_call(
        border_kernel,
        out_shape=[block((16, ROWS, 128), F32), block(low.shape, F32), block(high.shape, F32)],
        in_specs=[VMEM] * 14,
        out_specs=[HBM, VMEM, VMEM],
        scratch_shapes=[pltpu.SemaphoreType.DMA((3,))],
        input_output_aliases={12: 1, 13: 2},
        compiler_params=pltpu.CompilerParams(vmem_limit_bytes=LIMIT),
        cost_estimate=pl.CostEstimate(flops=60000000, bytes_accessed=1000000, transcendentals=60000),
        name="border_pass",
    )(rows, mask, first, second, side, pre, hidden, *late, bias, cells, low, high)
    return out


def shards(state, land_mask, kernel_one, bias_one, kernel_two, bias_two, kernel_three, bias_three):
    lon, lat = (lax.axis_size("lon"), lax.axis_size("lat"))
    biases = [x.reshape(1, x.shape[0]) for x in (bias_one, bias_two, bias_three)]
    cells, outer, inner, *biases = small_edges(state, biases)

    near = [(i, i + 1 - 2 * (i % 2)) for i in range(lon)]
    far = [(i, (i + 1 if i % 2 else i - 1) % lon) for i in range(lon)]
    inner = lax.ppermute(inner, "lon", near)
    outer = lax.ppermute(outer, "lon", far)
    rows, strip, all_outer, all_inner, north = rows_edges(lat, cells)
    all_inner = lax.ppermute(all_inner, "lon", near)
    all_outer = lax.ppermute(all_outer, "lon", far)
    parameters = (kernel_one, kernel_two, kernel_three, *biases)
    held = main_pass(rows, land_mask, parameters)

    def pairs(parity):
        result = []
        for i in range(lon):
            for j in range(parity, lat - 1, 2):
                result += [(i * lat + j, i * lat + j + 1), (i * lat + j + 1, i * lat + j)]
            if parity == 1:
                result.append((i * lat, (i + 1 - 2 * (i % 2)) * lat))
            if (lat - 1) % 2 == parity:
                result.append((i * lat + lat - 1, (lon - 1 - i) * lat + lat - 1))
        return result

    first, second = corners(lat, rows, inner, outer, north, held[0])
    held = main_pass(rows, land_mask, parameters, held, (second,))
    _, ocean, *weights, bias, main = held
    weights, late = weights[0:3], weights[3:6]
    first = lax.ppermute(first, ("lon", "lat"), pairs(0))
    second = lax.ppermute(second, ("lon", "lat"), pairs(1))
    cells, low, high, *own = strip_pass(
        rows, strip, all_inner, all_outer, main, ocean, weights, bias
    )
    return border_pass(rows, land_mask, first, second, *own, late, bias, cells, low, high)


def solution(mesh):
    return jax.shard_map(
        shards,
        mesh=mesh,
        in_specs=(P(None, "lat", "lon"), P("lat", "lon"), P(), P(), P(), P(), P(), P()),
        out_specs=P(None, "lat", "lon"),
        check_vma=False,
    )
```

```python
import functools

import jax
import jax.numpy as jnp
from jax import lax
from jax.experimental import pallas as pl
from jax.experimental.pallas import tpu as pltpu
from jax.sharding import PartitionSpec as P

F32 = jnp.float32
BF16 = jnp.bfloat16

ROWS = 64
PITCH = 72
BLOCK = 8
DEPTH = 512
SPAN = (BLOCK + 2) * 16
VMEM = pl.BlockSpec(memory_space=pltpu.VMEM)
HBM = pl.BlockSpec(memory_space=pltpu.HBM)
LIMIT = 40 * 2**20


def lanes():
    return lax.broadcasted_iota(jnp.int32, (8, 128), 1)


def turn(x, by):
    if isinstance(by, int):
        by = by % 128
        if by == 0:
            return x
    return pltpu.roll(x, by, x.ndim - 1)


def load_row(flat, row, half):
    return flat[pl.ds(8 * PITCH * half + row, 8, stride=PITCH), :]


def silu(v):
    half = 0.5 * v
    return half + half * jnp.tanh(half)


def dot(weights, x):
    return jnp.dot(weights, x, preferred_element_type=F32)


def even_place(axis):
    return lax.rem(lax.axis_index(axis), 2) == 0


def sides(inner, outer):
    even = even_place("lon")
    return (
        [jnp.where(even, inner[i], outer[i]) for i in range(4)],
        [jnp.where(even, outer[i], inner[i]) for i in range(4)],
    )


def tendency(q, north, south, east, west):
    sub = lax.broadcasted_iota(jnp.int32, (8, 128), 0)
    swapped = pltpu.roll(q[0], 4, 0)
    u = jnp.where(sub < 4, q[0], swapped)
    v = jnp.where(sub < 4, swapped, q[0])
    result = []
    for e, w, n, s, x in zip(east, west, north, south, q):
        total = -0.5 * (u * (e - w) + v * (n - s))
        result.append(total + 0.2 * (e + w + n + s - 4.0 * x))
    return result


def beside(e, e_at, w, w_at):
    return jnp.where(lanes() < 64, turn(e, -e_at), turn(w, 125 - w_at))


def turn_wide(x, c):
    return pltpu.roll(x, (1 - c) % 256, 1) if c != 1 else x


def spread(rows, width):
    blank = jnp.zeros((16, 2 * width), BF16)
    result = []
    for c in range(3):
        for row in rows:
            parts = [turn_wide(row[:, at : at + 256], c)[:, 0:width] for at in (0, 256)]
            result.append(jnp.concatenate(parts, axis=1))
        result.extend([blank] * ((BLOCK + 2 if c < 2 else BLOCK + 4) - len(rows)))
    return jnp.concatenate(result, axis=0)


def edges_kernel(state_ref, cells_ref, strip_ref, outer_ref, inner_ref, sems):
    fetches = []
    for half in range(2):
        span = pl.ds(8 * half, 8)
        target = cells_ref.at[span, pl.ds(0, ROWS), :]
        fetches.append(pltpu.make_async_copy(state_ref.at[span], target, sems.at[half]))
    for fetch in fetches:
        fetch.start()

    flat = cells_ref.reshape(16 * PITCH, 128)
    group = lanes() // 16
    part = (lanes() % 16) // 4
    even = even_place("lon")
    shifts = [
        [jnp.where(even, (4 * s - a) % 128, (4 * s - b) % 128) for s in range(4)]
        for a, b in ((6, 3), (3, 6))
    ]
    for fetch in fetches:
        fetch.wait()
    for half in range(2):
        strip = [jnp.zeros((8, 128), F32)] * 8
        for b in range(8):
            for r in range(8):
                x = load_row(flat, 8 * b + r, half)
                strip[r] = jnp.where(group == b, turn(x, 6 + 16 * b), strip[r])
        for r in range(8):
            strip_ref[r, half] = strip[r]
        for target, shift in zip((outer_ref, inner_ref), shifts):
            for q in range(2):
                value = jnp.zeros((8, 128), F32)
                for s in range(4):
                    value = jnp.where(part == s, turn(strip[4 * q + s], shift[s]), value)
                target[2 * q + half] = value


def edges(state):
    block = jax.ShapeDtypeStruct
    return pl.pallas_call(
        edges_kernel,
        out_shape=[
            block((16, PITCH, 128), F32),
            block((8, 2, 8, 128), F32),
            block((4, 8, 128), F32),
            block((4, 8, 128), F32),
        ],
        in_specs=[HBM],
        out_specs=[VMEM] * 4,
        scratch_shapes=[pltpu.SemaphoreType.DMA((2,))],
        compiler_params=pltpu.CompilerParams(vmem_limit_bytes=LIMIT),
        cost_estimate=pl.CostEstimate(flops=400000, bytes_accessed=1200000, transcendentals=0),
        name="tile_edges",
    )(pltpu.with_memory_space_constraint(state, pltpu.HBM))


def corners_kernel(size, rows_ref, outer_ref, inner_ref, north_ref, first_ref, second_ref):
    lat = lax.axis_index("lat")
    even = lax.rem(lat, 2) == 0
    for t in range(3):
        for half in range(2):
            at = 2 * t + half
            low = rows_ref[t, half]
            first_ref[at] = jnp.where(even, north_ref[at], low)
            second_ref[at] = jnp.where(even, low, north_ref[at])
    top = lat == size - 1
    col = lanes()
    part = col // 16
    straight = even_place("lon")
    mirrored = straight != top
    index = jnp.where(top, 112 + 4 * (3 - col // 4 % 4) + 2 - col % 4, 112 + col % 16)
    low = high = jnp.zeros((8, 128), F32)
    for i in range(4):
        half = i // 2
        pair = (inner_ref, outer_ref) if i % 2 == 0 else (outer_ref, inner_ref)
        x = jnp.where(straight, pair[0][half], pair[1][half])
        low = jnp.where(part == i, turn(x, 16 * i), low)
        x = jnp.where(mirrored, pair[0][2 + half], pair[1][2 + half])
        high = jnp.where(part == i, jnp.take_along_axis(x, index, axis=1), high)
    high = jnp.where(top & (col < 32), -high, high)
    first_ref[6] = jnp.where(even, high, low)
    second_ref[6] = jnp.where(even, low, high)


def corners(size, rows, inner, outer, north):
    return pl.pallas_call(
        functools.partial(corners_kernel, size),
        out_shape=[jax.ShapeDtypeStruct((7, 8, 128), F32)] * 2,
        in_specs=[VMEM] * 4,
        out_specs=[VMEM] * 2,
        compiler_params=pltpu.CompilerParams(vmem_limit_bytes=LIMIT),
        cost_estimate=pl.CostEstimate(flops=1000, bytes_accessed=100000, transcendentals=0),
        name="add_corners",
    )(rows, outer, inner, north)


def band(kernel_ref, wide_ref, target_ref):
    n = kernel_ref.shape[2]
    wide_ref[...] = jnp.zeros_like(wide_ref)
    tiles = [None] * (DEPTH // 128)
    for c in range(3):
        for a in range(3):
            wide_ref[3 * c + a, :, 0:16] = kernel_ref[a, c].astype(wide_ref.dtype)
            tile, off = divmod(SPAN * c + 16 * a, 128)
            x = turn(wide_ref[3 * c + a], off)
            tiles[tile] = x if tiles[tile] is None else tiles[tile] + x
    blank = jnp.zeros((n, 128), wide_ref.dtype)
    first = jnp.concatenate([blank if x is None else x for x in tiles], axis=1)
    rows = [first] + [pltpu.roll(first, 16 * r, 1) for r in range(1, BLOCK)]
    for r in range(0, BLOCK, 16 // n):
        target_ref[n * r : n * r + 16, :] = jnp.concatenate(rows[r : r + 16 // n], axis=0).astype(BF16)


def band_compact(wide_ref, target_ref, slots, outs):
    n = wide_ref.shape[1]
    tiles = [jnp.zeros((n, 128), wide_ref.dtype)] * (target_ref.shape[1] // 128)
    for c in range(3):
        for a in range(3):
            tile, off = divmod(16 * slots * c + 16 * a, 128)
            tiles[tile] = tiles[tile] + turn(wide_ref[3 * c + a], off)
    first = jnp.concatenate(tiles, axis=1)
    rows = [pltpu.roll(first, 16 * r, 1) if r else first for r in range(outs)]
    rows = rows + [jnp.zeros_like(first)] * (target_ref.shape[0] // n - outs)
    for r in range(0, len(rows), 16 // n):
        target_ref[n * r : n * r + 16, :] = jnp.concatenate(rows[r : r + 16 // n], axis=0).astype(BF16)


def main_kernel(
    size, cells_ref, mask_ref, k_one_ref, k_two_ref, k_three_ref, b_one_ref, b_two_ref, b_three_ref,
    rows_ref, out_ref, north_ref, ocean_ref, one_ref, two_ref, three_ref,
    late_one_ref, late_two_ref, late_three_ref, bias_ref,
    wide_ref, narrow_ref, first_ref, second_ref, third_ref, s_one_ref, s_two_ref, s_three_ref, sems,
):
    flat = cells_ref.reshape(16 * PITCH, 128)
    scalars = (s_one_ref, s_two_ref, s_three_ref)
    fetches = [
        pltpu.make_async_copy(source, target, sems.at[i])
        for i, (source, target) in enumerate(zip((b_one_ref, b_two_ref, b_three_ref), scalars))
    ]
    for fetch in fetches:
        fetch.start()

    top = lax.axis_index("lat") == size - 1
    col = lanes()
    for t in range(3):
        for half in range(2):
            folded = jnp.take_along_axis(load_row(flat, ROWS - 1 - t, half), 127 - col, axis=1)
            folded = -folded if half == 0 else folded
            north_ref[2 * t + half] = jnp.where(top, folded, load_row(flat, ROWS - 3 + t, half))
    ocean = jnp.zeros((8, 128), F32)
    for b in range(8):
        x = 0.1 * mask_ref[8 * b : 8 * b + 8, :].astype(F32)
        ocean = jnp.where(col // 16 == b, turn(x, 6 + 16 * b), ocean)
    ocean_ref[...] = ocean

    band(k_one_ref, wide_ref.at[0], one_ref)
    band(k_two_ref, wide_ref.at[1], two_ref)
    band(k_three_ref, narrow_ref, three_ref)
    band_compact(wide_ref.at[0], late_one_ref, 5, 3)
    band_compact(wide_ref.at[1], late_two_ref, 7, 5)
    band_compact(narrow_ref, late_three_ref, 5, 3)
    for ref in (first_ref, second_ref, third_ref):
        for c in range(3):
            for row in (0, ROWS + 1, ROWS + 2, ROWS + 3):
                ref[c, row] = jnp.zeros((16, 128), BF16)

    for row in range(ROWS):
        x = [load_row(flat, row, half) for half in range(2)]
        for half in range(2):
            rows_ref[row, half] = x[half]
        x = jnp.concatenate(x, axis=0).astype(BF16)
        for c in range(3):
            first_ref[c, row + 1] = turn(x, 1 - c)

    for fetch in fetches:
        fetch.wait()
    biases = []
    at = 0
    for ref in scalars:
        n = ref.shape[0]
        sub = lax.broadcasted_iota(jnp.int32, (n, 128), 0)
        value = jnp.zeros((n, 128), F32)
        for o in range(n):
            value = jnp.where(sub == o, ref[o], value)
        biases.append(value)
        bias_ref[at : at + n, :] = value
        at += n

    def layer(source, weights, at):
        parts = []
        for start in (at, at + ROWS // 2):
            for c in range(3):
                count = BLOCK + 2 if c < 2 else BLOCK + 4
                parts.append(source[c, start : start + count].reshape(16 * count, 128))
        x = jnp.concatenate(
            [jnp.concatenate(parts[0:3], axis=0), jnp.concatenate(parts[3:6], axis=0)], axis=1
        )
        return dot(weights[...], x)

    for source, weights, bias, target in (
        (first_ref, one_ref, biases[0], second_ref),
        (second_ref, two_ref, biases[1], third_ref),
    ):
        bias = jnp.concatenate([bias, bias], axis=1)
        for at in range(0, ROWS // 2, BLOCK):
            total = layer(source, weights, at).reshape(BLOCK, 16, 256)
            value = silu(total + bias[None]).astype(BF16).reshape(16 * BLOCK, 256)
            for part in range(2):
                start = at + ROWS // 2 * part + 1
                x = value[:, 128 * part : 128 * part + 128]
                for c in range(3):
                    target[c, start : start + BLOCK] = turn(x, 1 - c).reshape(BLOCK, 16, 128)

    bias = jnp.concatenate([biases[2], biases[2]], axis=1)
    for at in range(0, ROWS // 2, BLOCK):
        forcing = layer(third_ref, three_ref, at).reshape(BLOCK, 8, 256) + bias[None]
        for part in range(2):
            for r in range(BLOCK):
                row = at + ROWS // 2 * part + r
                near = [min(max(row + d, 0), ROWS - 1) for d in (0, 1, -1)]
                q, north, south = [[rows_ref[i, half] for half in range(2)] for i in near]
                east = [turn(x, -1) for x in q]
                west = [turn(x, 1) for x in q]
                new = tendency(q, north, south, east, west)
                new[0] = new[0] + forcing[r, :, 128 * part : 128 * part + 128]
                ocean = 0.1 * mask_ref[row : row + 1, :].astype(F32)
                for half in range(2):
                    out_ref[row, half] = q[half] + ocean * new[half]


def main_pass(size, cells, mask, kernels, biases):
    taps = pltpu.VMEM((3, ROWS + 4, 16, 128), BF16)
    block = jax.ShapeDtypeStruct
    return pl.pallas_call(
        functools.partial(main_kernel, size),
        out_shape=[
            block((ROWS, 2, 8, 128), F32),
            block((ROWS, 2, 8, 128), F32),
            block((6, 8, 128), F32),
            block((8, 128), F32),
            *[block((n, DEPTH), BF16) for n in (128, 128, 64)],
            *[block(shape, BF16) for shape in ((48, 256), (80, 384), (32, 256))],
            block((40, 128), F32),
        ],
        in_specs=[VMEM] * 5 + [HBM] * 3,
        out_specs=[VMEM] * 11,
        scratch_shapes=[
            pltpu.VMEM((2, 9, 16, 128), BF16),
            pltpu.VMEM((9, 8, 128), F32),
            *[taps] * 3,
            *[pltpu.SMEM(x.shape, F32) for x in biases],
            pltpu.SemaphoreType.DMA((3,)),
        ],
        compiler_params=pltpu.CompilerParams(vmem_limit_bytes=LIMIT),
        cost_estimate=pl.CostEstimate(
            flops=150000000, bytes_accessed=1500000, transcendentals=300000
        ),
        name="main_pass",
    )(cells, mask, *kernels, *[pltpu.with_memory_space_constraint(x, pltpu.HBM) for x in biases])


def taps(rows, count):
    blank = jnp.zeros_like(rows[0])
    result = []
    for c in range(3):
        for row in rows:
            width = row.shape[1] // 128
            parts = [turn(row[:, 128 * i : 128 * i + 128], 1 - c) for i in range(width)]
            result.append(jnp.concatenate(parts, axis=1) if width > 1 else parts[0])
        result.extend([blank] * ((BLOCK + 2 if c < 2 else BLOCK + 4) - len(rows)))
    return jnp.concatenate(result, axis=0)


def strip_kernel(
    rows_ref, strip_ref, outer_ref, inner_ref, main_ref, ocean_ref, one_ref, two_ref, three_ref,
    bias_ref, cells_ref, low_ref, high_ref, side_ref, pre_ref, hidden_ref,
):
    east, west = sides(inner_ref, outer_ref)
    col = lanes()
    at = col % 16
    cells = []
    for r in range(8):
        pair = [[], []]
        for half in range(2):
            block = 2 * (r // 4) + half
            own = strip_ref[r, half]
            pair[0].append(jnp.where(at < 6, own, turn(east[block], 6 - 4 * (r % 4))))
            pair[1].append(jnp.where(at < 3, turn(west[block], -4 * (r % 4)), turn(own, -3)))
        cells.append(pair)

    def moved(pair, by):
        return [[turn(x, by) for x in part] for part in pair]

    cells = [moved(x, 16) for x in cells[5:8]] + cells + [moved(x, -16) for x in cells[0:3]]
    rows = []
    for pair in cells:
        parts = [jnp.concatenate(part, axis=0) for part in pair]
        rows.append(jnp.concatenate(parts, axis=1).astype(BF16))

    for weights, bias_at in ((one_ref, 0), (two_ref, 16)):
        count = len(rows) - 2 - BLOCK
        bias = jnp.concatenate([bias_ref[bias_at : bias_at + 16, :]] * 2, axis=1)
        low = dot(weights[...], taps(rows[0:10], 256)).reshape(BLOCK, 16, 256)
        high = dot(weights[0 : 16 * count, :], taps(rows[BLOCK:], 256)).reshape(count, 16, 256)
        low = silu(low + bias[None]).astype(BF16)
        high = silu(high + bias[None]).astype(BF16)
        rows = [low[i] for i in range(BLOCK)] + [high[i] for i in range(count)]
    forcing = dot(three_ref[...], taps(rows, 256)).reshape(BLOCK, 8, 256)
    forcing = forcing + jnp.concatenate([bias_ref[32:40, :]] * 2, axis=1)[None]

    both = []
    for r in range(8):
        new = []
        for part in range(2):
            q, north, south = [cells[i][part] for i in (r + 3, r + 4, r + 2)]
            value = tendency(
                q, north, south, [turn(x, -1) for x in q], [turn(x, 1) for x in q]
            )
            value[0] = value[0] + forcing[r, :, 128 * part : 128 * part + 128]
            new.append(value)
        ocean = ocean_ref[r : r + 1, :]
        value = [jnp.where(at < 6, new[0][half], turn(new[1][half], 3)) for half in range(2)]
        both.append([strip_ref[r, half] + ocean * value[half] for half in range(2)])

    edge = (col < 3) | (col >= 125)
    for b in range(8):
        ref, start = (low_ref, 0) if b == 0 else (high_ref, 0) if b == 7 else (cells_ref, 8 * b - 8)
        pitch = ref.shape[1]
        flat = ref.reshape(16 * pitch, 128)
        for r in range(8):
            for half in range(2):
                value = turn(both[r][half], -(16 * b + 6))
                value = jnp.where(edge, value, main_ref[8 * b + r, half])
                flat[pl.ds(8 * pitch * half + start + r, 8, stride=pitch), :] = value


    def own(row):
        start = 16 * (row // 8) + 4 * (row % 4)
        block = 2 * (row % 8 // 4)
        return [beside(east[block + h], start, west[block + h], start) for h in range(2)]

    own_rows = []
    for row in list(range(6)) + list(range(ROWS - 6, ROWS)):
        side = own(row)
        at = row if row < 3 else row - ROWS + 6
        if row < 3 or row >= ROWS - 3:
            for half in range(2):
                side_ref[at, half] = side[half]
        parts = [
            jnp.concatenate([rows_ref[row, 0], rows_ref[row, 1]], axis=0),
            jnp.concatenate(side, axis=0),
        ]
        own_rows.append(jnp.concatenate(parts, axis=1).astype(BF16))
    blank = jnp.zeros((16, 256), BF16)
    low = [blank] * 3 + own_rows[0:6]
    high = own_rows[6:12] + [blank] * 3
    rows = [jnp.concatenate(pair, axis=1) for pair in zip(low, high)]
    total = dot(one_ref[0:112, :], spread(rows, 256)).reshape(7, 16, 512)
    total = total + jnp.concatenate([bias_ref[0:16, :]] * 4, axis=1)[None]
    for r in range(3):
        pre_ref[r] = jnp.concatenate([total[r, :, 0:256], total[4 + r, :, 256:512]], axis=1)
    for r in range(4):
        for strip, x in enumerate((total[3 + r, :, 0:256], total[r, :, 256:512])):
            value = silu(x).astype(BF16)
            for c in range(3):
                hidden_ref[strip, c, r] = turn_wide(value, c)


def strip_pass(rows, strip, inner, outer, main, ocean, weights, bias):
    block = jax.ShapeDtypeStruct
    return pl.pallas_call(
        strip_kernel,
        out_shape=[
            block((16, ROWS - 8, 128), F32),
            *[block((16, 8, 128), F32)] * 2,
            block((6, 2, 8, 128), F32),
            block((3, 16, 512), F32),
            block((2, 3, 4, 16, 256), BF16),
        ],
        in_specs=[VMEM] * 10,
        out_specs=[VMEM] * 6,
        compiler_params=pltpu.CompilerParams(vmem_limit_bytes=LIMIT),
        cost_estimate=pl.CostEstimate(
            flops=150000000, bytes_accessed=2000000, transcendentals=100000
        ),
        name="strip_pass",
    )(rows, strip, outer, inner, main, ocean, *weights, bias)


def border_kernel(
    rows_ref, mask_ref, first_ref, second_ref, side_ref, pre_ref, hidden_ref, one_ref, two_ref,
    three_ref, bias_ref, cells_ref, low_in_ref, high_in_ref, out_ref, low_ref, high_ref, sems,
):
    lat = lax.axis_index("lat")
    even = lax.rem(lat, 2) == 0
    span = pl.ds(8, ROWS - 16)
    source = cells_ref.at[:, pl.ds(0, ROWS - 16), :]
    stores = [pltpu.make_async_copy(source, out_ref.at[:, span, :], sems.at[0])]
    stores[0].start()

    south, north = [], []
    low, high = [], []
    for t in range(3):
        blocks = [[], [], [], []]
        for half in range(2):
            at = 2 * t + half
            corner = jnp.where(even, second_ref[6], first_ref[6])
            x = jnp.where(even, second_ref[at], first_ref[at])
            y = beside(corner, 32 * half + 4 + 4 * t, corner, 32 * half + 20 + 4 * t)
            blocks[0].append(jnp.where(lat == 0, 0.0, x))
            blocks[1].append(jnp.where(lat == 0, 0.0, y))
            corner = jnp.where(even, first_ref[6], second_ref[6])
            blocks[2].append(jnp.where(even, first_ref[at], second_ref[at]))
            blocks[3].append(beside(corner, 32 * half + 4 * t, corner, 32 * half + 16 + 4 * t))
        south.append(blocks[0])
        north.append(blocks[2])
        wide = [jnp.concatenate(x, axis=0) for x in blocks]
        low.append(jnp.concatenate(wide[0:2], axis=1).astype(BF16))
        high.append(jnp.concatenate(wide[2:4], axis=1).astype(BF16))

    blank = jnp.zeros((16, 256), BF16)
    operand = []
    for c in range(3):
        lows = [turn_wide(x, c) for x in low] + [blank] * 2
        highs = [blank] * 2 + [turn_wide(x, c) for x in high]
        operand.extend(jnp.concatenate(pair, axis=1) for pair in zip(lows, highs))
    operand.append(jnp.zeros((16, 512), BF16))
    total = dot(one_ref[...], jnp.concatenate(operand, axis=0)).reshape(3, 16, 512)
    late = silu(total + pre_ref[...]).astype(BF16)

    operand = []
    for c in range(3):
        lows = [turn_wide(late[r, :, 0:256], c) for r in range(3)]
        lows = lows + [hidden_ref[0, c, r] for r in range(4)]
        highs = [hidden_ref[1, c, r] for r in range(4)]
        highs = highs + [turn_wide(late[r, :, 256:512], c) for r in range(3)]
        operand.extend(jnp.concatenate(pair, axis=1) for pair in zip(lows, highs))
    operand.extend([jnp.zeros((16, 512), BF16)] * 3)
    total = dot(two_ref[...], jnp.concatenate(operand, axis=0)).reshape(5, 16, 512)
    value = silu(total + jnp.concatenate([bias_ref[16:32, :]] * 4, axis=1)[None]).astype(BF16)
    operand = []
    for c in range(3):
        for r in range(5):
            parts = [turn_wide(value[r, :, at : at + 256], c)[:, 0:128] for at in (0, 256)]
            operand.append(jnp.concatenate(parts, axis=1))
    operand.append(jnp.zeros((16, 256), BF16))
    total = dot(three_ref[...], jnp.concatenate(operand, axis=0)).reshape(4, 8, 256)
    total = total + jnp.concatenate([bias_ref[32:40, :]] * 2, axis=1)[None]

    col = lanes()
    own = {row: [rows_ref[row, half] for half in range(2)] for row in (0, 1, 2, 3, 60, 61, 62, 63)}
    own[-1], own[ROWS] = south[2], north[0]
    for strip in range(2):
        ref, at = ((low_ref, 0), (high_ref, ROWS - 8))[strip]
        flat = ref.reshape(128, 128)
        for t in range(3):
            row = t if strip == 0 else ROWS - 3 + t
            q = own[row]
            side = [side_ref[3 * strip + t, half] for half in range(2)]
            ocean = 0.1 * mask_ref[row : row + 1, :].astype(F32)
            e = [turn(jnp.where(col == 0, y, x), -1) for x, y in zip(q, side)]
            w = [turn(jnp.where(col == 127, y, x), 1) for x, y in zip(q, side)]
            new = tendency(q, own[row + 1], own[row - 1], e, w)
            new[0] = new[0] + total[t, :, 128 * strip : 128 * strip + 128]
            for half in range(2):
                flat[pl.ds(64 * half + row - at, 8, stride=8), :] = q[half] + ocean * new[half]
        store = pltpu.make_async_copy(ref, out_ref.at[:, pl.ds(at, 8), :], sems.at[1 + strip])
        store.start()
        stores.append(store)
    for store in stores:
        store.wait()


def border_pass(rows, mask, first, second, side, pre, hidden, late, bias, cells, low, high):
    block = jax.ShapeDtypeStruct
    out, _, _ = pl.pallas_call(
        border_kernel,
        out_shape=[block((16, ROWS, 128), F32), block(low.shape, F32), block(high.shape, F32)],
        in_specs=[VMEM] * 14,
        out_specs=[HBM, VMEM, VMEM],
        scratch_shapes=[pltpu.SemaphoreType.DMA((3,))],
        input_output_aliases={12: 1, 13: 2},
        compiler_params=pltpu.CompilerParams(vmem_limit_bytes=LIMIT),
        cost_estimate=pl.CostEstimate(flops=60000000, bytes_accessed=1000000, transcendentals=60000),
        name="border_pass",
    )(rows, mask, first, second, side, pre, hidden, *late, bias, cells, low, high)
    return out


def shards(state, land_mask, kernel_one, bias_one, kernel_two, bias_two, kernel_three, bias_three):
    lon, lat = (lax.axis_size("lon"), lax.axis_size("lat"))
    cells, strip, outer, inner = edges(state)

    inner = lax.ppermute(inner, "lon", [(i, i + 1 - 2 * (i % 2)) for i in range(lon)])
    outer = lax.ppermute(outer, "lon", [(i, (i + 1 if i % 2 else i - 1) % lon) for i in range(lon)])
    rows, main, north, ocean, *weights, bias = main_pass(
        lat, cells, land_mask, (kernel_one, kernel_two, kernel_three), (bias_one, bias_two, bias_three)
    )
    weights, late = weights[0:3], weights[3:6]

    def pairs(parity):
        result = []
        for i in range(lon):
            for j in range(parity, lat - 1, 2):
                result += [(i * lat + j, i * lat + j + 1), (i * lat + j + 1, i * lat + j)]
            if parity == 1:
                result.append((i * lat, (i + 1 - 2 * (i % 2)) * lat))
            if (lat - 1) % 2 == parity:
                result.append((i * lat + lat - 1, (lon - 1 - i) * lat + lat - 1))
        return result

    first, second = corners(lat, rows, inner, outer, north)
    first = lax.ppermute(first, ("lon", "lat"), pairs(0))
    second = lax.ppermute(second, ("lon", "lat"), pairs(1))
    cells, low, high, *own = strip_pass(
        rows, strip, inner, outer, main, ocean, weights, bias
    )
    return border_pass(rows, land_mask, first, second, *own, late, bias, cells, low, high)


def solution(mesh):
    return jax.shard_map(
        shards,
        mesh=mesh,
        in_specs=(P(None, "lat", "lon"), P("lat", "lon"), P(), P(), P(), P(), P(), P()),
        out_specs=P(None, "lat", "lon"),
        check_vma=False,
    )
```

```python
import functools

import jax
import jax.numpy as jnp
from jax import lax
from jax.experimental import pallas as pl
from jax.experimental.pallas import tpu as pltpu
from jax.sharding import PartitionSpec as P

F32 = jnp.float32
BF16 = jnp.bfloat16

ROWS = 64
PITCH = 72
BLOCK = 8
DEPTH = 512
SPAN = (BLOCK + 2) * 16
VMEM = pl.BlockSpec(memory_space=pltpu.VMEM)
HBM = pl.BlockSpec(memory_space=pltpu.HBM)
LIMIT = 40 * 2**20


def lanes():
    return lax.broadcasted_iota(jnp.int32, (8, 128), 1)


def turn(x, by):
    if isinstance(by, int):
        by = by % 128
        if by == 0:
            return x
    return pltpu.roll(x, by, x.ndim - 1)


def silu(v):
    half = 0.5 * v
    return half + half * jnp.tanh(half)


def dot(weights, x):
    return jnp.dot(weights, x, preferred_element_type=F32)


def even_place(axis):
    return lax.rem(lax.axis_index(axis), 2) == 0


def sides(inner, outer):
    even = even_place("lon")
    return (
        [jnp.where(even, inner[i], outer[i]) for i in range(4)],
        [jnp.where(even, outer[i], inner[i]) for i in range(4)],
    )


def tendency(q, north, south, east, west):
    sub = lax.broadcasted_iota(jnp.int32, (8, 128), 0)
    swapped = pltpu.roll(q[0], 4, 0)
    u = jnp.where(sub < 4, q[0], swapped)
    v = jnp.where(sub < 4, swapped, q[0])
    result = []
    for e, w, n, s, x in zip(east, west, north, south, q):
        total = -0.5 * (u * (e - w) + v * (n - s))
        result.append(total + 0.2 * (e + w + n + s - 4.0 * x))
    return result


def beside(e, e_at, w, w_at):
    return jnp.where(lanes() < 64, turn(e, -e_at), turn(w, 125 - w_at))


def turn_wide(x, c):
    return pltpu.roll(x, (1 - c) % 256, 1) if c != 1 else x


def spread(rows, width):
    blank = jnp.zeros((16, 2 * width), BF16)
    result = []
    for c in range(3):
        for row in rows:
            parts = [turn_wide(row[:, at : at + 256], c)[:, 0:width] for at in (0, 256)]
            result.append(jnp.concatenate(parts, axis=1))
        result.extend([blank] * ((BLOCK + 2 if c < 2 else BLOCK + 4) - len(rows)))
    return jnp.concatenate(result, axis=0)


def prepare_kernel(
    state_ref, b_one_ref, b_two_ref, b_three_ref,
    rows_ref, strip_ref, outer_ref, inner_ref, h_one_ref, h_two_ref, h_three_ref, cells_ref, sems,
):
    fetches = []
    for half in range(2):
        span = pl.ds(8 * half, 8)
        target = cells_ref.at[span, pl.ds(0, ROWS), :]
        fetches.append(pltpu.make_async_copy(state_ref.at[span], target, sems.at[half]))
    biases = ((b_one_ref, h_one_ref), (b_two_ref, h_two_ref), (b_three_ref, h_three_ref))
    for source, target in biases:
        fetches.append(pltpu.make_async_copy(source, target, sems.at[len(fetches)]))
    for i, fetch in enumerate(fetches):
        fetch.start(priority=i % 2)

    flat = cells_ref.reshape(16 * PITCH, 128)
    group = lanes() // 16
    part = (lanes() % 16) // 4
    even = even_place("lon")
    shifts = [
        [jnp.where(even, (4 * s - a) % 128, (4 * s - b) % 128) for s in range(4)]
        for a, b in ((6, 3), (3, 6))
    ]
    for fetch in fetches:
        fetch.wait()
    for half in range(2):
        strip = [jnp.zeros((8, 128), F32)] * 8
        for b in range(8):
            for r in range(8):
                x = flat[pl.ds(8 * PITCH * half + 8 * b + r, 8, stride=PITCH), :]
                rows_ref[8 * b + r, half] = x
                strip[r] = jnp.where(group == b, turn(x, 6 + 16 * b), strip[r])
        for r in range(8):
            strip_ref[r, half] = strip[r]
        for target, shift in zip((outer_ref, inner_ref), shifts):
            for q in range(2):
                value = jnp.zeros((8, 128), F32)
                for s in range(4):
                    value = jnp.where(part == s, turn(strip[4 * q + s], shift[s]), value)
                target[2 * q + half] = value


def prepare(state, biases):
    block = jax.ShapeDtypeStruct
    arrays = [pltpu.with_memory_space_constraint(x, pltpu.HBM) for x in (state, *biases)]
    return pl.pallas_call(
        prepare_kernel,
        out_shape=[
            block((ROWS, 2, 8, 128), F32),
            block((8, 2, 8, 128), F32),
            block((4, 8, 128), F32),
            block((4, 8, 128), F32),
            *[block(x.shape, F32) for x in biases],
        ],
        in_specs=[HBM] * 4,
        out_specs=[VMEM] * 7,
        scratch_shapes=[pltpu.VMEM((16, PITCH, 128), F32), pltpu.SemaphoreType.DMA((5,))],
        compiler_params=pltpu.CompilerParams(vmem_limit_bytes=LIMIT),
        cost_estimate=pl.CostEstimate(flops=400000, bytes_accessed=1200000, transcendentals=0),
        name="rows_edges",
    )(*arrays)


def corners_kernel(size, rows_ref, outer_ref, inner_ref, north_ref, first_ref, second_ref):
    lat = lax.axis_index("lat")
    even = lax.rem(lat, 2) == 0
    for t in range(3):
        for half in range(2):
            at = 2 * t + half
            low = rows_ref[t, half]
            first_ref[at] = jnp.where(even, north_ref[at], low)
            second_ref[at] = jnp.where(even, low, north_ref[at])
    top = lat == size - 1
    col = lanes()
    part = col // 16
    straight = even_place("lon")
    mirrored = straight != top
    index = jnp.where(top, 112 + 4 * (3 - col // 4 % 4) + 2 - col % 4, 112 + col % 16)
    low = high = jnp.zeros((8, 128), F32)
    for i in range(4):
        half = i // 2
        pair = (inner_ref, outer_ref) if i % 2 == 0 else (outer_ref, inner_ref)
        x = jnp.where(straight, pair[0][half], pair[1][half])
        low = jnp.where(part == i, turn(x, 16 * i), low)
        x = jnp.where(mirrored, pair[0][2 + half], pair[1][2 + half])
        high = jnp.where(part == i, jnp.take_along_axis(x, index, axis=1), high)
    high = jnp.where(top & (col < 32), -high, high)
    first_ref[6] = jnp.where(even, high, low)
    second_ref[6] = jnp.where(even, low, high)


def corners(size, rows, inner, outer, north):
    return pl.pallas_call(
        functools.partial(corners_kernel, size),
        out_shape=[jax.ShapeDtypeStruct((7, 8, 128), F32)] * 2,
        in_specs=[VMEM] * 4,
        out_specs=[VMEM] * 2,
        compiler_params=pltpu.CompilerParams(vmem_limit_bytes=LIMIT),
        cost_estimate=pl.CostEstimate(flops=1000, bytes_accessed=100000, transcendentals=0),
        name="add_corners",
    )(rows, outer, inner, north)


def band(kernel_ref, wide_ref, target_ref):
    n = kernel_ref.shape[2]
    wide_ref[...] = jnp.zeros_like(wide_ref)
    tiles = [None] * (DEPTH // 128)
    for c in range(3):
        for a in range(3):
            wide_ref[3 * c + a, :, 0:16] = kernel_ref[a, c].astype(wide_ref.dtype)
            tile, off = divmod(SPAN * c + 16 * a, 128)
            x = turn(wide_ref[3 * c + a], off)
            tiles[tile] = x if tiles[tile] is None else tiles[tile] + x
    blank = jnp.zeros((n, 128), wide_ref.dtype)
    first = jnp.concatenate([blank if x is None else x for x in tiles], axis=1)
    rows = [first] + [pltpu.roll(first, 16 * r, 1) for r in range(1, BLOCK)]
    for r in range(0, BLOCK, 16 // n):
        target_ref[n * r : n * r + 16, :] = jnp.concatenate(rows[r : r + 16 // n], axis=0).astype(BF16)


def band_compact(wide_ref, target_ref, slots, outs):
    n = wide_ref.shape[1]
    tiles = [jnp.zeros((n, 128), wide_ref.dtype)] * (target_ref.shape[1] // 128)
    for c in range(3):
        for a in range(3):
            tile, off = divmod(16 * slots * c + 16 * a, 128)
            tiles[tile] = tiles[tile] + turn(wide_ref[3 * c + a], off)
    first = jnp.concatenate(tiles, axis=1)
    rows = [pltpu.roll(first, 16 * r, 1) if r else first for r in range(outs)]
    rows = rows + [jnp.zeros_like(first)] * (target_ref.shape[0] // n - outs)
    for r in range(0, len(rows), 16 // n):
        target_ref[n * r : n * r + 16, :] = jnp.concatenate(rows[r : r + 16 // n], axis=0).astype(BF16)


def main_kernel(
    size, rows_ref, mask_ref, k_one_ref, k_two_ref, k_three_ref, b_one_ref, b_two_ref, b_three_ref,
    out_ref, north_ref, ocean_ref, one_ref, two_ref, three_ref,
    late_one_ref, late_two_ref, late_three_ref, bias_ref,
    wide_ref, narrow_ref, first_ref, second_ref, third_ref,
):
    top = lax.axis_index("lat") == size - 1
    col = lanes()
    for t in range(3):
        for half in range(2):
            folded = jnp.take_along_axis(rows_ref[ROWS - 1 - t, half], 127 - col, axis=1)
            folded = -folded if half == 0 else folded
            north_ref[2 * t + half] = jnp.where(top, folded, rows_ref[ROWS - 3 + t, half])
    ocean = jnp.zeros((8, 128), F32)
    for b in range(8):
        x = 0.1 * mask_ref[8 * b : 8 * b + 8, :].astype(F32)
        ocean = jnp.where(col // 16 == b, turn(x, 6 + 16 * b), ocean)
    ocean_ref[...] = ocean

    biases = []
    at = 0
    for ref in (b_one_ref, b_two_ref, b_three_ref):
        n = ref.shape[1]
        same = lax.broadcasted_iota(jnp.int32, (n, n), 0) == lax.broadcasted_iota(jnp.int32, (n, n), 1)
        column = jnp.sum(jnp.where(same, ref[...], 0.0), axis=1, keepdims=True)
        biases.append(jnp.broadcast_to(column, (n, 128)))
        bias_ref[at : at + n, :] = biases[-1]
        at += n
    band(k_one_ref, wide_ref.at[0], one_ref)
    band(k_two_ref, wide_ref.at[1], two_ref)
    band(k_three_ref, narrow_ref, three_ref)
    band_compact(wide_ref.at[0], late_one_ref, 5, 3)
    band_compact(wide_ref.at[1], late_two_ref, 7, 5)
    band_compact(narrow_ref, late_three_ref, 5, 3)
    for ref in (first_ref, second_ref, third_ref):
        for c in range(3):
            for row in (0, ROWS + 1, ROWS + 2, ROWS + 3):
                ref[c, row] = jnp.zeros((16, 128), BF16)

    for row in range(ROWS):
        x = jnp.concatenate([rows_ref[row, 0], rows_ref[row, 1]], axis=0).astype(BF16)
        for c in range(3):
            first_ref[c, row + 1] = turn(x, 1 - c)

    def layer(source, weights, at):
        parts = []
        for start in (at, at + ROWS // 2):
            for c in range(3):
                count = BLOCK + 2 if c < 2 else BLOCK + 4
                parts.append(source[c, start : start + count].reshape(16 * count, 128))
        x = jnp.concatenate(
            [jnp.concatenate(parts[0:3], axis=0), jnp.concatenate(parts[3:6], axis=0)], axis=1
        )
        return dot(weights[...], x)

    for source, weights, bias, target in (
        (first_ref, one_ref, biases[0], second_ref),
        (second_ref, two_ref, biases[1], third_ref),
    ):
        bias = jnp.concatenate([bias, bias], axis=1)
        for at in range(0, ROWS // 2, BLOCK):
            total = layer(source, weights, at).reshape(BLOCK, 16, 256)
            value = silu(total + bias[None]).astype(BF16).reshape(16 * BLOCK, 256)
            for part in range(2):
                start = at + ROWS // 2 * part + 1
                x = value[:, 128 * part : 128 * part + 128]
                for c in range(3):
                    target[c, start : start + BLOCK] = turn(x, 1 - c).reshape(BLOCK, 16, 128)

    bias = jnp.concatenate([biases[2], biases[2]], axis=1)
    for at in range(0, ROWS // 2, BLOCK):
        forcing = layer(third_ref, three_ref, at).reshape(BLOCK, 8, 256) + bias[None]
        for part in range(2):
            for r in range(BLOCK):
                row = at + ROWS // 2 * part + r
                near = [min(max(row + d, 0), ROWS - 1) for d in (0, 1, -1)]
                q, north, south = [[rows_ref[i, half] for half in range(2)] for i in near]
                east = [turn(x, -1) for x in q]
                west = [turn(x, 1) for x in q]
                new = tendency(q, north, south, east, west)
                new[0] = new[0] + forcing[r, :, 128 * part : 128 * part + 128]
                ocean = 0.1 * mask_ref[row : row + 1, :].astype(F32)
                for half in range(2):
                    out_ref[row, half] = q[half] + ocean * new[half]


def main_pass(size, rows, mask, parameters):
    taps = pltpu.VMEM((3, ROWS + 4, 16, 128), BF16)
    block = jax.ShapeDtypeStruct
    return pl.pallas_call(
        functools.partial(main_kernel, size),
        out_shape=[
            block(rows.shape, F32),
            block((6, 8, 128), F32),
            block((8, 128), F32),
            *[block((n, DEPTH), BF16) for n in (128, 128, 64)],
            *[block(shape, BF16) for shape in ((48, 256), (80, 384), (32, 256))],
            block((40, 128), F32),
        ],
        in_specs=[VMEM] * 8,
        out_specs=[VMEM] * 10,
        scratch_shapes=[
            pltpu.VMEM((2, 9, 16, 128), BF16),
            pltpu.VMEM((9, 8, 128), F32),
            *[taps] * 3,
        ],
        compiler_params=pltpu.CompilerParams(vmem_limit_bytes=LIMIT),
        cost_estimate=pl.CostEstimate(
            flops=150000000, bytes_accessed=1500000, transcendentals=300000
        ),
        name="main_pass",
    )(rows, mask, *parameters)


def taps(rows, count):
    blank = jnp.zeros_like(rows[0])
    result = []
    for c in range(3):
        for row in rows:
            width = row.shape[1] // 128
            parts = [turn(row[:, 128 * i : 128 * i + 128], 1 - c) for i in range(width)]
            result.append(jnp.concatenate(parts, axis=1) if width > 1 else parts[0])
        result.extend([blank] * ((BLOCK + 2 if c < 2 else BLOCK + 4) - len(rows)))
    return jnp.concatenate(result, axis=0)


def strip_kernel(
    rows_ref, strip_ref, outer_ref, inner_ref, main_ref, ocean_ref, one_ref, two_ref, three_ref,
    bias_ref, cells_ref, low_ref, high_ref, side_ref, pre_ref, hidden_ref,
):
    east, west = sides(inner_ref, outer_ref)
    col = lanes()
    at = col % 16
    cells = []
    for r in range(8):
        pair = [[], []]
        for half in range(2):
            block = 2 * (r // 4) + half
            own = strip_ref[r, half]
            pair[0].append(jnp.where(at < 6, own, turn(east[block], 6 - 4 * (r % 4))))
            pair[1].append(jnp.where(at < 3, turn(west[block], -4 * (r % 4)), turn(own, -3)))
        cells.append(pair)

    def moved(pair, by):
        return [[turn(x, by) for x in part] for part in pair]

    cells = [moved(x, 16) for x in cells[5:8]] + cells + [moved(x, -16) for x in cells[0:3]]
    rows = []
    for pair in cells:
        parts = [jnp.concatenate(part, axis=0) for part in pair]
        rows.append(jnp.concatenate(parts, axis=1).astype(BF16))

    for weights, bias_at in ((one_ref, 0), (two_ref, 16)):
        count = len(rows) - 2 - BLOCK
        bias = jnp.concatenate([bias_ref[bias_at : bias_at + 16, :]] * 2, axis=1)
        low = dot(weights[...], taps(rows[0:10], 256)).reshape(BLOCK, 16, 256)
        high = dot(weights[0 : 16 * count, :], taps(rows[BLOCK:], 256)).reshape(count, 16, 256)
        low = silu(low + bias[None]).astype(BF16)
        high = silu(high + bias[None]).astype(BF16)
        rows = [low[i] for i in range(BLOCK)] + [high[i] for i in range(count)]
    forcing = dot(three_ref[...], taps(rows, 256)).reshape(BLOCK, 8, 256)
    forcing = forcing + jnp.concatenate([bias_ref[32:40, :]] * 2, axis=1)[None]

    both = []
    for r in range(8):
        new = []
        for part in range(2):
            q, north, south = [cells[i][part] for i in (r + 3, r + 4, r + 2)]
            value = tendency(
                q, north, south, [turn(x, -1) for x in q], [turn(x, 1) for x in q]
            )
            value[0] = value[0] + forcing[r, :, 128 * part : 128 * part + 128]
            new.append(value)
        ocean = ocean_ref[r : r + 1, :]
        value = [jnp.where(at < 6, new[0][half], turn(new[1][half], 3)) for half in range(2)]
        both.append([strip_ref[r, half] + ocean * value[half] for half in range(2)])

    edge = (col < 3) | (col >= 125)
    for b in range(8):
        ref, start = (low_ref, 0) if b == 0 else (high_ref, 0) if b == 7 else (cells_ref, 8 * b - 8)
        pitch = ref.shape[1]
        flat = ref.reshape(16 * pitch, 128)
        for r in range(8):
            for half in range(2):
                value = turn(both[r][half], -(16 * b + 6))
                value = jnp.where(edge, value, main_ref[8 * b + r, half])
                flat[pl.ds(8 * pitch * half + start + r, 8, stride=pitch), :] = value


    def own(row):
        start = 16 * (row // 8) + 4 * (row % 4)
        block = 2 * (row % 8 // 4)
        return [beside(east[block + h], start, west[block + h], start) for h in range(2)]

    own_rows = []
    for row in list(range(6)) + list(range(ROWS - 6, ROWS)):
        side = own(row)
        at = row if row < 3 else row - ROWS + 6
        if row < 3 or row >= ROWS - 3:
            for half in range(2):
                side_ref[at, half] = side[half]
        parts = [
            jnp.concatenate([rows_ref[row, 0], rows_ref[row, 1]], axis=0),
            jnp.concatenate(side, axis=0),
        ]
        own_rows.append(jnp.concatenate(parts, axis=1).astype(BF16))
    blank = jnp.zeros((16, 256), BF16)
    low = [blank] * 3 + own_rows[0:6]
    high = own_rows[6:12] + [blank] * 3
    rows = [jnp.concatenate(pair, axis=1) for pair in zip(low, high)]
    total = dot(one_ref[0:112, :], spread(rows, 256)).reshape(7, 16, 512)
    total = total + jnp.concatenate([bias_ref[0:16, :]] * 4, axis=1)[None]
    for r in range(3):
        pre_ref[r] = jnp.concatenate([total[r, :, 0:256], total[4 + r, :, 256:512]], axis=1)
    for r in range(4):
        for strip, x in enumerate((total[3 + r, :, 0:256], total[r, :, 256:512])):
            value = silu(x).astype(BF16)
            for c in range(3):
                hidden_ref[strip, c, r] = turn_wide(value, c)


def strip_pass(rows, strip, inner, outer, main, ocean, weights, bias):
    block = jax.ShapeDtypeStruct
    return pl.pallas_call(
        strip_kernel,
        out_shape=[
            block((16, ROWS - 8, 128), F32),
            *[block((16, 8, 128), F32)] * 2,
            block((6, 2, 8, 128), F32),
            block((3, 16, 512), F32),
            block((2, 3, 4, 16, 256), BF16),
        ],
        in_specs=[VMEM] * 10,
        out_specs=[VMEM] * 6,
        compiler_params=pltpu.CompilerParams(vmem_limit_bytes=LIMIT),
        cost_estimate=pl.CostEstimate(
            flops=150000000, bytes_accessed=2000000, transcendentals=100000
        ),
        name="strip_pass",
    )(rows, strip, outer, inner, main, ocean, *weights, bias)


def border_kernel(
    rows_ref, mask_ref, first_ref, second_ref, side_ref, pre_ref, hidden_ref, one_ref, two_ref,
    three_ref, bias_ref, cells_ref, low_in_ref, high_in_ref, out_ref, low_ref, high_ref, sems,
):
    lat = lax.axis_index("lat")
    even = lax.rem(lat, 2) == 0
    span = pl.ds(8, ROWS - 16)
    source = cells_ref.at[:, pl.ds(0, ROWS - 16), :]
    stores = [pltpu.make_async_copy(source, out_ref.at[:, span, :], sems.at[0])]
    stores[0].start()

    south, north = [], []
    low, high = [], []
    for t in range(3):
        blocks = [[], [], [], []]
        for half in range(2):
            at = 2 * t + half
            corner = jnp.where(even, second_ref[6], first_ref[6])
            x = jnp.where(even, second_ref[at], first_ref[at])
            y = beside(corner, 32 * half + 4 + 4 * t, corner, 32 * half + 20 + 4 * t)
            blocks[0].append(jnp.where(lat == 0, 0.0, x))
            blocks[1].append(jnp.where(lat == 0, 0.0, y))
            corner = jnp.where(even, first_ref[6], second_ref[6])
            blocks[2].append(jnp.where(even, first_ref[at], second_ref[at]))
            blocks[3].append(beside(corner, 32 * half + 4 * t, corner, 32 * half + 16 + 4 * t))
        south.append(blocks[0])
        north.append(blocks[2])
        wide = [jnp.concatenate(x, axis=0) for x in blocks]
        low.append(jnp.concatenate(wide[0:2], axis=1).astype(BF16))
        high.append(jnp.concatenate(wide[2:4], axis=1).astype(BF16))

    blank = jnp.zeros((16, 256), BF16)
    operand = []
    for c in range(3):
        lows = [turn_wide(x, c) for x in low] + [blank] * 2
        highs = [blank] * 2 + [turn_wide(x, c) for x in high]
        operand.extend(jnp.concatenate(pair, axis=1) for pair in zip(lows, highs))
    operand.append(jnp.zeros((16, 512), BF16))
    total = dot(one_ref[...], jnp.concatenate(operand, axis=0)).reshape(3, 16, 512)
    late = silu(total + pre_ref[...]).astype(BF16)

    operand = []
    for c in range(3):
        lows = [turn_wide(late[r, :, 0:256], c) for r in range(3)]
        lows = lows + [hidden_ref[0, c, r] for r in range(4)]
        highs = [hidden_ref[1, c, r] for r in range(4)]
        highs = highs + [turn_wide(late[r, :, 256:512], c) for r in range(3)]
        operand.extend(jnp.concatenate(pair, axis=1) for pair in zip(lows, highs))
    operand.extend([jnp.zeros((16, 512), BF16)] * 3)
    total = dot(two_ref[...], jnp.concatenate(operand, axis=0)).reshape(5, 16, 512)
    value = silu(total + jnp.concatenate([bias_ref[16:32, :]] * 4, axis=1)[None]).astype(BF16)
    operand = []
    for c in range(3):
        for r in range(5):
            parts = [turn_wide(value[r, :, at : at + 256], c)[:, 0:128] for at in (0, 256)]
            operand.append(jnp.concatenate(parts, axis=1))
    operand.append(jnp.zeros((16, 256), BF16))
    total = dot(three_ref[...], jnp.concatenate(operand, axis=0)).reshape(4, 8, 256)
    total = total + jnp.concatenate([bias_ref[32:40, :]] * 2, axis=1)[None]

    col = lanes()
    own = {row: [rows_ref[row, half] for half in range(2)] for row in (0, 1, 2, 3, 60, 61, 62, 63)}
    own[-1], own[ROWS] = south[2], north[0]
    for strip in range(2):
        ref, at = ((low_ref, 0), (high_ref, ROWS - 8))[strip]
        flat = ref.reshape(128, 128)
        for t in range(3):
            row = t if strip == 0 else ROWS - 3 + t
            q = own[row]
            side = [side_ref[3 * strip + t, half] for half in range(2)]
            ocean = 0.1 * mask_ref[row : row + 1, :].astype(F32)
            e = [turn(jnp.where(col == 0, y, x), -1) for x, y in zip(q, side)]
            w = [turn(jnp.where(col == 127, y, x), 1) for x, y in zip(q, side)]
            new = tendency(q, own[row + 1], own[row - 1], e, w)
            new[0] = new[0] + total[t, :, 128 * strip : 128 * strip + 128]
            for half in range(2):
                flat[pl.ds(64 * half + row - at, 8, stride=8), :] = q[half] + ocean * new[half]
        store = pltpu.make_async_copy(ref, out_ref.at[:, pl.ds(at, 8), :], sems.at[1 + strip])
        store.start(priority=strip)
        stores.append(store)
    for store in stores:
        store.wait()


def border_pass(rows, mask, first, second, side, pre, hidden, late, bias, cells, low, high):
    block = jax.ShapeDtypeStruct
    out, _, _ = pl.pallas_call(
        border_kernel,
        out_shape=[block((16, ROWS, 128), F32), block(low.shape, F32), block(high.shape, F32)],
        in_specs=[VMEM] * 14,
        out_specs=[HBM, VMEM, VMEM],
        scratch_shapes=[pltpu.SemaphoreType.DMA((3,))],
        input_output_aliases={12: 1, 13: 2},
        compiler_params=pltpu.CompilerParams(vmem_limit_bytes=LIMIT),
        cost_estimate=pl.CostEstimate(flops=60000000, bytes_accessed=1000000, transcendentals=60000),
        name="border_pass",
    )(rows, mask, first, second, side, pre, hidden, *late, bias, cells, low, high)
    return out


def shards(state, land_mask, kernel_one, bias_one, kernel_two, bias_two, kernel_three, bias_three):
    lon, lat = (lax.axis_size("lon"), lax.axis_size("lat"))
    biases = [x.reshape(1, x.shape[0]) for x in (bias_one, bias_two, bias_three)]
    rows, strip, outer, inner, *biases = prepare(state, biases)
    parameters = (kernel_one, kernel_two, kernel_three, *biases)

    inner = lax.ppermute(inner, "lon", [(i, i + 1 - 2 * (i % 2)) for i in range(lon)])
    outer = lax.ppermute(outer, "lon", [(i, (i + 1 if i % 2 else i - 1) % lon) for i in range(lon)])
    main, north, ocean, *weights, bias = main_pass(lat, rows, land_mask, parameters)
    weights, late = weights[0:3], weights[3:6]

    def pairs(parity):
        result = []
        for i in range(lon):
            for j in range(parity, lat - 1, 2):
                result += [(i * lat + j, i * lat + j + 1), (i * lat + j + 1, i * lat + j)]
            if parity == 1:
                result.append((i * lat, (i + 1 - 2 * (i % 2)) * lat))
            if (lat - 1) % 2 == parity:
                result.append((i * lat + lat - 1, (lon - 1 - i) * lat + lat - 1))
        return result

    first, second = corners(lat, rows, inner, outer, north)
    first = lax.ppermute(first, ("lon", "lat"), pairs(0))
    second = lax.ppermute(second, ("lon", "lat"), pairs(1))
    cells, low, high, *own = strip_pass(
        rows, strip, inner, outer, main, ocean, weights, bias
    )
    return border_pass(rows, land_mask, first, second, *own, late, bias, cells, low, high)


def solution(mesh):
    return jax.shard_map(
        shards,
        mesh=mesh,
        in_specs=(P(None, "lat", "lon"), P("lat", "lon"), P(), P(), P(), P(), P(), P()),
        out_specs=P(None, "lat", "lon"),
        check_vma=False,
    )
```

```python
import functools

import jax
import jax.numpy as jnp
from jax import lax
from jax.experimental import pallas as pl
from jax.experimental.pallas import tpu as pltpu
from jax.sharding import PartitionSpec as P

F32 = jnp.float32
BF16 = jnp.bfloat16

ROWS = 64
PITCH = 72
BLOCK = 8
DEPTH = 512
SPAN = (BLOCK + 2) * 16
VMEM = pl.BlockSpec(memory_space=pltpu.VMEM)
HBM = pl.BlockSpec(memory_space=pltpu.HBM)
LIMIT = 40 * 2**20


def lanes():
    return lax.broadcasted_iota(jnp.int32, (8, 128), 1)


def turn(x, by):
    if isinstance(by, int):
        by = by % 128
        if by == 0:
            return x
    return pltpu.roll(x, by, x.ndim - 1)


def silu(v):
    half = 0.5 * v
    return half + half * jnp.tanh(half)


def dot(weights, x):
    return jnp.dot(weights, x, preferred_element_type=F32)


def even_place(axis):
    return lax.rem(lax.axis_index(axis), 2) == 0


def sides(inner, outer):
    even = even_place("lon")
    return (
        [jnp.where(even, inner[i], outer[i]) for i in range(4)],
        [jnp.where(even, outer[i], inner[i]) for i in range(4)],
    )


def tendency(q, north, south, east, west):
    sub = lax.broadcasted_iota(jnp.int32, (8, 128), 0)
    swapped = pltpu.roll(q[0], 4, 0)
    u = jnp.where(sub < 4, q[0], swapped)
    v = jnp.where(sub < 4, swapped, q[0])
    result = []
    for e, w, n, s, x in zip(east, west, north, south, q):
        total = -0.5 * (u * (e - w) + v * (n - s))
        result.append(total + 0.2 * (e + w + n + s - 4.0 * x))
    return result


def beside(e, e_at, w, w_at):
    return jnp.where(lanes() < 64, turn(e, -e_at), turn(w, 125 - w_at))


def turn_wide(x, c):
    return pltpu.roll(x, (1 - c) % 256, 1) if c != 1 else x


def spread(rows, width):
    blank = jnp.zeros((16, 2 * width), BF16)
    result = []
    for c in range(3):
        for row in rows:
            parts = [turn_wide(row[:, at : at + 256], c)[:, 0:width] for at in (0, 256)]
            result.append(jnp.concatenate(parts, axis=1))
        result.extend([blank] * ((BLOCK + 2 if c < 2 else BLOCK + 4) - len(rows)))
    return jnp.concatenate(result, axis=0)


def prepare_kernel(
    state_ref, b_one_ref, b_two_ref, b_three_ref,
    rows_ref, strip_ref, outer_ref, inner_ref, h_one_ref, h_two_ref, h_three_ref, cells_ref, sems,
):
    fetches = []
    for half in range(2):
        span = pl.ds(8 * half, 8)
        target = cells_ref.at[span, pl.ds(0, ROWS), :]
        fetches.append(pltpu.make_async_copy(state_ref.at[span], target, sems.at[half]))
    biases = ((b_one_ref, h_one_ref), (b_two_ref, h_two_ref), (b_three_ref, h_three_ref))
    for source, target in biases:
        fetches.append(pltpu.make_async_copy(source, target, sems.at[len(fetches)]))
    for fetch in fetches:
        fetch.start()

    flat = cells_ref.reshape(16 * PITCH, 128)
    group = lanes() // 16
    part = (lanes() % 16) // 4
    even = even_place("lon")
    shifts = [
        [jnp.where(even, (4 * s - a) % 128, (4 * s - b) % 128) for s in range(4)]
        for a, b in ((6, 3), (3, 6))
    ]
    for fetch in fetches[0:2]:
        fetch.wait()
    for half in range(2):
        strip = [jnp.zeros((8, 128), F32)] * 8
        for b in range(8):
            for r in range(8):
                x = flat[pl.ds(8 * PITCH * half + 8 * b + r, 8, stride=PITCH), :]
                rows_ref[8 * b + r, half] = x
                strip[r] = jnp.where(group == b, turn(x, 6 + 16 * b), strip[r])
        for r in range(8):
            strip_ref[r, half] = strip[r]
        for target, shift in zip((outer_ref, inner_ref), shifts):
            for q in range(2):
                value = jnp.zeros((8, 128), F32)
                for s in range(4):
                    value = jnp.where(part == s, turn(strip[4 * q + s], shift[s]), value)
                target[2 * q + half] = value
    for fetch in fetches[2:]:
        fetch.wait()


def prepare(state, biases):
    block = jax.ShapeDtypeStruct
    arrays = [pltpu.with_memory_space_constraint(x, pltpu.HBM) for x in (state, *biases)]
    return pl.pallas_call(
        prepare_kernel,
        out_shape=[
            block((ROWS, 2, 8, 128), F32),
            block((8, 2, 8, 128), F32),
            block((4, 8, 128), F32),
            block((4, 8, 128), F32),
            *[block(x.shape, F32) for x in biases],
        ],
        in_specs=[HBM] * 4,
        out_specs=[VMEM] * 7,
        scratch_shapes=[pltpu.VMEM((16, PITCH, 128), F32), pltpu.SemaphoreType.DMA((5,))],
        compiler_params=pltpu.CompilerParams(vmem_limit_bytes=LIMIT),
        cost_estimate=pl.CostEstimate(flops=400000, bytes_accessed=1200000, transcendentals=0),
        name="rows_edges",
    )(*arrays)


def corners_kernel(size, rows_ref, outer_ref, inner_ref, north_ref, first_ref, second_ref):
    lat = lax.axis_index("lat")
    even = lax.rem(lat, 2) == 0
    for t in range(3):
        for half in range(2):
            at = 2 * t + half
            low = rows_ref[t, half]
            first_ref[at] = jnp.where(even, north_ref[at], low)
            second_ref[at] = jnp.where(even, low, north_ref[at])
    top = lat == size - 1
    col = lanes()
    part = col // 16
    straight = even_place("lon")
    mirrored = straight != top
    index = jnp.where(top, 112 + 4 * (3 - col // 4 % 4) + 2 - col % 4, 112 + col % 16)
    low = high = jnp.zeros((8, 128), F32)
    for i in range(4):
        half = i // 2
        pair = (inner_ref, outer_ref) if i % 2 == 0 else (outer_ref, inner_ref)
        x = jnp.where(straight, pair[0][half], pair[1][half])
        low = jnp.where(part == i, turn(x, 16 * i), low)
        x = jnp.where(mirrored, pair[0][2 + half], pair[1][2 + half])
        high = jnp.where(part == i, jnp.take_along_axis(x, index, axis=1), high)
    high = jnp.where(top & (col < 32), -high, high)
    first_ref[6] = jnp.where(even, high, low)
    second_ref[6] = jnp.where(even, low, high)


def corners(size, rows, inner, outer, north):
    return pl.pallas_call(
        functools.partial(corners_kernel, size),
        out_shape=[jax.ShapeDtypeStruct((7, 8, 128), F32)] * 2,
        in_specs=[VMEM] * 4,
        out_specs=[VMEM] * 2,
        compiler_params=pltpu.CompilerParams(vmem_limit_bytes=LIMIT),
        cost_estimate=pl.CostEstimate(flops=1000, bytes_accessed=100000, transcendentals=0),
        name="add_corners",
    )(rows, outer, inner, north)


def band(kernel_ref, wide_ref, target_ref):
    n = kernel_ref.shape[2]
    wide_ref[...] = jnp.zeros_like(wide_ref)
    tiles = [None] * (DEPTH // 128)
    for c in range(3):
        for a in range(3):
            wide_ref[3 * c + a, :, 0:16] = kernel_ref[a, c].astype(wide_ref.dtype)
            tile, off = divmod(SPAN * c + 16 * a, 128)
            x = turn(wide_ref[3 * c + a], off)
            tiles[tile] = x if tiles[tile] is None else tiles[tile] + x
    blank = jnp.zeros((n, 128), wide_ref.dtype)
    first = jnp.concatenate([blank if x is None else x for x in tiles], axis=1)
    rows = [first] + [pltpu.roll(first, 16 * r, 1) for r in range(1, BLOCK)]
    for r in range(0, BLOCK, 16 // n):
        target_ref[n * r : n * r + 16, :] = jnp.concatenate(rows[r : r + 16 // n], axis=0).astype(BF16)


def band_compact(wide_ref, target_ref, slots, outs):
    n = wide_ref.shape[1]
    tiles = [jnp.zeros((n, 128), wide_ref.dtype)] * (target_ref.shape[1] // 128)
    for c in range(3):
        for a in range(3):
            tile, off = divmod(16 * slots * c + 16 * a, 128)
            tiles[tile] = tiles[tile] + turn(wide_ref[3 * c + a], off)
    first = jnp.concatenate(tiles, axis=1)
    rows = [pltpu.roll(first, 16 * r, 1) if r else first for r in range(outs)]
    rows = rows + [jnp.zeros_like(first)] * (target_ref.shape[0] // n - outs)
    for r in range(0, len(rows), 16 // n):
        target_ref[n * r : n * r + 16, :] = jnp.concatenate(rows[r : r + 16 // n], axis=0).astype(BF16)


def main_kernel(
    size, rows_ref, mask_ref, k_one_ref, k_two_ref, k_three_ref, b_one_ref, b_two_ref, b_three_ref,
    out_ref, north_ref, ocean_ref, one_ref, two_ref, three_ref,
    late_one_ref, late_two_ref, late_three_ref, bias_ref,
    wide_ref, narrow_ref, first_ref, second_ref, third_ref,
):
    top = lax.axis_index("lat") == size - 1
    col = lanes()
    for t in range(3):
        for half in range(2):
            folded = jnp.take_along_axis(rows_ref[ROWS - 1 - t, half], 127 - col, axis=1)
            folded = -folded if half == 0 else folded
            north_ref[2 * t + half] = jnp.where(top, folded, rows_ref[ROWS - 3 + t, half])
    ocean = jnp.zeros((8, 128), F32)
    for b in range(8):
        x = 0.1 * mask_ref[8 * b : 8 * b + 8, :].astype(F32)
        ocean = jnp.where(col // 16 == b, turn(x, 6 + 16 * b), ocean)
    ocean_ref[...] = ocean

    biases = []
    at = 0
    for ref in (b_one_ref, b_two_ref, b_three_ref):
        n = ref.shape[1]
        same = lax.broadcasted_iota(jnp.int32, (n, n), 0) == lax.broadcasted_iota(jnp.int32, (n, n), 1)
        column = jnp.sum(jnp.where(same, ref[...], 0.0), axis=1, keepdims=True)
        biases.append(jnp.broadcast_to(column, (n, 128)))
        bias_ref[at : at + n, :] = biases[-1]
        at += n
    band(k_one_ref, wide_ref.at[0], one_ref)
    band(k_two_ref, wide_ref.at[1], two_ref)
    band(k_three_ref, narrow_ref, three_ref)
    band_compact(wide_ref.at[0], late_one_ref, 5, 3)
    band_compact(wide_ref.at[1], late_two_ref, 7, 5)
    band_compact(narrow_ref, late_three_ref, 5, 3)
    for ref in (first_ref, second_ref, third_ref):
        for c in range(3):
            for row in (0, ROWS + 1, ROWS + 2, ROWS + 3):
                ref[c, row] = jnp.zeros((16, 128), BF16)

    for row in range(ROWS):
        x = jnp.concatenate([rows_ref[row, 0], rows_ref[row, 1]], axis=0).astype(BF16)
        for c in range(3):
            first_ref[c, row + 1] = turn(x, 1 - c)

    def layer(source, weights, at):
        parts = []
        for start in (at, at + ROWS // 2):
            for c in range(3):
                count = BLOCK + 2 if c < 2 else BLOCK + 4
                parts.append(source[c, start : start + count].reshape(16 * count, 128))
        x = jnp.concatenate(
            [jnp.concatenate(parts[0:3], axis=0), jnp.concatenate(parts[3:6], axis=0)], axis=1
        )
        return dot(weights[...], x)

    for source, weights, bias, target in (
        (first_ref, one_ref, biases[0], second_ref),
        (second_ref, two_ref, biases[1], third_ref),
    ):
        bias = jnp.concatenate([bias, bias], axis=1)
        for at in range(0, ROWS // 2, BLOCK):
            total = layer(source, weights, at).reshape(BLOCK, 16, 256)
            value = silu(total + bias[None]).astype(BF16).reshape(16 * BLOCK, 256)
            for part in range(2):
                start = at + ROWS // 2 * part + 1
                x = value[:, 128 * part : 128 * part + 128]
                for c in range(3):
                    target[c, start : start + BLOCK] = turn(x, 1 - c).reshape(BLOCK, 16, 128)

    bias = jnp.concatenate([biases[2], biases[2]], axis=1)
    for at in range(0, ROWS // 2, BLOCK):
        forcing = layer(third_ref, three_ref, at).reshape(BLOCK, 8, 256) + bias[None]
        for part in range(2):
            for r in range(BLOCK):
                row = at + ROWS // 2 * part + r
                near = [min(max(row + d, 0), ROWS - 1) for d in (0, 1, -1)]
                q, north, south = [[rows_ref[i, half] for half in range(2)] for i in near]
                east = [turn(x, -1) for x in q]
                west = [turn(x, 1) for x in q]
                new = tendency(q, north, south, east, west)
                new[0] = new[0] + forcing[r, :, 128 * part : 128 * part + 128]
                ocean = 0.1 * mask_ref[row : row + 1, :].astype(F32)
                for half in range(2):
                    out_ref[row, half] = q[half] + ocean * new[half]


def main_pass(size, rows, mask, parameters):
    taps = pltpu.VMEM((3, ROWS + 4, 16, 128), BF16)
    block = jax.ShapeDtypeStruct
    return pl.pallas_call(
        functools.partial(main_kernel, size),
        out_shape=[
            block(rows.shape, F32),
            block((6, 8, 128), F32),
            block((8, 128), F32),
            *[block((n, DEPTH), BF16) for n in (128, 128, 64)],
            *[block(shape, BF16) for shape in ((48, 256), (80, 384), (32, 256))],
            block((40, 128), F32),
        ],
        in_specs=[VMEM] * 8,
        out_specs=[VMEM] * 10,
        scratch_shapes=[
            pltpu.VMEM((2, 9, 16, 128), BF16),
            pltpu.VMEM((9, 8, 128), F32),
            *[taps] * 3,
        ],
        compiler_params=pltpu.CompilerParams(vmem_limit_bytes=LIMIT),
        cost_estimate=pl.CostEstimate(
            flops=150000000, bytes_accessed=1500000, transcendentals=300000
        ),
        name="main_pass",
    )(rows, mask, *parameters)


def taps(rows, count):
    blank = jnp.zeros_like(rows[0])
    result = []
    for c in range(3):
        for row in rows:
            width = row.shape[1] // 128
            parts = [turn(row[:, 128 * i : 128 * i + 128], 1 - c) for i in range(width)]
            result.append(jnp.concatenate(parts, axis=1) if width > 1 else parts[0])
        result.extend([blank] * ((BLOCK + 2 if c < 2 else BLOCK + 4) - len(rows)))
    return jnp.concatenate(result, axis=0)


def strip_kernel(
    rows_ref, strip_ref, outer_ref, inner_ref, main_ref, ocean_ref, one_ref, two_ref, three_ref,
    bias_ref, cells_ref, low_ref, high_ref, side_ref, pre_ref, hidden_ref,
):
    east, west = sides(inner_ref, outer_ref)
    col = lanes()
    at = col % 16
    cells = []
    for r in range(8):
        pair = [[], []]
        for half in range(2):
            block = 2 * (r // 4) + half
            own = strip_ref[r, half]
            pair[0].append(jnp.where(at < 6, own, turn(east[block], 6 - 4 * (r % 4))))
            pair[1].append(jnp.where(at < 3, turn(west[block], -4 * (r % 4)), turn(own, -3)))
        cells.append(pair)

    def moved(pair, by):
        return [[turn(x, by) for x in part] for part in pair]

    cells = [moved(x, 16) for x in cells[5:8]] + cells + [moved(x, -16) for x in cells[0:3]]
    rows = []
    for pair in cells:
        parts = [jnp.concatenate(part, axis=0) for part in pair]
        rows.append(jnp.concatenate(parts, axis=1).astype(BF16))

    for weights, bias_at in ((one_ref, 0), (two_ref, 16)):
        count = len(rows) - 2 - BLOCK
        bias = jnp.concatenate([bias_ref[bias_at : bias_at + 16, :]] * 2, axis=1)
        low = dot(weights[...], taps(rows[0:10], 256)).reshape(BLOCK, 16, 256)
        high = dot(weights[0 : 16 * count, :], taps(rows[BLOCK:], 256)).reshape(count, 16, 256)
        low = silu(low + bias[None]).astype(BF16)
        high = silu(high + bias[None]).astype(BF16)
        rows = [low[i] for i in range(BLOCK)] + [high[i] for i in range(count)]
    forcing = dot(three_ref[...], taps(rows, 256)).reshape(BLOCK, 8, 256)
    forcing = forcing + jnp.concatenate([bias_ref[32:40, :]] * 2, axis=1)[None]

    both = []
    for r in range(8):
        new = []
        for part in range(2):
            q, north, south = [cells[i][part] for i in (r + 3, r + 4, r + 2)]
            value = tendency(
                q, north, south, [turn(x, -1) for x in q], [turn(x, 1) for x in q]
            )
            value[0] = value[0] + forcing[r, :, 128 * part : 128 * part + 128]
            new.append(value)
        ocean = ocean_ref[r : r + 1, :]
        value = [jnp.where(at < 6, new[0][half], turn(new[1][half], 3)) for half in range(2)]
        both.append([strip_ref[r, half] + ocean * value[half] for half in range(2)])

    edge = (col < 3) | (col >= 125)
    for b in range(8):
        ref, start = (low_ref, 0) if b == 0 else (high_ref, 0) if b == 7 else (cells_ref, 8 * b - 8)
        pitch = ref.shape[1]
        flat = ref.reshape(16 * pitch, 128)
        for r in range(8):
            for half in range(2):
                value = turn(both[r][half], -(16 * b + 6))
                value = jnp.where(edge, value, main_ref[8 * b + r, half])
                flat[pl.ds(8 * pitch * half + start + r, 8, stride=pitch), :] = value


    def own(row):
        start = 16 * (row // 8) + 4 * (row % 4)
        block = 2 * (row % 8 // 4)
        return [beside(east[block + h], start, west[block + h], start) for h in range(2)]

    own_rows = []
    for row in list(range(6)) + list(range(ROWS - 6, ROWS)):
        side = own(row)
        at = row if row < 3 else row - ROWS + 6
        if row < 3 or row >= ROWS - 3:
            for half in range(2):
                side_ref[at, half] = side[half]
        parts = [
            jnp.concatenate([rows_ref[row, 0], rows_ref[row, 1]], axis=0),
            jnp.concatenate(side, axis=0),
        ]
        own_rows.append(jnp.concatenate(parts, axis=1).astype(BF16))
    blank = jnp.zeros((16, 256), BF16)
    low = [blank] * 3 + own_rows[0:6]
    high = own_rows[6:12] + [blank] * 3
    rows = [jnp.concatenate(pair, axis=1) for pair in zip(low, high)]
    total = dot(one_ref[0:112, :], spread(rows, 256)).reshape(7, 16, 512)
    total = total + jnp.concatenate([bias_ref[0:16, :]] * 4, axis=1)[None]
    for r in range(3):
        pre_ref[r] = jnp.concatenate([total[r, :, 0:256], total[4 + r, :, 256:512]], axis=1)
    for r in range(4):
        for strip, x in enumerate((total[3 + r, :, 0:256], total[r, :, 256:512])):
            value = silu(x).astype(BF16)
            for c in range(3):
                hidden_ref[strip, c, r] = turn_wide(value, c)


def strip_pass(rows, strip, inner, outer, main, ocean, weights, bias):
    block = jax.ShapeDtypeStruct
    return pl.pallas_call(
        strip_kernel,
        out_shape=[
            block((16, ROWS - 8, 128), F32),
            *[block((16, 8, 128), F32)] * 2,
            block((6, 2, 8, 128), F32),
            block((3, 16, 512), F32),
            block((2, 3, 4, 16, 256), BF16),
        ],
        in_specs=[VMEM] * 10,
        out_specs=[VMEM] * 6,
        compiler_params=pltpu.CompilerParams(vmem_limit_bytes=LIMIT),
        cost_estimate=pl.CostEstimate(
            flops=150000000, bytes_accessed=2000000, transcendentals=100000
        ),
        name="strip_pass",
    )(rows, strip, outer, inner, main, ocean, *weights, bias)


def border_kernel(
    rows_ref, mask_ref, first_ref, second_ref, side_ref, pre_ref, hidden_ref, one_ref, two_ref,
    three_ref, bias_ref, cells_ref, low_in_ref, high_in_ref, out_ref, low_ref, high_ref, sems,
):
    lat = lax.axis_index("lat")
    even = lax.rem(lat, 2) == 0
    span = pl.ds(8, ROWS - 16)
    source = cells_ref.at[:, pl.ds(0, ROWS - 16), :]
    stores = [pltpu.make_async_copy(source, out_ref.at[:, span, :], sems.at[0])]
    stores[0].start()

    south, north = [], []
    low, high = [], []
    for t in range(3):
        blocks = [[], [], [], []]
        for half in range(2):
            at = 2 * t + half
            corner = jnp.where(even, second_ref[6], first_ref[6])
            x = jnp.where(even, second_ref[at], first_ref[at])
            y = beside(corner, 32 * half + 4 + 4 * t, corner, 32 * half + 20 + 4 * t)
            blocks[0].append(jnp.where(lat == 0, 0.0, x))
            blocks[1].append(jnp.where(lat == 0, 0.0, y))
            corner = jnp.where(even, first_ref[6], second_ref[6])
            blocks[2].append(jnp.where(even, first_ref[at], second_ref[at]))
            blocks[3].append(beside(corner, 32 * half + 4 * t, corner, 32 * half + 16 + 4 * t))
        south.append(blocks[0])
        north.append(blocks[2])
        wide = [jnp.concatenate(x, axis=0) for x in blocks]
        low.append(jnp.concatenate(wide[0:2], axis=1).astype(BF16))
        high.append(jnp.concatenate(wide[2:4], axis=1).astype(BF16))

    blank = jnp.zeros((16, 256), BF16)
    operand = []
    for c in range(3):
        lows = [turn_wide(x, c) for x in low] + [blank] * 2
        highs = [blank] * 2 + [turn_wide(x, c) for x in high]
        operand.extend(jnp.concatenate(pair, axis=1) for pair in zip(lows, highs))
    operand.append(jnp.zeros((16, 512), BF16))
    total = dot(one_ref[...], jnp.concatenate(operand, axis=0)).reshape(3, 16, 512)
    late = silu(total + pre_ref[...]).astype(BF16)

    operand = []
    for c in range(3):
        lows = [turn_wide(late[r, :, 0:256], c) for r in range(3)]
        lows = lows + [hidden_ref[0, c, r] for r in range(4)]
        highs = [hidden_ref[1, c, r] for r in range(4)]
        highs = highs + [turn_wide(late[r, :, 256:512], c) for r in range(3)]
        operand.extend(jnp.concatenate(pair, axis=1) for pair in zip(lows, highs))
    operand.extend([jnp.zeros((16, 512), BF16)] * 3)
    total = dot(two_ref[...], jnp.concatenate(operand, axis=0)).reshape(5, 16, 512)
    value = silu(total + jnp.concatenate([bias_ref[16:32, :]] * 4, axis=1)[None]).astype(BF16)
    operand = []
    for c in range(3):
        for r in range(5):
            parts = [turn_wide(value[r, :, at : at + 256], c)[:, 0:128] for at in (0, 256)]
            operand.append(jnp.concatenate(parts, axis=1))
    operand.append(jnp.zeros((16, 256), BF16))
    total = dot(three_ref[...], jnp.concatenate(operand, axis=0)).reshape(4, 8, 256)
    total = total + jnp.concatenate([bias_ref[32:40, :]] * 2, axis=1)[None]

    low_ref[...] = low_in_ref[...]
    high_ref[...] = high_in_ref[...]
    col = lanes()
    own = {row: [rows_ref[row, half] for half in range(2)] for row in (0, 1, 2, 3, 60, 61, 62, 63)}
    own[-1], own[ROWS] = south[2], north[0]
    for strip in range(2):
        ref, at = ((low_ref, 0), (high_ref, ROWS - 8))[strip]
        flat = ref.reshape(128, 128)
        for t in range(3):
            row = t if strip == 0 else ROWS - 3 + t
            q = own[row]
            side = [side_ref[3 * strip + t, half] for half in range(2)]
            ocean = 0.1 * mask_ref[row : row + 1, :].astype(F32)
            e = [turn(jnp.where(col == 0, y, x), -1) for x, y in zip(q, side)]
            w = [turn(jnp.where(col == 127, y, x), 1) for x, y in zip(q, side)]
            new = tendency(q, own[row + 1], own[row - 1], e, w)
            new[0] = new[0] + total[t, :, 128 * strip : 128 * strip + 128]
            for half in range(2):
                flat[pl.ds(64 * half + row - at, 8, stride=8), :] = q[half] + ocean * new[half]
        store = pltpu.make_async_copy(ref, out_ref.at[:, pl.ds(at, 8), :], sems.at[1 + strip])
        store.start()
        stores.append(store)
    for store in stores:
        store.wait()


def border_pass(rows, mask, first, second, side, pre, hidden, late, bias, cells, low, high):
    return pl.pallas_call(
        border_kernel,
        out_shape=jax.ShapeDtypeStruct((16, ROWS, 128), F32),
        in_specs=[VMEM] * 14,
        out_specs=HBM,
        scratch_shapes=[
            pltpu.VMEM(low.shape, F32),
            pltpu.VMEM(high.shape, F32),
            pltpu.SemaphoreType.DMA((3,)),
        ],
        compiler_params=pltpu.CompilerParams(vmem_limit_bytes=LIMIT),
        cost_estimate=pl.CostEstimate(flops=60000000, bytes_accessed=1000000, transcendentals=60000),
        name="border_pass",
    )(rows, mask, first, second, side, pre, hidden, *late, bias, cells, low, high)


def shards(state, land_mask, kernel_one, bias_one, kernel_two, bias_two, kernel_three, bias_three):
    lon, lat = (lax.axis_size("lon"), lax.axis_size("lat"))
    biases = [x.reshape(1, x.shape[0]) for x in (bias_one, bias_two, bias_three)]
    rows, strip, outer, inner, *biases = prepare(state, biases)
    parameters = (kernel_one, kernel_two, kernel_three, *biases)

    inner = lax.ppermute(inner, "lon", [(i, i + 1 - 2 * (i % 2)) for i in range(lon)])
    outer = lax.ppermute(outer, "lon", [(i, (i + 1 if i % 2 else i - 1) % lon) for i in range(lon)])
    main, north, ocean, *weights, bias = main_pass(lat, rows, land_mask, parameters)
    weights, late = weights[0:3], weights[3:6]

    def pairs(parity):
        result = []
        for i in range(lon):
            for j in range(parity, lat - 1, 2):
                result += [(i * lat + j, i * lat + j + 1), (i * lat + j + 1, i * lat + j)]
            if parity == 1:
                result.append((i * lat, (i + 1 - 2 * (i % 2)) * lat))
            if (lat - 1) % 2 == parity:
                result.append((i * lat + lat - 1, (lon - 1 - i) * lat + lat - 1))
        return result

    first, second = corners(lat, rows, inner, outer, north)
    first = lax.ppermute(first, ("lon", "lat"), pairs(0))
    second = lax.ppermute(second, ("lon", "lat"), pairs(1))
    cells, low, high, *own = strip_pass(
        rows, strip, inner, outer, main, ocean, weights, bias
    )
    return border_pass(rows, land_mask, first, second, *own, late, bias, cells, low, high)


def solution(mesh):
    return jax.shard_map(
        shards,
        mesh=mesh,
        in_specs=(P(None, "lat", "lon"), P("lat", "lon"), P(), P(), P(), P(), P(), P()),
        out_specs=P(None, "lat", "lon"),
        check_vma=False,
    )
```

```python
import functools

import jax
import jax.numpy as jnp
from jax import lax
from jax.experimental import pallas as pl
from jax.experimental.pallas import tpu as pltpu
from jax.sharding import PartitionSpec as P

F32 = jnp.float32
BF16 = jnp.bfloat16

ROWS = 64
PITCH = 72
BLOCK = 8
DEPTH = 512
SPAN = (BLOCK + 2) * 16
VMEM = pl.BlockSpec(memory_space=pltpu.VMEM)
HBM = pl.BlockSpec(memory_space=pltpu.HBM)
LIMIT = 40 * 2**20


def lanes():
    return lax.broadcasted_iota(jnp.int32, (8, 128), 1)


def turn(x, by):
    if isinstance(by, int):
        by = by % 128
        if by == 0:
            return x
    return pltpu.roll(x, by, x.ndim - 1)


def silu(v):
    half = 0.5 * v
    return half + half * jnp.tanh(half)


def dot(weights, x):
    return jnp.dot(weights, x, preferred_element_type=F32)


def even_place(axis):
    return lax.rem(lax.axis_index(axis), 2) == 0


def sides(inner, outer):
    even = even_place("lon")
    return (
        [jnp.where(even, inner[i], outer[i]) for i in range(4)],
        [jnp.where(even, outer[i], inner[i]) for i in range(4)],
    )


def tendency(q, north, south, east, west):
    sub = lax.broadcasted_iota(jnp.int32, (8, 128), 0)
    swapped = pltpu.roll(q[0], 4, 0)
    u = jnp.where(sub < 4, q[0], swapped)
    v = jnp.where(sub < 4, swapped, q[0])
    result = []
    for e, w, n, s, x in zip(east, west, north, south, q):
        total = -0.5 * (u * (e - w) + v * (n - s))
        result.append(total + 0.2 * (e + w + n + s - 4.0 * x))
    return result


def beside(e, e_at, w, w_at):
    return jnp.where(lanes() < 64, turn(e, -e_at), turn(w, 125 - w_at))


def turn_wide(x, c):
    return pltpu.roll(x, (1 - c) % 256, 1) if c != 1 else x


def spread(rows, width):
    blank = jnp.zeros((16, 2 * width), BF16)
    result = []
    for c in range(3):
        for row in rows:
            parts = [turn_wide(row[:, at : at + 256], c)[:, 0:width] for at in (0, 256)]
            result.append(jnp.concatenate(parts, axis=1))
        result.extend([blank] * ((BLOCK + 2 if c < 2 else BLOCK + 4) - len(rows)))
    return jnp.concatenate(result, axis=0)


def prepare_kernel(
    state_ref, b_one_ref, b_two_ref, b_three_ref,
    rows_ref, strip_ref, outer_ref, inner_ref, h_one_ref, h_two_ref, h_three_ref, cells_ref, sems,
):
    fetches = []
    for half in range(2):
        span = pl.ds(8 * half, 8)
        target = cells_ref.at[span, pl.ds(0, ROWS), :]
        fetches.append(pltpu.make_async_copy(state_ref.at[span], target, sems.at[half]))
    biases = ((b_one_ref, h_one_ref), (b_two_ref, h_two_ref), (b_three_ref, h_three_ref))
    for source, target in biases:
        fetches.append(pltpu.make_async_copy(source, target, sems.at[len(fetches)]))
    for fetch in fetches:
        fetch.start()

    flat = cells_ref.reshape(16 * PITCH, 128)
    group = lanes() // 16
    part = (lanes() % 16) // 4
    even = even_place("lon")
    shifts = [
        [jnp.where(even, (4 * s - a) % 128, (4 * s - b) % 128) for s in range(4)]
        for a, b in ((6, 3), (3, 6))
    ]
    for fetch in fetches[0:2]:
        fetch.wait()
    for half in range(2):
        strip = [jnp.zeros((8, 128), F32)] * 8
        for b in range(8):
            for r in range(8):
                x = flat[pl.ds(8 * PITCH * half + 8 * b + r, 8, stride=PITCH), :]
                rows_ref[8 * b + r, half] = x
                strip[r] = jnp.where(group == b, turn(x, 6 + 16 * b), strip[r])
        for r in range(8):
            strip_ref[r, half] = strip[r]
        for target, shift in zip((outer_ref, inner_ref), shifts):
            for q in range(2):
                value = jnp.zeros((8, 128), F32)
                for s in range(4):
                    value = jnp.where(part == s, turn(strip[4 * q + s], shift[s]), value)
                target[2 * q + half] = value
    for fetch in fetches[2:]:
        fetch.wait()


def prepare(state, biases):
    block = jax.ShapeDtypeStruct
    arrays = [pltpu.with_memory_space_constraint(x, pltpu.HBM) for x in (state, *biases)]
    return pl.pallas_call(
        prepare_kernel,
        out_shape=[
            block((ROWS, 2, 8, 128), F32),
            block((8, 2, 8, 128), F32),
            block((4, 8, 128), F32),
            block((4, 8, 128), F32),
            *[block(x.shape, F32) for x in biases],
        ],
        in_specs=[HBM] * 4,
        out_specs=[VMEM] * 7,
        scratch_shapes=[pltpu.VMEM((16, PITCH, 128), F32), pltpu.SemaphoreType.DMA((5,))],
        compiler_params=pltpu.CompilerParams(vmem_limit_bytes=LIMIT),
        cost_estimate=pl.CostEstimate(flops=400000, bytes_accessed=1200000, transcendentals=0),
        name="rows_edges",
    )(*arrays)


def corners_kernel(size, rows_ref, outer_ref, inner_ref, north_ref, first_ref, second_ref):
    lat = lax.axis_index("lat")
    even = lax.rem(lat, 2) == 0
    for t in range(3):
        for half in range(2):
            at = 2 * t + half
            low = rows_ref[t, half]
            first_ref[at] = jnp.where(even, north_ref[at], low)
            second_ref[at] = jnp.where(even, low, north_ref[at])
    top = lat == size - 1
    col = lanes()
    part = col // 16
    straight = even_place("lon")
    mirrored = straight != top
    index = jnp.where(top, 112 + 4 * (3 - col // 4 % 4) + 2 - col % 4, 112 + col % 16)
    low = high = jnp.zeros((8, 128), F32)
    for i in range(4):
        half = i // 2
        pair = (inner_ref, outer_ref) if i % 2 == 0 else (outer_ref, inner_ref)
        x = jnp.where(straight, pair[0][half], pair[1][half])
        low = jnp.where(part == i, turn(x, 16 * i), low)
        x = jnp.where(mirrored, pair[0][2 + half], pair[1][2 + half])
        high = jnp.where(part == i, jnp.take_along_axis(x, index, axis=1), high)
    high = jnp.where(top & (col < 32), -high, high)
    first_ref[6] = jnp.where(even, high, low)
    second_ref[6] = jnp.where(even, low, high)


def corners(size, rows, inner, outer, north):
    return pl.pallas_call(
        functools.partial(corners_kernel, size),
        out_shape=[jax.ShapeDtypeStruct((7, 8, 128), F32)] * 2,
        in_specs=[VMEM] * 4,
        out_specs=[VMEM] * 2,
        compiler_params=pltpu.CompilerParams(vmem_limit_bytes=LIMIT),
        cost_estimate=pl.CostEstimate(flops=1000, bytes_accessed=100000, transcendentals=0),
        name="add_corners",
    )(rows, outer, inner, north)


def band(kernel_ref, wide_ref, target_ref):
    n = kernel_ref.shape[2]
    wide_ref[...] = jnp.zeros_like(wide_ref)
    tiles = [None] * (DEPTH // 128)
    for c in range(3):
        for a in range(3):
            wide_ref[3 * c + a, :, 0:16] = kernel_ref[a, c].astype(wide_ref.dtype)
            tile, off = divmod(SPAN * c + 16 * a, 128)
            x = turn(wide_ref[3 * c + a], off)
            tiles[tile] = x if tiles[tile] is None else tiles[tile] + x
    blank = jnp.zeros((n, 128), wide_ref.dtype)
    first = jnp.concatenate([blank if x is None else x for x in tiles], axis=1)
    rows = [first] + [pltpu.roll(first, 16 * r, 1) for r in range(1, BLOCK)]
    for r in range(0, BLOCK, 16 // n):
        target_ref[n * r : n * r + 16, :] = jnp.concatenate(rows[r : r + 16 // n], axis=0).astype(BF16)


def band_compact(wide_ref, target_ref, slots, outs):
    n = wide_ref.shape[1]
    tiles = [jnp.zeros((n, 128), wide_ref.dtype)] * (target_ref.shape[1] // 128)
    for c in range(3):
        for a in range(3):
            tile, off = divmod(16 * slots * c + 16 * a, 128)
            tiles[tile] = tiles[tile] + turn(wide_ref[3 * c + a], off)
    first = jnp.concatenate(tiles, axis=1)
    rows = [pltpu.roll(first, 16 * r, 1) if r else first for r in range(outs)]
    rows = rows + [jnp.zeros_like(first)] * (target_ref.shape[0] // n - outs)
    for r in range(0, len(rows), 16 // n):
        target_ref[n * r : n * r + 16, :] = jnp.concatenate(rows[r : r + 16 // n], axis=0).astype(BF16)


def main_kernel(
    size, rows_ref, mask_ref, k_one_ref, k_two_ref, k_three_ref, b_one_ref, b_two_ref, b_three_ref,
    out_ref, north_ref, ocean_ref, one_ref, two_ref, three_ref,
    late_one_ref, late_two_ref, late_three_ref, bias_ref,
    wide_ref, narrow_ref, first_ref, second_ref, third_ref,
):
    top = lax.axis_index("lat") == size - 1
    col = lanes()
    for t in range(3):
        for half in range(2):
            folded = jnp.take_along_axis(rows_ref[ROWS - 1 - t, half], 127 - col, axis=1)
            folded = -folded if half == 0 else folded
            north_ref[2 * t + half] = jnp.where(top, folded, rows_ref[ROWS - 3 + t, half])
    ocean = jnp.zeros((8, 128), F32)
    for b in range(8):
        x = 0.1 * mask_ref[8 * b : 8 * b + 8, :].astype(F32)
        ocean = jnp.where(col // 16 == b, turn(x, 6 + 16 * b), ocean)
    ocean_ref[...] = ocean

    biases = []
    at = 0
    for ref in (b_one_ref, b_two_ref, b_three_ref):
        n = ref.shape[1]
        same = lax.broadcasted_iota(jnp.int32, (n, n), 0) == lax.broadcasted_iota(jnp.int32, (n, n), 1)
        column = jnp.sum(jnp.where(same, ref[...], 0.0), axis=1, keepdims=True)
        biases.append(jnp.broadcast_to(column, (n, 128)))
        bias_ref[at : at + n, :] = biases[-1]
        at += n
    band(k_one_ref, wide_ref.at[0], one_ref)
    band(k_two_ref, wide_ref.at[1], two_ref)
    band(k_three_ref, narrow_ref, three_ref)
    band_compact(wide_ref.at[0], late_one_ref, 5, 3)
    band_compact(wide_ref.at[1], late_two_ref, 5, 3)
    band_compact(narrow_ref, late_three_ref, 5, 3)
    for ref in (first_ref, second_ref, third_ref):
        for c in range(3):
            for row in (0, ROWS + 1, ROWS + 2, ROWS + 3):
                ref[c, row] = jnp.zeros((16, 128), BF16)

    for row in range(ROWS):
        x = jnp.concatenate([rows_ref[row, 0], rows_ref[row, 1]], axis=0).astype(BF16)
        for c in range(3):
            first_ref[c, row + 1] = turn(x, 1 - c)

    def layer(source, weights, at):
        parts = []
        for start in (at, at + ROWS // 2):
            for c in range(3):
                count = BLOCK + 2 if c < 2 else BLOCK + 4
                parts.append(source[c, start : start + count].reshape(16 * count, 128))
        x = jnp.concatenate(
            [jnp.concatenate(parts[0:3], axis=0), jnp.concatenate(parts[3:6], axis=0)], axis=1
        )
        return dot(weights[...], x)

    for source, weights, bias, target in (
        (first_ref, one_ref, biases[0], second_ref),
        (second_ref, two_ref, biases[1], third_ref),
    ):
        bias = jnp.concatenate([bias, bias], axis=1)
        for at in range(0, ROWS // 2, BLOCK):
            total = layer(source, weights, at).reshape(BLOCK, 16, 256)
            value = silu(total + bias[None]).astype(BF16).reshape(16 * BLOCK, 256)
            for part in range(2):
                start = at + ROWS // 2 * part + 1
                x = value[:, 128 * part : 128 * part + 128]
                for c in range(3):
                    target[c, start : start + BLOCK] = turn(x, 1 - c).reshape(BLOCK, 16, 128)

    bias = jnp.concatenate([biases[2], biases[2]], axis=1)
    for at in range(0, ROWS // 2, BLOCK):
        forcing = layer(third_ref, three_ref, at).reshape(BLOCK, 8, 256) + bias[None]
        for part in range(2):
            for r in range(BLOCK):
                row = at + ROWS // 2 * part + r
                near = [min(max(row + d, 0), ROWS - 1) for d in (0, 1, -1)]
                q, north, south = [[rows_ref[i, half] for half in range(2)] for i in near]
                east = [turn(x, -1) for x in q]
                west = [turn(x, 1) for x in q]
                new = tendency(q, north, south, east, west)
                new[0] = new[0] + forcing[r, :, 128 * part : 128 * part + 128]
                ocean = 0.1 * mask_ref[row : row + 1, :].astype(F32)
                for half in range(2):
                    out_ref[row, half] = q[half] + ocean * new[half]


def main_pass(size, rows, mask, parameters):
    taps = pltpu.VMEM((3, ROWS + 4, 16, 128), BF16)
    block = jax.ShapeDtypeStruct
    return pl.pallas_call(
        functools.partial(main_kernel, size),
        out_shape=[
            block(rows.shape, F32),
            block((6, 8, 128), F32),
            block((8, 128), F32),
            *[block((n, DEPTH), BF16) for n in (128, 128, 64)],
            *[block(shape, BF16) for shape in ((48, 256), (48, 256), (32, 256))],
            block((40, 128), F32),
        ],
        in_specs=[VMEM] * 8,
        out_specs=[VMEM] * 10,
        scratch_shapes=[
            pltpu.VMEM((2, 9, 16, 128), BF16),
            pltpu.VMEM((9, 8, 128), F32),
            *[taps] * 3,
        ],
        compiler_params=pltpu.CompilerParams(vmem_limit_bytes=LIMIT),
        cost_estimate=pl.CostEstimate(
            flops=150000000, bytes_accessed=1500000, transcendentals=300000
        ),
        name="main_pass",
    )(rows, mask, *parameters)


def taps(rows, count):
    blank = jnp.zeros_like(rows[0])
    result = []
    for c in range(3):
        for row in rows:
            width = row.shape[1] // 128
            parts = [turn(row[:, 128 * i : 128 * i + 128], 1 - c) for i in range(width)]
            result.append(jnp.concatenate(parts, axis=1) if width > 1 else parts[0])
        result.extend([blank] * ((BLOCK + 2 if c < 2 else BLOCK + 4) - len(rows)))
    return jnp.concatenate(result, axis=0)


def strip_kernel(
    rows_ref, strip_ref, outer_ref, inner_ref, main_ref, ocean_ref, one_ref, two_ref, three_ref,
    bias_ref, cells_ref, low_ref, high_ref, side_ref, pre_one_ref, pre_two_ref, pre_three_ref,
):
    east, west = sides(inner_ref, outer_ref)
    col = lanes()
    at = col % 16
    cells = []
    for r in range(8):
        pair = [[], []]
        for half in range(2):
            block = 2 * (r // 4) + half
            own = strip_ref[r, half]
            pair[0].append(jnp.where(at < 6, own, turn(east[block], 6 - 4 * (r % 4))))
            pair[1].append(jnp.where(at < 3, turn(west[block], -4 * (r % 4)), turn(own, -3)))
        cells.append(pair)

    def own(row):
        start = 16 * (row // 8) + 4 * (row % 4)
        block = 2 * (row % 8 // 4)
        return [beside(east[block + h], start, west[block + h], start) for h in range(2)]

    low, high = [], []
    for row in list(range(6)) + list(range(ROWS - 6, ROWS)):
        side = own(row)
        slot = row if row < 3 else row - ROWS + 6
        if row < 3 or row >= ROWS - 3:
            for half in range(2):
                side_ref[slot, half] = side[half]
        parts = [
            jnp.concatenate([rows_ref[row, 0], rows_ref[row, 1]], axis=0),
            jnp.concatenate(side, axis=0),
        ]
        (low if row < 6 else high).append(jnp.concatenate(parts, axis=1).astype(BF16))
    blank = jnp.zeros((16, 256), BF16)
    for weights, count, bias_at, pre_ref, width in (
        (one_ref, 7, 0, pre_one_ref, 256),
        (two_ref, 5, 16, pre_two_ref, 256),
        (three_ref, 3, 32, pre_three_ref, 128),
    ):
        rows = zip([blank] * 3 + low, high + [blank] * 3)
        operand = spread([jnp.concatenate(pair, axis=1) for pair in rows], width)
        n = weights.shape[0] // BLOCK
        total = dot(weights[0 : (count + count % 2) * n, :], operand).reshape(-1, n, 2 * width)
        total = total + jnp.concatenate([bias_ref[bias_at : bias_at + n, :]] * (width // 64), axis=1)[None]
        for r in range(3):
            parts = [total[r, :, 0:width], total[count - 3 + r, :, width : 2 * width]]
            pre_ref[r] = jnp.concatenate(parts, axis=1)
        low = [silu(total[r, :, 0:width]).astype(BF16) for r in range(3, count)]
        high = [silu(total[r, :, width : 2 * width]).astype(BF16) for r in range(count - 3)]

    def moved(pair, by):
        return [[turn(x, by) for x in part] for part in pair]

    cells = [moved(x, 16) for x in cells[5:8]] + cells + [moved(x, -16) for x in cells[0:3]]
    rows = []
    for pair in cells:
        parts = [jnp.concatenate(part, axis=0) for part in pair]
        rows.append(jnp.concatenate(parts, axis=1).astype(BF16))

    for weights, bias_at in ((one_ref, 0), (two_ref, 16)):
        count = len(rows) - 2 - BLOCK
        bias = jnp.concatenate([bias_ref[bias_at : bias_at + 16, :]] * 2, axis=1)
        low = dot(weights[...], taps(rows[0:10], 256)).reshape(BLOCK, 16, 256)
        high = dot(weights[0 : 16 * count, :], taps(rows[BLOCK:], 256)).reshape(count, 16, 256)
        low = silu(low + bias[None]).astype(BF16)
        high = silu(high + bias[None]).astype(BF16)
        rows = [low[i] for i in range(BLOCK)] + [high[i] for i in range(count)]
    forcing = dot(three_ref[...], taps(rows, 256)).reshape(BLOCK, 8, 256)
    forcing = forcing + jnp.concatenate([bias_ref[32:40, :]] * 2, axis=1)[None]

    both = []
    for r in range(8):
        new = []
        for part in range(2):
            q, north, south = [cells[i][part] for i in (r + 3, r + 4, r + 2)]
            value = tendency(
                q, north, south, [turn(x, -1) for x in q], [turn(x, 1) for x in q]
            )
            value[0] = value[0] + forcing[r, :, 128 * part : 128 * part + 128]
            new.append(value)
        ocean = ocean_ref[r : r + 1, :]
        value = [jnp.where(at < 6, new[0][half], turn(new[1][half], 3)) for half in range(2)]
        both.append([strip_ref[r, half] + ocean * value[half] for half in range(2)])

    edge = (col < 3) | (col >= 125)
    for b in range(8):
        ref, start = (low_ref, 0) if b == 0 else (high_ref, 0) if b == 7 else (cells_ref, 8 * b - 8)
        pitch = ref.shape[1]
        flat = ref.reshape(16 * pitch, 128)
        for r in range(8):
            for half in range(2):
                value = turn(both[r][half], -(16 * b + 6))
                value = jnp.where(edge, value, main_ref[8 * b + r, half])
                flat[pl.ds(8 * pitch * half + start + r, 8, stride=pitch), :] = value


def strip_pass(rows, strip, inner, outer, main, ocean, weights, bias):
    block = jax.ShapeDtypeStruct
    return pl.pallas_call(
        strip_kernel,
        out_shape=[
            block((16, ROWS - 8, 128), F32),
            *[block((16, 8, 128), F32)] * 2,
            block((6, 2, 8, 128), F32),
            *[block(shape, F32) for shape in ((3, 16, 512), (3, 16, 512), (3, 8, 256))],
        ],
        in_specs=[VMEM] * 10,
        out_specs=[VMEM] * 7,
        compiler_params=pltpu.CompilerParams(vmem_limit_bytes=LIMIT),
        cost_estimate=pl.CostEstimate(
            flops=150000000, bytes_accessed=2000000, transcendentals=100000
        ),
        name="strip_pass",
    )(rows, strip, outer, inner, main, ocean, *weights, bias)


def border_kernel(
    rows_ref, mask_ref, first_ref, second_ref, side_ref, pre_one_ref, pre_two_ref, pre_three_ref,
    one_ref, two_ref, three_ref, cells_ref, low_in_ref, high_in_ref, out_ref, low_ref, high_ref, sems,
):
    lat = lax.axis_index("lat")
    even = lax.rem(lat, 2) == 0
    span = pl.ds(8, ROWS - 16)
    source = cells_ref.at[:, pl.ds(0, ROWS - 16), :]
    stores = [pltpu.make_async_copy(source, out_ref.at[:, span, :], sems.at[0])]
    stores[0].start()

    south, north = [], []
    low, high = [], []
    for t in range(3):
        blocks = [[], [], [], []]
        for half in range(2):
            at = 2 * t + half
            corner = jnp.where(even, second_ref[6], first_ref[6])
            x = jnp.where(even, second_ref[at], first_ref[at])
            y = beside(corner, 32 * half + 4 + 4 * t, corner, 32 * half + 20 + 4 * t)
            blocks[0].append(jnp.where(lat == 0, 0.0, x))
            blocks[1].append(jnp.where(lat == 0, 0.0, y))
            corner = jnp.where(even, first_ref[6], second_ref[6])
            blocks[2].append(jnp.where(even, first_ref[at], second_ref[at]))
            blocks[3].append(beside(corner, 32 * half + 4 * t, corner, 32 * half + 16 + 4 * t))
        south.append(blocks[0])
        north.append(blocks[2])
        wide = [jnp.concatenate(x, axis=0) for x in blocks]
        low.append(jnp.concatenate(wide[0:2], axis=1).astype(BF16))
        high.append(jnp.concatenate(wide[2:4], axis=1).astype(BF16))

    def late(weights, low, high, width):
        blank = jnp.zeros((16, width), BF16)
        operand = []
        for c in range(3):
            lows = [turn_wide(x, c)[:, 0:width] for x in low] + [blank] * 2
            highs = [blank] * 2 + [turn_wide(x, c)[:, 0:width] for x in high]
            operand.extend(jnp.concatenate(pair, axis=1) for pair in zip(lows, highs))
        operand.append(jnp.zeros((16, 2 * width), BF16))
        return dot(weights[...], jnp.concatenate(operand, axis=0))

    total = late(one_ref, low, high, 256)
    low_ref[...] = low_in_ref[...]
    high_ref[...] = high_in_ref[...]
    for pre_ref, weights, width in ((pre_one_ref, two_ref, 256), (pre_two_ref, three_ref, 128)):
        value = silu(total.reshape(3, 16, 512) + pre_ref[...]).astype(BF16)
        low = [value[r, :, 0:256] for r in range(3)]
        high = [value[r, :, 256:512] for r in range(3)]
        total = late(weights, low, high, width)
    total = total.reshape(4, 8, 256)[0:3] + pre_three_ref[...]

    col = lanes()
    own = {row: [rows_ref[row, half] for half in range(2)] for row in (0, 1, 2, 3, 60, 61, 62, 63)}
    own[-1], own[ROWS] = south[2], north[0]
    for strip in range(2):
        ref, at = ((low_ref, 0), (high_ref, ROWS - 8))[strip]
        flat = ref.reshape(128, 128)
        for t in range(3):
            row = t if strip == 0 else ROWS - 3 + t
            q = own[row]
            side = [side_ref[3 * strip + t, half] for half in range(2)]
            ocean = 0.1 * mask_ref[row : row + 1, :].astype(F32)
            e = [turn(jnp.where(col == 0, y, x), -1) for x, y in zip(q, side)]
            w = [turn(jnp.where(col == 127, y, x), 1) for x, y in zip(q, side)]
            new = tendency(q, own[row + 1], own[row - 1], e, w)
            new[0] = new[0] + total[t, :, 128 * strip : 128 * strip + 128]
            for half in range(2):
                flat[pl.ds(64 * half + row - at, 8, stride=8), :] = q[half] + ocean * new[half]
        store = pltpu.make_async_copy(ref, out_ref.at[:, pl.ds(at, 8), :], sems.at[1 + strip])
        store.start()
        stores.append(store)
    for store in stores:
        store.wait()


def border_pass(rows, mask, first, second, side, pre, late, cells, low, high):
    return pl.pallas_call(
        border_kernel,
        out_shape=jax.ShapeDtypeStruct((16, ROWS, 128), F32),
        in_specs=[VMEM] * 14,
        out_specs=HBM,
        scratch_shapes=[
            pltpu.VMEM(low.shape, F32),
            pltpu.VMEM(high.shape, F32),
            pltpu.SemaphoreType.DMA((3,)),
        ],
        compiler_params=pltpu.CompilerParams(vmem_limit_bytes=LIMIT),
        cost_estimate=pl.CostEstimate(flops=60000000, bytes_accessed=1000000, transcendentals=60000),
        name="border_pass",
    )(rows, mask, first, second, side, *pre, *late, cells, low, high)


def shards(state, land_mask, kernel_one, bias_one, kernel_two, bias_two, kernel_three, bias_three):
    lon, lat = (lax.axis_size("lon"), lax.axis_size("lat"))
    biases = [x.reshape(1, x.shape[0]) for x in (bias_one, bias_two, bias_three)]
    rows, strip, outer, inner, *biases = prepare(state, biases)
    parameters = (kernel_one, kernel_two, kernel_three, *biases)

    inner = lax.ppermute(inner, "lon", [(i, i + 1 - 2 * (i % 2)) for i in range(lon)])
    outer = lax.ppermute(outer, "lon", [(i, (i + 1 if i % 2 else i - 1) % lon) for i in range(lon)])
    main, north, ocean, *weights, bias = main_pass(lat, rows, land_mask, parameters)
    weights, late = weights[0:3], weights[3:6]

    def pairs(parity):
        result = []
        for i in range(lon):
            for j in range(parity, lat - 1, 2):
                result += [(i * lat + j, i * lat + j + 1), (i * lat + j + 1, i * lat + j)]
            if parity == 1:
                result.append((i * lat, (i + 1 - 2 * (i % 2)) * lat))
            if (lat - 1) % 2 == parity:
                result.append((i * lat + lat - 1, (lon - 1 - i) * lat + lat - 1))
        return result

    first, second = corners(lat, rows, inner, outer, north)
    first = lax.ppermute(first, ("lon", "lat"), pairs(0))
    second = lax.ppermute(second, ("lon", "lat"), pairs(1))
    cells, low, high, side, *pre = strip_pass(
        rows, strip, inner, outer, main, ocean, weights, bias
    )
    return border_pass(rows, land_mask, first, second, side, pre, late, cells, low, high)


def solution(mesh):
    return jax.shard_map(
        shards,
        mesh=mesh,
        in_specs=(P(None, "lat", "lon"), P("lat", "lon"), P(), P(), P(), P(), P(), P()),
        out_specs=P(None, "lat", "lon"),
        check_vma=False,
    )
```

```python
import functools

import jax
import jax.numpy as jnp
from jax import lax
from jax.experimental import pallas as pl
from jax.experimental.pallas import tpu as pltpu
from jax.sharding import PartitionSpec as P

F32 = jnp.float32
BF16 = jnp.bfloat16

ROWS = 64
PITCH = 72
BLOCK = 8
DEPTH = 512
SPAN = (BLOCK + 2) * 16
VMEM = pl.BlockSpec(memory_space=pltpu.VMEM)
HBM = pl.BlockSpec(memory_space=pltpu.HBM)
LIMIT = 40 * 2**20


def lanes():
    return lax.broadcasted_iota(jnp.int32, (8, 128), 1)


def turn(x, by):
    if isinstance(by, int):
        by = by % 128
        if by == 0:
            return x
    return pltpu.roll(x, by, x.ndim - 1)


def silu(v):
    half = 0.5 * v
    return half + half * jnp.tanh(half)


def dot(weights, x):
    return jnp.dot(weights, x, preferred_element_type=F32)


def even_place(axis):
    return lax.rem(lax.axis_index(axis), 2) == 0


def sides(inner, outer):
    even = even_place("lon")
    return (
        [jnp.where(even, inner[i], outer[i]) for i in range(4)],
        [jnp.where(even, outer[i], inner[i]) for i in range(4)],
    )


def tendency(q, north, south, east, west):
    sub = lax.broadcasted_iota(jnp.int32, (8, 128), 0)
    swapped = pltpu.roll(q[0], 4, 0)
    u = jnp.where(sub < 4, q[0], swapped)
    v = jnp.where(sub < 4, swapped, q[0])
    result = []
    for e, w, n, s, x in zip(east, west, north, south, q):
        total = -0.5 * (u * (e - w) + v * (n - s))
        result.append(total + 0.2 * (e + w + n + s - 4.0 * x))
    return result


def beside(e, e_at, w, w_at):
    return jnp.where(lanes() < 64, turn(e, -e_at), turn(w, 125 - w_at))


def turn_wide(x, c):
    return pltpu.roll(x, (1 - c) % 256, 1) if c != 1 else x


def spread(rows, width):
    blank = jnp.zeros((16, 2 * width), BF16)
    result = []
    for c in range(3):
        for row in rows:
            parts = [turn_wide(row[:, at : at + 256], c)[:, 0:width] for at in (0, 256)]
            result.append(jnp.concatenate(parts, axis=1))
        result.extend([blank] * ((BLOCK + 2 if c < 2 else BLOCK + 4) - len(rows)))
    return jnp.concatenate(result, axis=0)


def prepare_kernel(
    state_ref, b_one_ref, b_two_ref, b_three_ref,
    rows_ref, strip_ref, outer_ref, inner_ref, h_one_ref, h_two_ref, h_three_ref, cells_ref, sems,
):
    fetches = []
    for half in range(2):
        span = pl.ds(8 * half, 8)
        target = cells_ref.at[span, pl.ds(0, ROWS), :]
        fetches.append(pltpu.make_async_copy(state_ref.at[span], target, sems.at[half]))
    biases = ((b_one_ref, h_one_ref), (b_two_ref, h_two_ref), (b_three_ref, h_three_ref))
    for source, target in biases:
        fetches.append(pltpu.make_async_copy(source, target, sems.at[len(fetches)]))
    for fetch in fetches:
        fetch.start()

    flat = cells_ref.reshape(16 * PITCH, 128)
    group = lanes() // 16
    part = (lanes() % 16) // 4
    even = even_place("lon")
    shifts = [
        [jnp.where(even, (4 * s - a) % 128, (4 * s - b) % 128) for s in range(4)]
        for a, b in ((6, 3), (3, 6))
    ]
    for fetch in fetches[0:2]:
        fetch.wait()
    for half in range(2):
        strip = [jnp.zeros((8, 128), F32)] * 8
        for b in range(8):
            for r in range(8):
                x = flat[pl.ds(8 * PITCH * half + 8 * b + r, 8, stride=PITCH), :]
                rows_ref[8 * b + r, half] = x
                strip[r] = jnp.where(group == b, turn(x, 6 + 16 * b), strip[r])
        for r in range(8):
            strip_ref[r, half] = strip[r]
        for target, shift in zip((outer_ref, inner_ref), shifts):
            for q in range(2):
                value = jnp.zeros((8, 128), F32)
                for s in range(4):
                    value = jnp.where(part == s, turn(strip[4 * q + s], shift[s]), value)
                target[2 * q + half] = value
    for fetch in fetches[2:]:
        fetch.wait()


def prepare(state, biases):
    block = jax.ShapeDtypeStruct
    arrays = [pltpu.with_memory_space_constraint(x, pltpu.HBM) for x in (state, *biases)]
    return pl.pallas_call(
        prepare_kernel,
        out_shape=[
            block((ROWS, 2, 8, 128), F32),
            block((8, 2, 8, 128), F32),
            block((4, 8, 128), F32),
            block((4, 8, 128), F32),
            *[block(x.shape, F32) for x in biases],
        ],
        in_specs=[HBM] * 4,
        out_specs=[VMEM] * 7,
        scratch_shapes=[pltpu.VMEM((16, PITCH, 128), F32), pltpu.SemaphoreType.DMA((5,))],
        compiler_params=pltpu.CompilerParams(vmem_limit_bytes=LIMIT),
        cost_estimate=pl.CostEstimate(flops=400000, bytes_accessed=1200000, transcendentals=0),
        name="rows_edges",
    )(*arrays)


def corners_kernel(size, rows_ref, outer_ref, inner_ref, north_ref, first_ref, second_ref):
    lat = lax.axis_index("lat")
    even = lax.rem(lat, 2) == 0
    for t in range(3):
        for half in range(2):
            at = 2 * t + half
            low = rows_ref[t, half]
            first_ref[at] = jnp.where(even, north_ref[at], low)
            second_ref[at] = jnp.where(even, low, north_ref[at])
    top = lat == size - 1
    col = lanes()
    part = col // 16
    straight = even_place("lon")
    mirrored = straight != top
    index = jnp.where(top, 112 + 4 * (3 - col // 4 % 4) + 2 - col % 4, 112 + col % 16)
    low = high = jnp.zeros((8, 128), F32)
    for i in range(4):
        half = i // 2
        pair = (inner_ref, outer_ref) if i % 2 == 0 else (outer_ref, inner_ref)
        x = jnp.where(straight, pair[0][half], pair[1][half])
        low = jnp.where(part == i, turn(x, 16 * i), low)
        x = jnp.where(mirrored, pair[0][2 + half], pair[1][2 + half])
        high = jnp.where(part == i, jnp.take_along_axis(x, index, axis=1), high)
    high = jnp.where(top & (col < 32), -high, high)
    first_ref[6] = jnp.where(even, high, low)
    second_ref[6] = jnp.where(even, low, high)


def corners(size, rows, inner, outer, north):
    return pl.pallas_call(
        functools.partial(corners_kernel, size),
        out_shape=[jax.ShapeDtypeStruct((7, 8, 128), F32)] * 2,
        in_specs=[VMEM] * 4,
        out_specs=[VMEM] * 2,
        compiler_params=pltpu.CompilerParams(vmem_limit_bytes=LIMIT),
        cost_estimate=pl.CostEstimate(flops=1000, bytes_accessed=100000, transcendentals=0),
        name="add_corners",
    )(rows, outer, inner, north)


def band(kernel_ref, wide_ref, target_ref):
    n = kernel_ref.shape[2]
    wide_ref[...] = jnp.zeros_like(wide_ref)
    tiles = [None] * (DEPTH // 128)
    for c in range(3):
        for a in range(3):
            wide_ref[3 * c + a, :, 0:16] = kernel_ref[a, c].astype(wide_ref.dtype)
            tile, off = divmod(SPAN * c + 16 * a, 128)
            x = turn(wide_ref[3 * c + a], off)
            tiles[tile] = x if tiles[tile] is None else tiles[tile] + x
    blank = jnp.zeros((n, 128), wide_ref.dtype)
    first = jnp.concatenate([blank if x is None else x for x in tiles], axis=1)
    rows = [first] + [pltpu.roll(first, 16 * r, 1) for r in range(1, BLOCK)]
    for r in range(0, BLOCK, 16 // n):
        target_ref[n * r : n * r + 16, :] = jnp.concatenate(rows[r : r + 16 // n], axis=0).astype(BF16)


def band_compact(wide_ref, target_ref, slots, outs):
    n = wide_ref.shape[1]
    tiles = [jnp.zeros((n, 128), wide_ref.dtype)] * (target_ref.shape[1] // 128)
    for c in range(3):
        for a in range(3):
            tile, off = divmod(16 * slots * c + 16 * a, 128)
            tiles[tile] = tiles[tile] + turn(wide_ref[3 * c + a], off)
    first = jnp.concatenate(tiles, axis=1)
    rows = [pltpu.roll(first, 16 * r, 1) if r else first for r in range(outs)]
    rows = rows + [jnp.zeros_like(first)] * (target_ref.shape[0] // n - outs)
    for r in range(0, len(rows), 16 // n):
        target_ref[n * r : n * r + 16, :] = jnp.concatenate(rows[r : r + 16 // n], axis=0).astype(BF16)


def main_kernel(
    size, rows_ref, mask_ref, k_one_ref, k_two_ref, k_three_ref, b_one_ref, b_two_ref, b_three_ref,
    out_ref, north_ref, ocean_ref, one_ref, two_ref, three_ref,
    late_one_ref, late_two_ref, late_three_ref, bias_ref,
    wide_ref, narrow_ref, first_ref, second_ref, third_ref,
):
    top = lax.axis_index("lat") == size - 1
    col = lanes()
    for t in range(3):
        for half in range(2):
            folded = jnp.take_along_axis(rows_ref[ROWS - 1 - t, half], 127 - col, axis=1)
            folded = -folded if half == 0 else folded
            north_ref[2 * t + half] = jnp.where(top, folded, rows_ref[ROWS - 3 + t, half])
    ocean = jnp.zeros((8, 128), F32)
    for b in range(8):
        x = 0.1 * mask_ref[8 * b : 8 * b + 8, :].astype(F32)
        ocean = jnp.where(col // 16 == b, turn(x, 6 + 16 * b), ocean)
    ocean_ref[...] = ocean

    biases = []
    at = 0
    for ref in (b_one_ref, b_two_ref, b_three_ref):
        n = ref.shape[1]
        same = lax.broadcasted_iota(jnp.int32, (n, n), 0) == lax.broadcasted_iota(jnp.int32, (n, n), 1)
        column = jnp.sum(jnp.where(same, ref[...], 0.0), axis=1, keepdims=True)
        biases.append(jnp.broadcast_to(column, (n, 128)))
        bias_ref[at : at + n, :] = biases[-1]
        at += n
    band(k_one_ref, wide_ref.at[0], one_ref)
    band(k_two_ref, wide_ref.at[1], two_ref)
    band(k_three_ref, narrow_ref, three_ref)
    band_compact(wide_ref.at[0], late_one_ref, 5, 3)
    band_compact(wide_ref.at[1], late_two_ref, 5, 3)
    band_compact(narrow_ref, late_three_ref, 5, 3)
    for ref in (first_ref, second_ref, third_ref):
        for c in range(3):
            for row in (0, ROWS + 1, ROWS + 2, ROWS + 3):
                ref[c, row] = jnp.zeros((16, 128), BF16)

    for row in range(ROWS):
        x = jnp.concatenate([rows_ref[row, 0], rows_ref[row, 1]], axis=0).astype(BF16)
        for c in range(3):
            first_ref[c, row + 1] = turn(x, 1 - c)

    def layer(source, weights, at):
        parts = []
        for start in (at, at + ROWS // 2):
            for c in range(3):
                count = BLOCK + 2 if c < 2 else BLOCK + 4
                parts.append(source[c, start : start + count].reshape(16 * count, 128))
        x = jnp.concatenate(
            [jnp.concatenate(parts[0:3], axis=0), jnp.concatenate(parts[3:6], axis=0)], axis=1
        )
        return dot(weights[...], x)

    for source, weights, bias, target in (
        (first_ref, one_ref, biases[0], second_ref),
        (second_ref, two_ref, biases[1], third_ref),
    ):
        bias = jnp.concatenate([bias, bias], axis=1)
        ahead = layer(source, weights, 0)
        for at in range(0, ROWS // 2, BLOCK):
            total = ahead.reshape(BLOCK, 16, 256)
            if at + BLOCK < ROWS // 2:
                ahead = layer(source, weights, at + BLOCK)
            value = silu(total + bias[None]).astype(BF16).reshape(16 * BLOCK, 256)
            for part in range(2):
                start = at + ROWS // 2 * part + 1
                x = value[:, 128 * part : 128 * part + 128]
                for c in range(3):
                    target[c, start : start + BLOCK] = turn(x, 1 - c).reshape(BLOCK, 16, 128)

    bias = jnp.concatenate([biases[2], biases[2]], axis=1)
    ahead = layer(third_ref, three_ref, 0)
    for at in range(0, ROWS // 2, BLOCK):
        forcing = ahead.reshape(BLOCK, 8, 256) + bias[None]
        if at + BLOCK < ROWS // 2:
            ahead = layer(third_ref, three_ref, at + BLOCK)
        for part in range(2):
            for r in range(BLOCK):
                row = at + ROWS // 2 * part + r
                near = [min(max(row + d, 0), ROWS - 1) for d in (0, 1, -1)]
                q, north, south = [[rows_ref[i, half] for half in range(2)] for i in near]
                east = [turn(x, -1) for x in q]
                west = [turn(x, 1) for x in q]
                new = tendency(q, north, south, east, west)
                new[0] = new[0] + forcing[r, :, 128 * part : 128 * part + 128]
                ocean = 0.1 * mask_ref[row : row + 1, :].astype(F32)
                for half in range(2):
                    out_ref[row, half] = q[half] + ocean * new[half]


def main_pass(size, rows, mask, parameters):
    taps = pltpu.VMEM((3, ROWS + 4, 16, 128), BF16)
    block = jax.ShapeDtypeStruct
    return pl.pallas_call(
        functools.partial(main_kernel, size),
        out_shape=[
            block(rows.shape, F32),
            block((6, 8, 128), F32),
            block((8, 128), F32),
            *[block((n, DEPTH), BF16) for n in (128, 128, 64)],
            *[block(shape, BF16) for shape in ((48, 256), (48, 256), (32, 256))],
            block((40, 128), F32),
        ],
        in_specs=[VMEM] * 8,
        out_specs=[VMEM] * 10,
        scratch_shapes=[
            pltpu.VMEM((2, 9, 16, 128), BF16),
            pltpu.VMEM((9, 8, 128), F32),
            *[taps] * 3,
        ],
        compiler_params=pltpu.CompilerParams(vmem_limit_bytes=LIMIT),
        cost_estimate=pl.CostEstimate(
            flops=150000000, bytes_accessed=1500000, transcendentals=300000
        ),
        name="main_pass",
    )(rows, mask, *parameters)


def taps(rows, count):
    blank = jnp.zeros_like(rows[0])
    result = []
    for c in range(3):
        for row in rows:
            width = row.shape[1] // 128
            parts = [turn(row[:, 128 * i : 128 * i + 128], 1 - c) for i in range(width)]
            result.append(jnp.concatenate(parts, axis=1) if width > 1 else parts[0])
        result.extend([blank] * ((BLOCK + 2 if c < 2 else BLOCK + 4) - len(rows)))
    return jnp.concatenate(result, axis=0)


def strip_kernel(
    rows_ref, strip_ref, outer_ref, inner_ref, main_ref, ocean_ref, one_ref, two_ref, three_ref,
    bias_ref, cells_ref, low_ref, high_ref, side_ref, pre_one_ref, pre_two_ref, pre_three_ref,
):
    east, west = sides(inner_ref, outer_ref)
    col = lanes()
    at = col % 16
    cells = []
    for r in range(8):
        pair = [[], []]
        for half in range(2):
            block = 2 * (r // 4) + half
            own = strip_ref[r, half]
            pair[0].append(jnp.where(at < 6, own, turn(east[block], 6 - 4 * (r % 4))))
            pair[1].append(jnp.where(at < 3, turn(west[block], -4 * (r % 4)), turn(own, -3)))
        cells.append(pair)

    def own(row):
        start = 16 * (row // 8) + 4 * (row % 4)
        block = 2 * (row % 8 // 4)
        return [beside(east[block + h], start, west[block + h], start) for h in range(2)]

    low, high = [], []
    for row in list(range(6)) + list(range(ROWS - 6, ROWS)):
        side = own(row)
        slot = row if row < 3 else row - ROWS + 6
        if row < 3 or row >= ROWS - 3:
            for half in range(2):
                side_ref[slot, half] = side[half]
        parts = [
            jnp.concatenate([rows_ref[row, 0], rows_ref[row, 1]], axis=0),
            jnp.concatenate(side, axis=0),
        ]
        (low if row < 6 else high).append(jnp.concatenate(parts, axis=1).astype(BF16))
    def moved(pair, by):
        return [[turn(x, by) for x in part] for part in pair]

    cells = [moved(x, 16) for x in cells[5:8]] + cells + [moved(x, -16) for x in cells[0:3]]
    rows = []
    for pair in cells:
        parts = [jnp.concatenate(part, axis=0) for part in pair]
        rows.append(jnp.concatenate(parts, axis=1).astype(BF16))

    blank = jnp.zeros((16, 256), BF16)
    for weights, count, bias_at, pre_ref, width in (
        (one_ref, 7, 0, pre_one_ref, 256),
        (two_ref, 5, 16, pre_two_ref, 256),
        (three_ref, 3, 32, pre_three_ref, 128),
    ):
        n = weights.shape[0] // BLOCK
        more = len(rows) - 2 - BLOCK
        first = dot(weights[...], taps(rows[0:10], 256)).reshape(BLOCK, n, 256)
        if more > 0:
            second = dot(weights[0 : n * more, :], taps(rows[BLOCK:], 256)).reshape(more, n, 256)
        pairs = zip([blank] * 3 + low, high + [blank] * 3)
        operand = spread([jnp.concatenate(pair, axis=1) for pair in pairs], width)
        total = dot(weights[0 : (count + count % 2) * n, :], operand).reshape(-1, n, 2 * width)
        bias = bias_ref[bias_at : bias_at + n, :]
        first = first + jnp.concatenate([bias] * 2, axis=1)[None]
        if more > 0:
            second = second + jnp.concatenate([bias] * 2, axis=1)[None]
            rows = [silu(first[i]).astype(BF16) for i in range(BLOCK)]
            rows = rows + [silu(second[i]).astype(BF16) for i in range(more)]
        total = total + jnp.concatenate([bias] * (width // 64), axis=1)[None]
        for r in range(3):
            parts = [total[r, :, 0:width], total[count - 3 + r, :, width : 2 * width]]
            pre_ref[r] = jnp.concatenate(parts, axis=1)
        low = [silu(total[r, :, 0:width]).astype(BF16) for r in range(3, count)]
        high = [silu(total[r, :, width : 2 * width]).astype(BF16) for r in range(count - 3)]
    forcing = first

    both = []
    for r in range(8):
        new = []
        for part in range(2):
            q, north, south = [cells[i][part] for i in (r + 3, r + 4, r + 2)]
            value = tendency(
                q, north, south, [turn(x, -1) for x in q], [turn(x, 1) for x in q]
            )
            value[0] = value[0] + forcing[r, :, 128 * part : 128 * part + 128]
            new.append(value)
        ocean = ocean_ref[r : r + 1, :]
        value = [jnp.where(at < 6, new[0][half], turn(new[1][half], 3)) for half in range(2)]
        both.append([strip_ref[r, half] + ocean * value[half] for half in range(2)])

    edge = (col < 3) | (col >= 125)
    for b in range(8):
        ref, start = (low_ref, 0) if b == 0 else (high_ref, 0) if b == 7 else (cells_ref, 8 * b - 8)
        pitch = ref.shape[1]
        flat = ref.reshape(16 * pitch, 128)
        for r in range(8):
            for half in range(2):
                value = turn(both[r][half], -(16 * b + 6))
                value = jnp.where(edge, value, main_ref[8 * b + r, half])
                flat[pl.ds(8 * pitch * half + start + r, 8, stride=pitch), :] = value


def strip_pass(rows, strip, inner, outer, main, ocean, weights, bias):
    block = jax.ShapeDtypeStruct
    return pl.pallas_call(
        strip_kernel,
        out_shape=[
            block((16, ROWS - 8, 128), F32),
            *[block((16, 8, 128), F32)] * 2,
            block((6, 2, 8, 128), F32),
            *[block(shape, F32) for shape in ((3, 16, 512), (3, 16, 512), (3, 8, 256))],
        ],
        in_specs=[VMEM] * 10,
        out_specs=[VMEM] * 7,
        compiler_params=pltpu.CompilerParams(vmem_limit_bytes=LIMIT),
        cost_estimate=pl.CostEstimate(
            flops=150000000, bytes_accessed=2000000, transcendentals=100000
        ),
        name="strip_pass",
    )(rows, strip, outer, inner, main, ocean, *weights, bias)


def border_kernel(
    rows_ref, mask_ref, first_ref, second_ref, side_ref, pre_one_ref, pre_two_ref, pre_three_ref,
    one_ref, two_ref, three_ref, cells_ref, low_in_ref, high_in_ref, out_ref, low_ref, high_ref, sems,
):
    lat = lax.axis_index("lat")
    even = lax.rem(lat, 2) == 0
    span = pl.ds(8, ROWS - 16)
    source = cells_ref.at[:, pl.ds(0, ROWS - 16), :]
    stores = [pltpu.make_async_copy(source, out_ref.at[:, span, :], sems.at[0])]
    stores[0].start()

    south, north = [], []
    low, high = [], []
    for t in range(3):
        blocks = [[], [], [], []]
        for half in range(2):
            at = 2 * t + half
            corner = jnp.where(even, second_ref[6], first_ref[6])
            x = jnp.where(even, second_ref[at], first_ref[at])
            y = beside(corner, 32 * half + 4 + 4 * t, corner, 32 * half + 20 + 4 * t)
            blocks[0].append(jnp.where(lat == 0, 0.0, x))
            blocks[1].append(jnp.where(lat == 0, 0.0, y))
            corner = jnp.where(even, first_ref[6], second_ref[6])
            blocks[2].append(jnp.where(even, first_ref[at], second_ref[at]))
            blocks[3].append(beside(corner, 32 * half + 4 * t, corner, 32 * half + 16 + 4 * t))
        south.append(blocks[0])
        north.append(blocks[2])
        wide = [jnp.concatenate(x, axis=0) for x in blocks]
        low.append(jnp.concatenate(wide[0:2], axis=1).astype(BF16))
        high.append(jnp.concatenate(wide[2:4], axis=1).astype(BF16))

    def late(weights, low, high, width):
        blank = jnp.zeros((16, width), BF16)
        operand = []
        for c in range(3):
            lows = [turn_wide(x, c)[:, 0:width] for x in low] + [blank] * 2
            highs = [blank] * 2 + [turn_wide(x, c)[:, 0:width] for x in high]
            operand.extend(jnp.concatenate(pair, axis=1) for pair in zip(lows, highs))
        operand.append(jnp.zeros((16, 2 * width), BF16))
        return dot(weights[...], jnp.concatenate(operand, axis=0))

    total = late(one_ref, low, high, 256)
    low_ref[...] = low_in_ref[...]
    high_ref[...] = high_in_ref[...]
    for pre_ref, weights, width in ((pre_one_ref, two_ref, 256), (pre_two_ref, three_ref, 128)):
        value = silu(total.reshape(3, 16, 512) + pre_ref[...]).astype(BF16)
        low = [value[r, :, 0:256] for r in range(3)]
        high = [value[r, :, 256:512] for r in range(3)]
        total = late(weights, low, high, width)
    total = total.reshape(4, 8, 256)[0:3] + pre_three_ref[...]

    col = lanes()
    own = {row: [rows_ref[row, half] for half in range(2)] for row in (0, 1, 2, 3, 60, 61, 62, 63)}
    own[-1], own[ROWS] = south[2], north[0]
    for strip in range(2):
        ref, at = ((low_ref, 0), (high_ref, ROWS - 8))[strip]
        flat = ref.reshape(128, 128)
        for t in range(3):
            row = t if strip == 0 else ROWS - 3 + t
            q = own[row]
            side = [side_ref[3 * strip + t, half] for half in range(2)]
            ocean = 0.1 * mask_ref[row : row + 1, :].astype(F32)
            e = [turn(jnp.where(col == 0, y, x), -1) for x, y in zip(q, side)]
            w = [turn(jnp.where(col == 127, y, x), 1) for x, y in zip(q, side)]
            new = tendency(q, own[row + 1], own[row - 1], e, w)
            new[0] = new[0] + total[t, :, 128 * strip : 128 * strip + 128]
            for half in range(2):
                flat[pl.ds(64 * half + row - at, 8, stride=8), :] = q[half] + ocean * new[half]
        store = pltpu.make_async_copy(ref, out_ref.at[:, pl.ds(at, 8), :], sems.at[1 + strip])
        store.start()
        stores.append(store)
    for store in stores:
        store.wait()


def border_pass(rows, mask, first, second, side, pre, late, cells, low, high):
    return pl.pallas_call(
        border_kernel,
        out_shape=jax.ShapeDtypeStruct((16, ROWS, 128), F32),
        in_specs=[VMEM] * 14,
        out_specs=HBM,
        scratch_shapes=[
            pltpu.VMEM(low.shape, F32),
            pltpu.VMEM(high.shape, F32),
            pltpu.SemaphoreType.DMA((3,)),
        ],
        compiler_params=pltpu.CompilerParams(vmem_limit_bytes=LIMIT),
        cost_estimate=pl.CostEstimate(flops=60000000, bytes_accessed=1000000, transcendentals=60000),
        name="border_pass",
    )(rows, mask, first, second, side, *pre, *late, cells, low, high)


def shards(state, land_mask, kernel_one, bias_one, kernel_two, bias_two, kernel_three, bias_three):
    lon, lat = (lax.axis_size("lon"), lax.axis_size("lat"))
    biases = [x.reshape(1, x.shape[0]) for x in (bias_one, bias_two, bias_three)]
    rows, strip, outer, inner, *biases = prepare(state, biases)
    parameters = (kernel_one, kernel_two, kernel_three, *biases)

    inner = lax.ppermute(inner, "lon", [(i, i + 1 - 2 * (i % 2)) for i in range(lon)])
    outer = lax.ppermute(outer, "lon", [(i, (i + 1 if i % 2 else i - 1) % lon) for i in range(lon)])
    main, north, ocean, *weights, bias = main_pass(lat, rows, land_mask, parameters)
    weights, late = weights[0:3], weights[3:6]

    def pairs(parity):
        result = []
        for i in range(lon):
            for j in range(parity, lat - 1, 2):
                result += [(i * lat + j, i * lat + j + 1), (i * lat + j + 1, i * lat + j)]
            if parity == 1:
                result.append((i * lat, (i + 1 - 2 * (i % 2)) * lat))
            if (lat - 1) % 2 == parity:
                result.append((i * lat + lat - 1, (lon - 1 - i) * lat + lat - 1))
        return result

    first, second = corners(lat, rows, inner, outer, north)
    first = lax.ppermute(first, ("lon", "lat"), pairs(0))
    second = lax.ppermute(second, ("lon", "lat"), pairs(1))
    cells, low, high, side, *pre = strip_pass(
        rows, strip, inner, outer, main, ocean, weights, bias
    )
    return border_pass(rows, land_mask, first, second, side, pre, late, cells, low, high)


def solution(mesh):
    return jax.shard_map(
        shards,
        mesh=mesh,
        in_specs=(P(None, "lat", "lon"), P("lat", "lon"), P(), P(), P(), P(), P(), P()),
        out_specs=P(None, "lat", "lon"),
        check_vma=False,
    )
```

```python
import functools

import jax
import jax.numpy as jnp
from jax import lax
from jax.experimental import pallas as pl
from jax.experimental.pallas import tpu as pltpu
from jax.sharding import PartitionSpec as P

F32 = jnp.float32
BF16 = jnp.bfloat16

ROWS = 64
PITCH = 72
BLOCK = 8
DEPTH = 512
SPAN = (BLOCK + 2) * 16
VMEM = pl.BlockSpec(memory_space=pltpu.VMEM)
HBM = pl.BlockSpec(memory_space=pltpu.HBM)
LIMIT = 40 * 2**20


def lanes():
    return lax.broadcasted_iota(jnp.int32, (8, 128), 1)


def turn(x, by):
    if isinstance(by, int):
        by = by % 128
        if by == 0:
            return x
    return pltpu.roll(x, by, x.ndim - 1)


def silu(v):
    half = 0.5 * v
    return half + half * jnp.tanh(half)


def dot(weights, x):
    return jnp.dot(weights, x, preferred_element_type=F32)


def even_place(axis):
    return lax.rem(lax.axis_index(axis), 2) == 0


def sides(inner, outer):
    even = even_place("lon")
    return (
        [jnp.where(even, inner[i], outer[i]) for i in range(4)],
        [jnp.where(even, outer[i], inner[i]) for i in range(4)],
    )


def tendency(q, north, south, east, west):
    sub = lax.broadcasted_iota(jnp.int32, (8, 128), 0)
    swapped = pltpu.roll(q[0], 4, 0)
    u = jnp.where(sub < 4, q[0], swapped)
    v = jnp.where(sub < 4, swapped, q[0])
    result = []
    for e, w, n, s, x in zip(east, west, north, south, q):
        total = -0.5 * (u * (e - w) + v * (n - s))
        result.append(total + 0.2 * (e + w + n + s - 4.0 * x))
    return result


def beside(e, e_at, w, w_at):
    return jnp.where(lanes() < 64, turn(e, -e_at), turn(w, 125 - w_at))


def turn_wide(x, c):
    return pltpu.roll(x, (1 - c) % 256, 1) if c != 1 else x


def spread(rows, width):
    blank = jnp.zeros((16, 2 * width), BF16)
    result = []
    for c in range(3):
        for row in rows:
            parts = [turn_wide(row[:, at : at + 256], c)[:, 0:width] for at in (0, 256)]
            result.append(jnp.concatenate(parts, axis=1))
        result.extend([blank] * ((BLOCK + 2 if c < 2 else BLOCK + 4) - len(rows)))
    return jnp.concatenate(result, axis=0)


def prepare_kernel(
    state_ref, b_one_ref, b_two_ref, b_three_ref,
    rows_ref, strip_ref, outer_ref, inner_ref, h_one_ref, h_two_ref, h_three_ref, cells_ref, sems,
):
    fetches = []
    for half in range(2):
        span = pl.ds(8 * half, 8)
        target = cells_ref.at[span, pl.ds(0, ROWS), :]
        fetches.append(pltpu.make_async_copy(state_ref.at[span], target, sems.at[half]))
    biases = ((b_one_ref, h_one_ref), (b_two_ref, h_two_ref), (b_three_ref, h_three_ref))
    for source, target in biases:
        fetches.append(pltpu.make_async_copy(source, target, sems.at[len(fetches)]))
    for fetch in fetches:
        fetch.start()

    flat = cells_ref.reshape(16 * PITCH, 128)
    group = lanes() // 16
    part = (lanes() % 16) // 4
    even = even_place("lon")
    shifts = [
        [jnp.where(even, (4 * s - a) % 128, (4 * s - b) % 128) for s in range(4)]
        for a, b in ((6, 3), (3, 6))
    ]
    for fetch in fetches[0:2]:
        fetch.wait()
    strip = [[jnp.zeros((8, 128), F32)] * 8 for half in range(2)]
    for b in range(8):
        for half in range(2):
            for r in range(8):
                x = flat[pl.ds(8 * PITCH * half + 8 * b + r, 8, stride=PITCH), :]
                rows_ref[8 * b + r, half] = x
                strip[half][r] = jnp.where(group == b, turn(x, 6 + 16 * b), strip[half][r])
    for target, shift in zip((outer_ref, inner_ref), shifts):
        for q in range(2):
            for half in range(2):
                value = jnp.zeros((8, 128), F32)
                for s in range(4):
                    value = jnp.where(part == s, turn(strip[half][4 * q + s], shift[s]), value)
                target[2 * q + half] = value
    for half in range(2):
        for r in range(8):
            strip_ref[r, half] = strip[half][r]
    for fetch in fetches[2:]:
        fetch.wait()


def prepare(state, biases):
    block = jax.ShapeDtypeStruct
    arrays = [pltpu.with_memory_space_constraint(x, pltpu.HBM) for x in (state, *biases)]
    return pl.pallas_call(
        prepare_kernel,
        out_shape=[
            block((ROWS, 2, 8, 128), F32),
            block((8, 2, 8, 128), F32),
            block((4, 8, 128), F32),
            block((4, 8, 128), F32),
            *[block(x.shape, F32) for x in biases],
        ],
        in_specs=[HBM] * 4,
        out_specs=[VMEM] * 7,
        scratch_shapes=[pltpu.VMEM((16, PITCH, 128), F32), pltpu.SemaphoreType.DMA((5,))],
        compiler_params=pltpu.CompilerParams(vmem_limit_bytes=LIMIT),
        cost_estimate=pl.CostEstimate(flops=400000, bytes_accessed=1200000, transcendentals=0),
        name="rows_edges",
    )(*arrays)


def corners_kernel(size, rows_ref, outer_ref, inner_ref, north_ref, first_ref, second_ref):
    lat = lax.axis_index("lat")
    even = lax.rem(lat, 2) == 0
    for t in range(3):
        for half in range(2):
            at = 2 * t + half
            low = rows_ref[t, half]
            first_ref[at] = jnp.where(even, north_ref[at], low)
            second_ref[at] = jnp.where(even, low, north_ref[at])
    top = lat == size - 1
    col = lanes()
    part = col // 16
    straight = even_place("lon")
    mirrored = straight != top
    index = jnp.where(top, 112 + 4 * (3 - col // 4 % 4) + 2 - col % 4, 112 + col % 16)
    low = high = jnp.zeros((8, 128), F32)
    for i in range(4):
        half = i // 2
        pair = (inner_ref, outer_ref) if i % 2 == 0 else (outer_ref, inner_ref)
        x = jnp.where(straight, pair[0][half], pair[1][half])
        low = jnp.where(part == i, turn(x, 16 * i), low)
        x = jnp.where(mirrored, pair[0][2 + half], pair[1][2 + half])
        high = jnp.where(part == i, jnp.take_along_axis(x, index, axis=1), high)
    high = jnp.where(top & (col < 32), -high, high)
    first_ref[6] = jnp.where(even, high, low)
    second_ref[6] = jnp.where(even, low, high)


def corners(size, rows, inner, outer, north):
    return pl.pallas_call(
        functools.partial(corners_kernel, size),
        out_shape=[jax.ShapeDtypeStruct((7, 8, 128), F32)] * 2,
        in_specs=[VMEM] * 4,
        out_specs=[VMEM] * 2,
        compiler_params=pltpu.CompilerParams(vmem_limit_bytes=LIMIT),
        cost_estimate=pl.CostEstimate(flops=1000, bytes_accessed=100000, transcendentals=0),
        name="add_corners",
    )(rows, outer, inner, north)


def band(kernel_ref, wide_ref, target_ref):
    n = kernel_ref.shape[2]
    wide_ref[...] = jnp.zeros_like(wide_ref)
    tiles = [None] * (DEPTH // 128)
    for c in range(3):
        for a in range(3):
            wide_ref[3 * c + a, :, 0:16] = kernel_ref[a, c].astype(wide_ref.dtype)
            tile, off = divmod(SPAN * c + 16 * a, 128)
            x = turn(wide_ref[3 * c + a], off)
            tiles[tile] = x if tiles[tile] is None else tiles[tile] + x
    blank = jnp.zeros((n, 128), wide_ref.dtype)
    first = jnp.concatenate([blank if x is None else x for x in tiles], axis=1)
    rows = [first] + [pltpu.roll(first, 16 * r, 1) for r in range(1, BLOCK)]
    for r in range(0, BLOCK, 16 // n):
        target_ref[n * r : n * r + 16, :] = jnp.concatenate(rows[r : r + 16 // n], axis=0).astype(BF16)


def band_compact(wide_ref, target_ref, slots, outs):
    n = wide_ref.shape[1]
    tiles = [jnp.zeros((n, 128), wide_ref.dtype)] * (target_ref.shape[1] // 128)
    for c in range(3):
        for a in range(3):
            tile, off = divmod(16 * slots * c + 16 * a, 128)
            tiles[tile] = tiles[tile] + turn(wide_ref[3 * c + a], off)
    first = jnp.concatenate(tiles, axis=1)
    rows = [pltpu.roll(first, 16 * r, 1) if r else first for r in range(outs)]
    rows = rows + [jnp.zeros_like(first)] * (target_ref.shape[0] // n - outs)
    for r in range(0, len(rows), 16 // n):
        target_ref[n * r : n * r + 16, :] = jnp.concatenate(rows[r : r + 16 // n], axis=0).astype(BF16)


def main_kernel(
    size, rows_ref, mask_ref, k_one_ref, k_two_ref, k_three_ref, b_one_ref, b_two_ref, b_three_ref,
    out_ref, north_ref, ocean_ref, one_ref, two_ref, three_ref,
    late_one_ref, late_two_ref, late_three_ref, bias_ref,
    wide_ref, narrow_ref, first_ref, second_ref, third_ref,
):
    top = lax.axis_index("lat") == size - 1
    col = lanes()
    for t in range(3):
        for half in range(2):
            folded = jnp.take_along_axis(rows_ref[ROWS - 1 - t, half], 127 - col, axis=1)
            folded = -folded if half == 0 else folded
            north_ref[2 * t + half] = jnp.where(top, folded, rows_ref[ROWS - 3 + t, half])
    ocean = jnp.zeros((8, 128), F32)
    for b in range(8):
        x = 0.1 * mask_ref[8 * b : 8 * b + 8, :].astype(F32)
        ocean = jnp.where(col // 16 == b, turn(x, 6 + 16 * b), ocean)
    ocean_ref[...] = ocean

    biases = []
    at = 0
    for ref in (b_one_ref, b_two_ref, b_three_ref):
        n = ref.shape[1]
        same = lax.broadcasted_iota(jnp.int32, (n, n), 0) == lax.broadcasted_iota(jnp.int32, (n, n), 1)
        column = jnp.sum(jnp.where(same, ref[...], 0.0), axis=1, keepdims=True)
        biases.append(jnp.broadcast_to(column, (n, 128)))
        bias_ref[at : at + n, :] = biases[-1]
        at += n
    band(k_one_ref, wide_ref.at[0], one_ref)
    band(k_two_ref, wide_ref.at[1], two_ref)
    band(k_three_ref, narrow_ref, three_ref)
    band_compact(wide_ref.at[0], late_one_ref, 5, 3)
    band_compact(wide_ref.at[1], late_two_ref, 5, 3)
    band_compact(narrow_ref, late_three_ref, 5, 3)
    for ref in (first_ref, second_ref, third_ref):
        for c in range(3):
            for row in (0, ROWS + 1, ROWS + 2, ROWS + 3):
                ref[c, row] = jnp.zeros((16, 128), BF16)

    for row in range(ROWS):
        x = jnp.concatenate([rows_ref[row, 0], rows_ref[row, 1]], axis=0).astype(BF16)
        for c in range(3):
            first_ref[c, row + 1] = turn(x, 1 - c)

    def layer(source, weights, at):
        parts = []
        for start in (at, at + ROWS // 2):
            for c in range(3):
                count = BLOCK + 2 if c < 2 else BLOCK + 4
                parts.append(source[c, start : start + count].reshape(16 * count, 128))
        x = jnp.concatenate(
            [jnp.concatenate(parts[0:3], axis=0), jnp.concatenate(parts[3:6], axis=0)], axis=1
        )
        return dot(weights[...], x)

    for source, weights, bias, target in (
        (first_ref, one_ref, biases[0], second_ref),
        (second_ref, two_ref, biases[1], third_ref),
    ):
        bias = jnp.concatenate([bias, bias], axis=1)
        ahead = layer(source, weights, 0)
        for at in range(0, ROWS // 2, BLOCK):
            total = ahead.reshape(BLOCK, 16, 256)
            if at + BLOCK < ROWS // 2:
                ahead = layer(source, weights, at + BLOCK)
            value = silu(total + bias[None]).astype(BF16).reshape(16 * BLOCK, 256)
            for part in range(2):
                start = at + ROWS // 2 * part + 1
                x = value[:, 128 * part : 128 * part + 128]
                for c in range(3):
                    target[c, start : start + BLOCK] = turn(x, 1 - c).reshape(BLOCK, 16, 128)

    bias = jnp.concatenate([biases[2], biases[2]], axis=1)
    ahead = layer(third_ref, three_ref, 0)
    for at in range(0, ROWS // 2, BLOCK):
        forcing = ahead.reshape(BLOCK, 8, 256) + bias[None]
        if at + BLOCK < ROWS // 2:
            ahead = layer(third_ref, three_ref, at + BLOCK)
        for part in range(2):
            for r in range(BLOCK):
                row = at + ROWS // 2 * part + r
                near = [min(max(row + d, 0), ROWS - 1) for d in (0, 1, -1)]
                q, north, south = [[rows_ref[i, half] for half in range(2)] for i in near]
                east = [turn(x, -1) for x in q]
                west = [turn(x, 1) for x in q]
                new = tendency(q, north, south, east, west)
                new[0] = new[0] + forcing[r, :, 128 * part : 128 * part + 128]
                ocean = 0.1 * mask_ref[row : row + 1, :].astype(F32)
                for half in range(2):
                    out_ref[row, half] = q[half] + ocean * new[half]


def main_pass(size, rows, mask, parameters):
    taps = pltpu.VMEM((3, ROWS + 4, 16, 128), BF16)
    block = jax.ShapeDtypeStruct
    return pl.pallas_call(
        functools.partial(main_kernel, size),
        out_shape=[
            block(rows.shape, F32),
            block((6, 8, 128), F32),
            block((8, 128), F32),
            *[block((n, DEPTH), BF16) for n in (128, 128, 64)],
            *[block(shape, BF16) for shape in ((48, 256), (48, 256), (32, 256))],
            block((40, 128), F32),
        ],
        in_specs=[VMEM] * 8,
        out_specs=[VMEM] * 10,
        scratch_shapes=[
            pltpu.VMEM((2, 9, 16, 128), BF16),
            pltpu.VMEM((9, 8, 128), F32),
            *[taps] * 3,
        ],
        compiler_params=pltpu.CompilerParams(vmem_limit_bytes=LIMIT),
        cost_estimate=pl.CostEstimate(
            flops=150000000, bytes_accessed=1500000, transcendentals=300000
        ),
        name="main_pass",
    )(rows, mask, *parameters)


def taps(rows, count):
    blank = jnp.zeros_like(rows[0])
    result = []
    for c in range(3):
        for row in rows:
            width = row.shape[1] // 128
            parts = [turn(row[:, 128 * i : 128 * i + 128], 1 - c) for i in range(width)]
            result.append(jnp.concatenate(parts, axis=1) if width > 1 else parts[0])
        result.extend([blank] * ((BLOCK + 2 if c < 2 else BLOCK + 4) - len(rows)))
    return jnp.concatenate(result, axis=0)


def strip_kernel(
    rows_ref, strip_ref, outer_ref, inner_ref, main_ref, ocean_ref, one_ref, two_ref, three_ref,
    bias_ref, cells_ref, low_ref, high_ref, side_ref, pre_one_ref, pre_two_ref, pre_three_ref,
):
    east, west = sides(inner_ref, outer_ref)
    col = lanes()
    at = col % 16
    cells = []
    for r in range(8):
        pair = [[], []]
        for half in range(2):
            block = 2 * (r // 4) + half
            own = strip_ref[r, half]
            pair[0].append(jnp.where(at < 6, own, turn(east[block], 6 - 4 * (r % 4))))
            pair[1].append(jnp.where(at < 3, turn(west[block], -4 * (r % 4)), turn(own, -3)))
        cells.append(pair)

    def own(row):
        start = 16 * (row // 8) + 4 * (row % 4)
        block = 2 * (row % 8 // 4)
        return [beside(east[block + h], start, west[block + h], start) for h in range(2)]

    low, high = [], []
    for row in list(range(6)) + list(range(ROWS - 6, ROWS)):
        side = own(row)
        slot = row if row < 3 else row - ROWS + 6
        if row < 3 or row >= ROWS - 3:
            for half in range(2):
                side_ref[slot, half] = side[half]
        parts = [
            jnp.concatenate([rows_ref[row, 0], rows_ref[row, 1]], axis=0),
            jnp.concatenate(side, axis=0),
        ]
        (low if row < 6 else high).append(jnp.concatenate(parts, axis=1).astype(BF16))
    def moved(pair, by):
        return [[turn(x, by) for x in part] for part in pair]

    cells = [moved(x, 16) for x in cells[5:8]] + cells + [moved(x, -16) for x in cells[0:3]]
    rows = []
    for pair in cells:
        parts = [jnp.concatenate(part, axis=0) for part in pair]
        rows.append(jnp.concatenate(parts, axis=1).astype(BF16))

    blank = jnp.zeros((16, 256), BF16)
    for weights, count, bias_at, pre_ref, width in (
        (one_ref, 7, 0, pre_one_ref, 256),
        (two_ref, 5, 16, pre_two_ref, 256),
        (three_ref, 3, 32, pre_three_ref, 128),
    ):
        n = weights.shape[0] // BLOCK
        more = len(rows) - 2 - BLOCK
        first = dot(weights[...], taps(rows[0:10], 256)).reshape(BLOCK, n, 256)
        if more > 0:
            second = dot(weights[0 : n * more, :], taps(rows[BLOCK:], 256)).reshape(more, n, 256)
        pairs = zip([blank] * 3 + low, high + [blank] * 3)
        operand = spread([jnp.concatenate(pair, axis=1) for pair in pairs], width)
        total = dot(weights[0 : (count + count % 2) * n, :], operand).reshape(-1, n, 2 * width)
        bias = bias_ref[bias_at : bias_at + n, :]
        first = first + jnp.concatenate([bias] * 2, axis=1)[None]
        if more > 0:
            second = second + jnp.concatenate([bias] * 2, axis=1)[None]
            rows = [silu(first[i]).astype(BF16) for i in range(BLOCK)]
            rows = rows + [silu(second[i]).astype(BF16) for i in range(more)]
        total = total + jnp.concatenate([bias] * (width // 64), axis=1)[None]
        for r in range(3):
            parts = [total[r, :, 0:width], total[count - 3 + r, :, width : 2 * width]]
            pre_ref[r] = jnp.concatenate(parts, axis=1)
        low = [silu(total[r, :, 0:width]).astype(BF16) for r in range(3, count)]
        high = [silu(total[r, :, width : 2 * width]).astype(BF16) for r in range(count - 3)]
    forcing = first

    both = []
    for r in range(8):
        new = []
        for part in range(2):
            q, north, south = [cells[i][part] for i in (r + 3, r + 4, r + 2)]
            value = tendency(
                q, north, south, [turn(x, -1) for x in q], [turn(x, 1) for x in q]
            )
            value[0] = value[0] + forcing[r, :, 128 * part : 128 * part + 128]
            new.append(value)
        ocean = ocean_ref[r : r + 1, :]
        value = [jnp.where(at < 6, new[0][half], turn(new[1][half], 3)) for half in range(2)]
        both.append([strip_ref[r, half] + ocean * value[half] for half in range(2)])

    edge = (col < 3) | (col >= 125)
    for b in range(8):
        ref, start = (low_ref, 0) if b == 0 else (high_ref, 0) if b == 7 else (cells_ref, 8 * b - 8)
        pitch = ref.shape[1]
        flat = ref.reshape(16 * pitch, 128)
        for r in range(8):
            for half in range(2):
                value = turn(both[r][half], -(16 * b + 6))
                value = jnp.where(edge, value, main_ref[8 * b + r, half])
                flat[pl.ds(8 * pitch * half + start + r, 8, stride=pitch), :] = value


def strip_pass(rows, strip, inner, outer, main, ocean, weights, bias):
    block = jax.ShapeDtypeStruct
    return pl.pallas_call(
        strip_kernel,
        out_shape=[
            block((16, ROWS - 8, 128), F32),
            *[block((16, 8, 128), F32)] * 2,
            block((6, 2, 8, 128), F32),
            *[block(shape, F32) for shape in ((3, 16, 512), (3, 16, 512), (3, 8, 256))],
        ],
        in_specs=[VMEM] * 10,
        out_specs=[VMEM] * 7,
        compiler_params=pltpu.CompilerParams(vmem_limit_bytes=LIMIT),
        cost_estimate=pl.CostEstimate(
            flops=150000000, bytes_accessed=2000000, transcendentals=100000
        ),
        name="strip_pass",
    )(rows, strip, outer, inner, main, ocean, *weights, bias)


def border_kernel(
    rows_ref, mask_ref, first_ref, second_ref, side_ref, pre_one_ref, pre_two_ref, pre_three_ref,
    one_ref, two_ref, three_ref, cells_ref, low_in_ref, high_in_ref, out_ref, low_ref, high_ref, sems,
):
    lat = lax.axis_index("lat")
    even = lax.rem(lat, 2) == 0
    span = pl.ds(8, ROWS - 16)
    source = cells_ref.at[:, pl.ds(0, ROWS - 16), :]
    stores = [pltpu.make_async_copy(source, out_ref.at[:, span, :], sems.at[0])]
    stores[0].start()

    south, north = [], []
    low, high = [], []
    for t in range(3):
        blocks = [[], [], [], []]
        for half in range(2):
            at = 2 * t + half
            corner = jnp.where(even, second_ref[6], first_ref[6])
            x = jnp.where(even, second_ref[at], first_ref[at])
            y = beside(corner, 32 * half + 4 + 4 * t, corner, 32 * half + 20 + 4 * t)
            blocks[0].append(jnp.where(lat == 0, 0.0, x))
            blocks[1].append(jnp.where(lat == 0, 0.0, y))
            corner = jnp.where(even, first_ref[6], second_ref[6])
            blocks[2].append(jnp.where(even, first_ref[at], second_ref[at]))
            blocks[3].append(beside(corner, 32 * half + 4 * t, corner, 32 * half + 16 + 4 * t))
        south.append(blocks[0])
        north.append(blocks[2])
        wide = [jnp.concatenate(x, axis=0) for x in blocks]
        low.append(jnp.concatenate(wide[0:2], axis=1).astype(BF16))
        high.append(jnp.concatenate(wide[2:4], axis=1).astype(BF16))

    def late(weights, low, high, width):
        blank = jnp.zeros((16, width), BF16)
        operand = []
        for c in range(3):
            lows = [turn_wide(x, c)[:, 0:width] for x in low] + [blank] * 2
            highs = [blank] * 2 + [turn_wide(x, c)[:, 0:width] for x in high]
            operand.extend(jnp.concatenate(pair, axis=1) for pair in zip(lows, highs))
        operand.append(jnp.zeros((16, 2 * width), BF16))
        return dot(weights[...], jnp.concatenate(operand, axis=0))

    total = late(one_ref, low, high, 256)
    low_ref[...] = low_in_ref[...]
    high_ref[...] = high_in_ref[...]
    col = lanes()
    own = {row: [rows_ref[row, half] for half in range(2)] for row in (0, 1, 2, 3, 60, 61, 62, 63)}
    own[-1], own[ROWS] = south[2], north[0]
    ready = []
    for at, row in enumerate((0, 1, 2, ROWS - 3, ROWS - 2, ROWS - 1)):
        q = own[row]
        side = [side_ref[at, half] for half in range(2)]
        e = [turn(jnp.where(col == 0, y, x), -1) for x, y in zip(q, side)]
        w = [turn(jnp.where(col == 127, y, x), 1) for x, y in zip(q, side)]
        new = tendency(q, own[row + 1], own[row - 1], e, w)
        ocean = 0.1 * mask_ref[row : row + 1, :].astype(F32)
        ready.append((q[0] + ocean * new[0], q[1] + ocean * new[1], ocean))

    for pre_ref, weights, width in ((pre_one_ref, two_ref, 256), (pre_two_ref, three_ref, 128)):
        value = silu(total.reshape(3, 16, 512) + pre_ref[...]).astype(BF16)
        low = [value[r, :, 0:256] for r in range(3)]
        high = [value[r, :, 256:512] for r in range(3)]
        total = late(weights, low, high, width)
    total = total.reshape(4, 8, 256)[0:3] + pre_three_ref[...]

    for strip in range(2):
        ref, at, start = ((low_ref, 0, 0), (high_ref, ROWS - 8, 5))[strip]
        flat = ref.reshape(128, 128)
        for t in range(3):
            first, second, ocean = ready[3 * strip + t]
            forcing = total[t, :, 128 * strip : 128 * strip + 128]
            new = (first + ocean * forcing, second)
            row = start + t
            for half in range(2):
                flat[pl.ds(64 * half + row, 8, stride=8), :] = new[half]
        store = pltpu.make_async_copy(ref, out_ref.at[:, pl.ds(at, 8), :], sems.at[1 + strip])
        store.start()
        stores.append(store)
    for store in stores:
        store.wait()


def border_pass(rows, mask, first, second, side, pre, late, cells, low, high):
    return pl.pallas_call(
        border_kernel,
        out_shape=jax.ShapeDtypeStruct((16, ROWS, 128), F32),
        in_specs=[VMEM] * 14,
        out_specs=HBM,
        scratch_shapes=[
            pltpu.VMEM(low.shape, F32),
            pltpu.VMEM(high.shape, F32),
            pltpu.SemaphoreType.DMA((3,)),
        ],
        compiler_params=pltpu.CompilerParams(vmem_limit_bytes=LIMIT),
        cost_estimate=pl.CostEstimate(flops=60000000, bytes_accessed=1000000, transcendentals=60000),
        name="border_pass",
    )(rows, mask, first, second, side, *pre, *late, cells, low, high)


def shards(state, land_mask, kernel_one, bias_one, kernel_two, bias_two, kernel_three, bias_three):
    lon, lat = (lax.axis_size("lon"), lax.axis_size("lat"))
    biases = [x.reshape(1, x.shape[0]) for x in (bias_one, bias_two, bias_three)]
    rows, strip, outer, inner, *biases = prepare(state, biases)
    parameters = (kernel_one, kernel_two, kernel_three, *biases)

    inner = lax.ppermute(inner, "lon", [(i, i + 1 - 2 * (i % 2)) for i in range(lon)])
    outer = lax.ppermute(outer, "lon", [(i, (i + 1 if i % 2 else i - 1) % lon) for i in range(lon)])
    main, north, ocean, *weights, bias = main_pass(lat, rows, land_mask, parameters)
    weights, late = weights[0:3], weights[3:6]

    def pairs(parity):
        result = []
        for i in range(lon):
            for j in range(parity, lat - 1, 2):
                result += [(i * lat + j, i * lat + j + 1), (i * lat + j + 1, i * lat + j)]
            if parity == 1:
                result.append((i * lat, (i + 1 - 2 * (i % 2)) * lat))
            if (lat - 1) % 2 == parity:
                result.append((i * lat + lat - 1, (lon - 1 - i) * lat + lat - 1))
        return result

    first, second = corners(lat, rows, inner, outer, north)
    first = lax.ppermute(first, ("lon", "lat"), pairs(0))
    second = lax.ppermute(second, ("lon", "lat"), pairs(1))
    cells, low, high, side, *pre = strip_pass(
        rows, strip, inner, outer, main, ocean, weights, bias
    )
    return border_pass(rows, land_mask, first, second, side, pre, late, cells, low, high)


def solution(mesh):
    return jax.shard_map(
        shards,
        mesh=mesh,
        in_specs=(P(None, "lat", "lon"), P("lat", "lon"), P(), P(), P(), P(), P(), P()),
        out_specs=P(None, "lat", "lon"),
        check_vma=False,
    )
```

```python
import functools

import jax
import jax.numpy as jnp
from jax import lax
from jax.experimental import pallas as pl
from jax.experimental.pallas import tpu as pltpu
from jax.sharding import PartitionSpec as P

F32 = jnp.float32
BF16 = jnp.bfloat16

ROWS = 64
PITCH = 72
BLOCK = 8
DEPTH = 512
SPAN = (BLOCK + 2) * 16
VMEM = pl.BlockSpec(memory_space=pltpu.VMEM)
HBM = pl.BlockSpec(memory_space=pltpu.HBM)
LIMIT = 40 * 2**20


def lanes():
    return lax.broadcasted_iota(jnp.int32, (8, 128), 1)


def turn(x, by):
    if isinstance(by, int):
        by = by % 128
        if by == 0:
            return x
    return pltpu.roll(x, by, x.ndim - 1)


def silu(v):
    half = 0.5 * v
    return half + half * jnp.tanh(half)


def dot(weights, x):
    return jnp.dot(weights, x, preferred_element_type=F32)


def even_place(axis):
    return lax.rem(lax.axis_index(axis), 2) == 0


def sides(inner, outer):
    even = even_place("lon")
    return (
        [jnp.where(even, inner[i], outer[i]) for i in range(4)],
        [jnp.where(even, outer[i], inner[i]) for i in range(4)],
    )


def tendency(q, north, south, east, west):
    sub = lax.broadcasted_iota(jnp.int32, (8, 128), 0)
    swapped = pltpu.roll(q[0], 4, 0)
    u = jnp.where(sub < 4, q[0], swapped)
    v = jnp.where(sub < 4, swapped, q[0])
    result = []
    for e, w, n, s, x in zip(east, west, north, south, q):
        total = -0.5 * (u * (e - w) + v * (n - s))
        result.append(total + 0.2 * (e + w + n + s - 4.0 * x))
    return result


def beside(e, e_at, w, w_at):
    return jnp.where(lanes() < 64, turn(e, -e_at), turn(w, 125 - w_at))


def turn_wide(x, c):
    return pltpu.roll(x, (1 - c) % 256, 1) if c != 1 else x


def spread(rows, width):
    blank = jnp.zeros((16, 2 * width), BF16)
    result = []
    for c in range(3):
        for row in rows:
            parts = [turn_wide(row[:, at : at + 256], c)[:, 0:width] for at in (0, 256)]
            result.append(jnp.concatenate(parts, axis=1))
        result.extend([blank] * ((BLOCK + 2 if c < 2 else BLOCK + 4) - len(rows)))
    return jnp.concatenate(result, axis=0)


def prepare_kernel(
    state_ref, b_one_ref, b_two_ref, b_three_ref,
    rows_ref, strip_ref, outer_ref, inner_ref, h_one_ref, h_two_ref, h_three_ref, cells_ref, sems,
):
    fetches = []
    for half in range(2):
        span = pl.ds(8 * half, 8)
        target = cells_ref.at[span, pl.ds(0, ROWS), :]
        fetches.append(pltpu.make_async_copy(state_ref.at[span], target, sems.at[half]))
    biases = ((b_one_ref, h_one_ref), (b_two_ref, h_two_ref), (b_three_ref, h_three_ref))
    for source, target in biases:
        fetches.append(pltpu.make_async_copy(source, target, sems.at[len(fetches)]))
    for fetch in fetches:
        fetch.start()

    flat = cells_ref.reshape(16 * PITCH, 128)
    group = lanes() // 16
    part = (lanes() % 16) // 4
    even = even_place("lon")
    shifts = [
        [jnp.where(even, (4 * s - a) % 128, (4 * s - b) % 128) for s in range(4)]
        for a, b in ((6, 3), (3, 6))
    ]
    for fetch in fetches[0:2]:
        fetch.wait()
    strip = [[jnp.zeros((8, 128), F32)] * 8 for half in range(2)]
    for b in range(8):
        for half in range(2):
            for r in range(8):
                x = flat[pl.ds(8 * PITCH * half + 8 * b + r, 8, stride=PITCH), :]
                rows_ref[8 * b + r, half] = x
                strip[half][r] = jnp.where(group == b, turn(x, 6 + 16 * b), strip[half][r])
    for target, shift in zip((outer_ref, inner_ref), shifts):
        for q in range(2):
            for half in range(2):
                value = jnp.zeros((8, 128), F32)
                for s in range(4):
                    value = jnp.where(part == s, turn(strip[half][4 * q + s], shift[s]), value)
                target[2 * q + half] = value
    for half in range(2):
        for r in range(8):
            strip_ref[r, half] = strip[half][r]
    for fetch in fetches[2:]:
        fetch.wait()


def prepare(state, biases):
    block = jax.ShapeDtypeStruct
    arrays = [pltpu.with_memory_space_constraint(x, pltpu.HBM) for x in (state, *biases)]
    return pl.pallas_call(
        prepare_kernel,
        out_shape=[
            block((ROWS, 2, 8, 128), F32),
            block((8, 2, 8, 128), F32),
            block((4, 8, 128), F32),
            block((4, 8, 128), F32),
            *[block(x.shape, F32) for x in biases],
        ],
        in_specs=[HBM] * 4,
        out_specs=[VMEM] * 7,
        scratch_shapes=[pltpu.VMEM((16, PITCH, 128), F32), pltpu.SemaphoreType.DMA((5,))],
        compiler_params=pltpu.CompilerParams(vmem_limit_bytes=LIMIT),
        cost_estimate=pl.CostEstimate(flops=400000, bytes_accessed=1200000, transcendentals=0),
        name="rows_edges",
    )(*arrays)


def corners_kernel(size, rows_ref, outer_ref, inner_ref, north_ref, first_ref, second_ref):
    lat = lax.axis_index("lat")
    even = lax.rem(lat, 2) == 0
    for t in range(3):
        for half in range(2):
            at = 2 * t + half
            low = rows_ref[t, half]
            first_ref[at] = jnp.where(even, north_ref[at], low)
            second_ref[at] = jnp.where(even, low, north_ref[at])
    top = lat == size - 1
    col = lanes()
    part = col // 16
    straight = even_place("lon")
    mirrored = straight != top
    index = jnp.where(top, 112 + 4 * (3 - col // 4 % 4) + 2 - col % 4, 112 + col % 16)
    low = high = jnp.zeros((8, 128), F32)
    for i in range(4):
        half = i // 2
        pair = (inner_ref, outer_ref) if i % 2 == 0 else (outer_ref, inner_ref)
        x = jnp.where(straight, pair[0][half], pair[1][half])
        low = jnp.where(part == i, turn(x, 16 * i), low)
        x = jnp.where(mirrored, pair[0][2 + half], pair[1][2 + half])
        high = jnp.where(part == i, jnp.take_along_axis(x, index, axis=1), high)
    high = jnp.where(top & (col < 32), -high, high)
    first_ref[6] = jnp.where(even, high, low)
    second_ref[6] = jnp.where(even, low, high)


def corners(size, rows, inner, outer, north):
    return pl.pallas_call(
        functools.partial(corners_kernel, size),
        out_shape=[jax.ShapeDtypeStruct((7, 8, 128), F32)] * 2,
        in_specs=[VMEM] * 4,
        out_specs=[VMEM] * 2,
        compiler_params=pltpu.CompilerParams(vmem_limit_bytes=LIMIT),
        cost_estimate=pl.CostEstimate(flops=1000, bytes_accessed=100000, transcendentals=0),
        name="add_corners",
    )(rows, outer, inner, north)


def band(kernel_ref, wide_ref, target_ref):
    n = kernel_ref.shape[2]
    wide_ref[...] = jnp.zeros_like(wide_ref)
    tiles = [None] * (DEPTH // 128)
    for c in range(3):
        for a in range(3):
            wide_ref[3 * c + a, :, 0:16] = kernel_ref[a, c].astype(wide_ref.dtype)
            tile, off = divmod(SPAN * c + 16 * a, 128)
            x = turn(wide_ref[3 * c + a], off)
            tiles[tile] = x if tiles[tile] is None else tiles[tile] + x
    blank = jnp.zeros((n, 128), wide_ref.dtype)
    first = jnp.concatenate([blank if x is None else x for x in tiles], axis=1)
    rows = [first] + [pltpu.roll(first, 16 * r, 1) for r in range(1, BLOCK)]
    for r in range(0, BLOCK, 16 // n):
        target_ref[n * r : n * r + 16, :] = jnp.concatenate(rows[r : r + 16 // n], axis=0).astype(BF16)


def band_compact(wide_ref, target_ref, slots, outs):
    n = wide_ref.shape[1]
    tiles = [jnp.zeros((n, 128), wide_ref.dtype)] * (target_ref.shape[1] // 128)
    for c in range(3):
        for a in range(3):
            tile, off = divmod(16 * slots * c + 16 * a, 128)
            tiles[tile] = tiles[tile] + turn(wide_ref[3 * c + a], off)
    first = jnp.concatenate(tiles, axis=1)
    rows = [pltpu.roll(first, 16 * r, 1) if r else first for r in range(outs)]
    rows = rows + [jnp.zeros_like(first)] * (target_ref.shape[0] // n - outs)
    for r in range(0, len(rows), 16 // n):
        target_ref[n * r : n * r + 16, :] = jnp.concatenate(rows[r : r + 16 // n], axis=0).astype(BF16)


def main_kernel(
    size, rows_ref, mask_ref, k_one_ref, k_two_ref, k_three_ref, b_one_ref, b_two_ref, b_three_ref,
    out_ref, north_ref, ocean_ref, one_ref, two_ref, three_ref,
    late_one_ref, late_two_ref, late_three_ref, bias_ref,
    wide_ref, narrow_ref, first_ref, second_ref, third_ref,
):
    top = lax.axis_index("lat") == size - 1
    col = lanes()
    for t in range(3):
        for half in range(2):
            folded = jnp.take_along_axis(rows_ref[ROWS - 1 - t, half], 127 - col, axis=1)
            folded = -folded if half == 0 else folded
            north_ref[2 * t + half] = jnp.where(top, folded, rows_ref[ROWS - 3 + t, half])
    ocean = jnp.zeros((8, 128), F32)
    for b in range(8):
        x = 0.1 * mask_ref[8 * b : 8 * b + 8, :].astype(F32)
        ocean = jnp.where(col // 16 == b, turn(x, 6 + 16 * b), ocean)
    ocean_ref[...] = ocean

    biases = []
    at = 0
    for ref in (b_one_ref, b_two_ref, b_three_ref):
        n = ref.shape[1]
        same = lax.broadcasted_iota(jnp.int32, (n, n), 0) == lax.broadcasted_iota(jnp.int32, (n, n), 1)
        column = jnp.sum(jnp.where(same, ref[...], 0.0), axis=1, keepdims=True)
        biases.append(jnp.broadcast_to(column, (n, 128)))
        bias_ref[at : at + n, :] = biases[-1]
        at += n
    band(k_one_ref, wide_ref.at[0], one_ref)
    band(k_two_ref, wide_ref.at[1], two_ref)
    band(k_three_ref, narrow_ref, three_ref)
    band_compact(wide_ref.at[0], late_one_ref, 5, 3)
    band_compact(wide_ref.at[1], late_two_ref, 5, 3)
    band_compact(narrow_ref, late_three_ref, 5, 3)
    for ref in (first_ref, second_ref, third_ref):
        for c in range(3):
            for row in (0, ROWS + 1, ROWS + 2, ROWS + 3):
                ref[c, row] = jnp.zeros((16, 128), BF16)

    for row in range(ROWS):
        x = jnp.concatenate([rows_ref[row, 0], rows_ref[row, 1]], axis=0).astype(BF16)
        for c in range(3):
            first_ref[c, row + 1] = turn(x, 1 - c)

    def layer(source, weights, at):
        parts = []
        for start in (at, at + ROWS // 2):
            for c in range(3):
                count = BLOCK + 2 if c < 2 else BLOCK + 4
                parts.append(source[c, start : start + count].reshape(16 * count, 128))
        x = jnp.concatenate(
            [jnp.concatenate(parts[0:3], axis=0), jnp.concatenate(parts[3:6], axis=0)], axis=1
        )
        return dot(weights[...], x)

    for source, weights, bias, target in (
        (first_ref, one_ref, biases[0], second_ref),
        (second_ref, two_ref, biases[1], third_ref),
    ):
        bias = jnp.concatenate([bias, bias], axis=1)
        ahead = layer(source, weights, 0)
        for at in range(0, ROWS // 2, BLOCK):
            total = ahead.reshape(BLOCK, 16, 256)
            if at + BLOCK < ROWS // 2:
                ahead = layer(source, weights, at + BLOCK)
            value = silu(total + bias[None]).astype(BF16).reshape(16 * BLOCK, 256)
            for part in range(2):
                start = at + ROWS // 2 * part + 1
                x = value[:, 128 * part : 128 * part + 128]
                for c in range(3):
                    target[c, start : start + BLOCK] = turn(x, 1 - c).reshape(BLOCK, 16, 128)

    bias = jnp.concatenate([biases[2], biases[2]], axis=1)
    ahead = layer(third_ref, three_ref, 0)
    for at in range(0, ROWS // 2, BLOCK):
        forcing = ahead.reshape(BLOCK, 8, 256) + bias[None]
        if at + BLOCK < ROWS // 2:
            ahead = layer(third_ref, three_ref, at + BLOCK)
        for part in range(2):
            for r in range(BLOCK):
                row = at + ROWS // 2 * part + r
                near = [min(max(row + d, 0), ROWS - 1) for d in (0, 1, -1)]
                q, north, south = [[rows_ref[i, half] for half in range(2)] for i in near]
                east = [turn(x, -1) for x in q]
                west = [turn(x, 1) for x in q]
                new = tendency(q, north, south, east, west)
                new[0] = new[0] + forcing[r, :, 128 * part : 128 * part + 128]
                ocean = 0.1 * mask_ref[row : row + 1, :].astype(F32)
                for half in range(2):
                    out_ref[row, half] = q[half] + ocean * new[half]


def main_pass(size, rows, mask, parameters):
    taps = pltpu.VMEM((3, ROWS + 4, 16, 128), BF16)
    block = jax.ShapeDtypeStruct
    return pl.pallas_call(
        functools.partial(main_kernel, size),
        out_shape=[
            block(rows.shape, F32),
            block((6, 8, 128), F32),
            block((8, 128), F32),
            *[block((n, DEPTH), BF16) for n in (128, 128, 64)],
            *[block(shape, BF16) for shape in ((48, 256), (48, 256), (32, 256))],
            block((40, 128), F32),
        ],
        in_specs=[VMEM] * 8,
        out_specs=[VMEM] * 10,
        scratch_shapes=[
            pltpu.VMEM((2, 9, 16, 128), BF16),
            pltpu.VMEM((9, 8, 128), F32),
            *[taps] * 3,
        ],
        compiler_params=pltpu.CompilerParams(vmem_limit_bytes=LIMIT),
        cost_estimate=pl.CostEstimate(
            flops=150000000, bytes_accessed=1500000, transcendentals=300000
        ),
        name="main_pass",
    )(rows, mask, *parameters)


def taps(rows, count):
    blank = jnp.zeros_like(rows[0])
    result = []
    for c in range(3):
        for row in rows:
            width = row.shape[1] // 128
            parts = [turn(row[:, 128 * i : 128 * i + 128], 1 - c) for i in range(width)]
            result.append(jnp.concatenate(parts, axis=1) if width > 1 else parts[0])
        result.extend([blank] * ((BLOCK + 2 if c < 2 else BLOCK + 4) - len(rows)))
    return jnp.concatenate(result, axis=0)


def strip_kernel(
    rows_ref, strip_ref, outer_ref, inner_ref, main_ref, ocean_ref, one_ref, two_ref, three_ref,
    bias_ref, cells_ref, low_ref, high_ref, side_ref, pre_one_ref, pre_two_ref, pre_three_ref,
):
    east, west = sides(inner_ref, outer_ref)
    col = lanes()
    at = col % 16
    cells = []
    for r in range(8):
        pair = [[], []]
        for half in range(2):
            block = 2 * (r // 4) + half
            own = strip_ref[r, half]
            pair[0].append(jnp.where(at < 6, own, turn(east[block], 6 - 4 * (r % 4))))
            pair[1].append(jnp.where(at < 3, turn(west[block], -4 * (r % 4)), turn(own, -3)))
        cells.append(pair)

    def own(row):
        start = 16 * (row // 8) + 4 * (row % 4)
        block = 2 * (row % 8 // 4)
        return [beside(east[block + h], start, west[block + h], start) for h in range(2)]

    low, high = [], []
    for row in list(range(6)) + list(range(ROWS - 6, ROWS)):
        side = own(row)
        slot = row if row < 3 else row - ROWS + 6
        if row < 3 or row >= ROWS - 3:
            for half in range(2):
                side_ref[slot, half] = side[half]
        parts = [
            jnp.concatenate([rows_ref[row, 0], rows_ref[row, 1]], axis=0),
            jnp.concatenate(side, axis=0),
        ]
        (low if row < 6 else high).append(jnp.concatenate(parts, axis=1).astype(BF16))
    def moved(pair, by):
        return [[turn(x, by) for x in part] for part in pair]

    cells = [moved(x, 16) for x in cells[5:8]] + cells + [moved(x, -16) for x in cells[0:3]]
    rows = []
    for pair in cells:
        parts = [jnp.concatenate(part, axis=0) for part in pair]
        rows.append(jnp.concatenate(parts, axis=1).astype(BF16))

    blank = jnp.zeros((16, 256), BF16)
    for weights, count, bias_at, pre_ref, width in (
        (one_ref, 7, 0, pre_one_ref, 256),
        (two_ref, 5, 16, pre_two_ref, 256),
        (three_ref, 3, 32, pre_three_ref, 128),
    ):
        n = weights.shape[0] // BLOCK
        more = len(rows) - 2 - BLOCK
        first = dot(weights[...], taps(rows[0:10], 256)).reshape(BLOCK, n, 256)
        if more > 0:
            second = dot(weights[0 : n * more, :], taps(rows[BLOCK:], 256)).reshape(more, n, 256)
        pairs = zip([blank] * 3 + low, high + [blank] * 3)
        operand = spread([jnp.concatenate(pair, axis=1) for pair in pairs], width)
        total = dot(weights[0 : (count + count % 2) * n, :], operand).reshape(-1, n, 2 * width)
        bias = bias_ref[bias_at : bias_at + n, :]
        first = first + jnp.concatenate([bias] * 2, axis=1)[None]
        if more > 0:
            second = second + jnp.concatenate([bias] * 2, axis=1)[None]
            rows = [silu(first[i]).astype(BF16) for i in range(BLOCK)]
            rows = rows + [silu(second[i]).astype(BF16) for i in range(more)]
        total = total + jnp.concatenate([bias] * (width // 64), axis=1)[None]
        for r in range(3):
            parts = [total[r, :, 0:width], total[count - 3 + r, :, width : 2 * width]]
            pre_ref[r] = jnp.concatenate(parts, axis=1)
        low = [silu(total[r, :, 0:width]).astype(BF16) for r in range(3, count)]
        high = [silu(total[r, :, width : 2 * width]).astype(BF16) for r in range(count - 3)]
    forcing = first

    both = []
    for r in range(8):
        new = []
        for part in range(2):
            q, north, south = [cells[i][part] for i in (r + 3, r + 4, r + 2)]
            value = tendency(
                q, north, south, [turn(x, -1) for x in q], [turn(x, 1) for x in q]
            )
            value[0] = value[0] + forcing[r, :, 128 * part : 128 * part + 128]
            new.append(value)
        ocean = ocean_ref[r : r + 1, :]
        value = [jnp.where(at < 6, new[0][half], turn(new[1][half], 3)) for half in range(2)]
        both.append([strip_ref[r, half] + ocean * value[half] for half in range(2)])

    edge = (col < 3) | (col >= 125)
    for b in range(8):
        ref, start = (low_ref, 0) if b == 0 else (high_ref, 0) if b == 7 else (cells_ref, 8 * b - 8)
        pitch = ref.shape[1]
        flat = ref.reshape(16 * pitch, 128)
        for r in range(8):
            for half in range(2):
                value = turn(both[r][half], -(16 * b + 6))
                value = jnp.where(edge, value, main_ref[8 * b + r, half])
                flat[pl.ds(8 * pitch * half + start + r, 8, stride=pitch), :] = value


def strip_pass(rows, strip, inner, outer, main, ocean, weights, bias):
    block = jax.ShapeDtypeStruct
    return pl.pallas_call(
        strip_kernel,
        out_shape=[
            block((16, ROWS - 8, 128), F32),
            *[block((16, 8, 128), F32)] * 2,
            block((6, 2, 8, 128), F32),
            *[block(shape, F32) for shape in ((3, 16, 512), (3, 16, 512), (3, 8, 256))],
        ],
        in_specs=[VMEM] * 10,
        out_specs=[VMEM] * 7,
        compiler_params=pltpu.CompilerParams(vmem_limit_bytes=LIMIT),
        cost_estimate=pl.CostEstimate(
            flops=150000000, bytes_accessed=2000000, transcendentals=100000
        ),
        name="strip_pass",
    )(rows, strip, outer, inner, main, ocean, *weights, bias)


def copy_middle(cells_ref, out_ref, sem):
    source = cells_ref.at[:, pl.ds(0, ROWS - 16), :]
    return pltpu.make_async_copy(source, out_ref.at[:, pl.ds(8, ROWS - 16), :], sem)


def early_middle(lat, size):
    return lat == size - 2


def middle_kernel(size, cells_ref, out_ref, sem):
    @pl.when(early_middle(lax.axis_index("lat"), size))
    def _():
        copy = copy_middle(cells_ref, out_ref, sem)
        copy.start()
        copy.wait()


def store_middle(size, cells):
    return pl.pallas_call(
        functools.partial(middle_kernel, size),
        out_shape=jax.ShapeDtypeStruct((16, ROWS, 128), F32),
        in_specs=[VMEM],
        out_specs=HBM,
        scratch_shapes=[pltpu.SemaphoreType.DMA(())],
        compiler_params=pltpu.CompilerParams(vmem_limit_bytes=LIMIT),
        cost_estimate=pl.CostEstimate(flops=1000, bytes_accessed=800000, transcendentals=0),
        name="store_middle",
    )(cells)


def border_kernel(
    size, rows_ref, mask_ref, first_ref, second_ref, side_ref, pre_one_ref, pre_two_ref, pre_three_ref,
    one_ref, two_ref, three_ref, cells_ref, low_in_ref, high_in_ref, _, out_ref, low_ref, high_ref, sems,
):
    lat = lax.axis_index("lat")
    even = lax.rem(lat, 2) == 0
    middle = copy_middle(cells_ref, out_ref, sems.at[0])
    late_middle = jnp.logical_not(early_middle(lat, size))

    @pl.when(late_middle)
    def _():
        middle.start()

    south, north = [], []
    low, high = [], []
    for t in range(3):
        blocks = [[], [], [], []]
        for half in range(2):
            at = 2 * t + half
            corner = jnp.where(even, second_ref[6], first_ref[6])
            x = jnp.where(even, second_ref[at], first_ref[at])
            y = beside(corner, 32 * half + 4 + 4 * t, corner, 32 * half + 20 + 4 * t)
            blocks[0].append(jnp.where(lat == 0, 0.0, x))
            blocks[1].append(jnp.where(lat == 0, 0.0, y))
            corner = jnp.where(even, first_ref[6], second_ref[6])
            blocks[2].append(jnp.where(even, first_ref[at], second_ref[at]))
            blocks[3].append(beside(corner, 32 * half + 4 * t, corner, 32 * half + 16 + 4 * t))
        south.append(blocks[0])
        north.append(blocks[2])
        wide = [jnp.concatenate(x, axis=0) for x in blocks]
        low.append(jnp.concatenate(wide[0:2], axis=1).astype(BF16))
        high.append(jnp.concatenate(wide[2:4], axis=1).astype(BF16))

    def late(weights, low, high, width):
        blank = jnp.zeros((16, width), BF16)
        operand = []
        for c in range(3):
            lows = [turn_wide(x, c)[:, 0:width] for x in low] + [blank] * 2
            highs = [blank] * 2 + [turn_wide(x, c)[:, 0:width] for x in high]
            operand.extend(jnp.concatenate(pair, axis=1) for pair in zip(lows, highs))
        operand.append(jnp.zeros((16, 2 * width), BF16))
        return dot(weights[...], jnp.concatenate(operand, axis=0))

    total = late(one_ref, low, high, 256)
    low_ref[...] = low_in_ref[...]
    high_ref[...] = high_in_ref[...]
    col = lanes()
    own = {row: [rows_ref[row, half] for half in range(2)] for row in (0, 1, 2, 3, 60, 61, 62, 63)}
    own[-1], own[ROWS] = south[2], north[0]
    ready = []
    for at, row in enumerate((0, 1, 2, ROWS - 3, ROWS - 2, ROWS - 1)):
        q = own[row]
        side = [side_ref[at, half] for half in range(2)]
        e = [turn(jnp.where(col == 0, y, x), -1) for x, y in zip(q, side)]
        w = [turn(jnp.where(col == 127, y, x), 1) for x, y in zip(q, side)]
        new = tendency(q, own[row + 1], own[row - 1], e, w)
        ocean = 0.1 * mask_ref[row : row + 1, :].astype(F32)
        ready.append((q[0] + ocean * new[0], q[1] + ocean * new[1], ocean))

    for pre_ref, weights, width in ((pre_one_ref, two_ref, 256), (pre_two_ref, three_ref, 128)):
        value = silu(total.reshape(3, 16, 512) + pre_ref[...]).astype(BF16)
        low = [value[r, :, 0:256] for r in range(3)]
        high = [value[r, :, 256:512] for r in range(3)]
        total = late(weights, low, high, width)
    total = total.reshape(4, 8, 256)[0:3] + pre_three_ref[...]

    stores = []
    for strip in range(2):
        ref, at, start = ((low_ref, 0, 0), (high_ref, ROWS - 8, 5))[strip]
        flat = ref.reshape(128, 128)
        for t in range(3):
            first, second, ocean = ready[3 * strip + t]
            forcing = total[t, :, 128 * strip : 128 * strip + 128]
            new = (first + ocean * forcing, second)
            row = start + t
            for half in range(2):
                flat[pl.ds(64 * half + row, 8, stride=8), :] = new[half]
        store = pltpu.make_async_copy(ref, out_ref.at[:, pl.ds(at, 8), :], sems.at[1 + strip])
        store.start()
        stores.append(store)
    for store in stores:
        store.wait()

    @pl.when(late_middle)
    def _():
        middle.wait()


def border_pass(size, rows, mask, first, second, side, pre, late, cells, low, high, out):
    return pl.pallas_call(
        functools.partial(border_kernel, size),
        out_shape=jax.ShapeDtypeStruct((16, ROWS, 128), F32),
        in_specs=[VMEM] * 14 + [HBM],
        out_specs=HBM,
        input_output_aliases={14: 0},
        scratch_shapes=[
            pltpu.VMEM(low.shape, F32),
            pltpu.VMEM(high.shape, F32),
            pltpu.SemaphoreType.DMA((3,)),
        ],
        compiler_params=pltpu.CompilerParams(vmem_limit_bytes=LIMIT),
        cost_estimate=pl.CostEstimate(flops=60000000, bytes_accessed=1000000, transcendentals=60000),
        name="border_pass",
    )(rows, mask, first, second, side, *pre, *late, cells, low, high, out)


def shards(state, land_mask, kernel_one, bias_one, kernel_two, bias_two, kernel_three, bias_three):
    lon, lat = (lax.axis_size("lon"), lax.axis_size("lat"))
    biases = [x.reshape(1, x.shape[0]) for x in (bias_one, bias_two, bias_three)]
    rows, strip, outer, inner, *biases = prepare(state, biases)
    parameters = (kernel_one, kernel_two, kernel_three, *biases)

    inner = lax.ppermute(inner, "lon", [(i, i + 1 - 2 * (i % 2)) for i in range(lon)])
    outer = lax.ppermute(outer, "lon", [(i, (i + 1 if i % 2 else i - 1) % lon) for i in range(lon)])
    main, north, ocean, *weights, bias = main_pass(lat, rows, land_mask, parameters)
    weights, late = weights[0:3], weights[3:6]

    def pairs(parity):
        result = []
        for i in range(lon):
            for j in range(parity, lat - 1, 2):
                result += [(i * lat + j, i * lat + j + 1), (i * lat + j + 1, i * lat + j)]
            if parity == 1:
                result.append((i * lat, (i + 1 - 2 * (i % 2)) * lat))
            if (lat - 1) % 2 == parity:
                result.append((i * lat + lat - 1, (lon - 1 - i) * lat + lat - 1))
        return result

    first, second = corners(lat, rows, inner, outer, north)
    first = lax.ppermute(first, ("lon", "lat"), pairs(0))
    second = lax.ppermute(second, ("lon", "lat"), pairs(1))
    cells, low, high, side, *pre = strip_pass(
        rows, strip, inner, outer, main, ocean, weights, bias
    )
    out = store_middle(lat, cells)
    return border_pass(
        lat, rows, land_mask, first, second, side, pre, late, cells, low, high, out
    )


def solution(mesh):
    return jax.shard_map(
        shards,
        mesh=mesh,
        in_specs=(P(None, "lat", "lon"), P("lat", "lon"), P(), P(), P(), P(), P(), P()),
        out_specs=P(None, "lat", "lon"),
        check_vma=False,
    )
```

```python
import functools

import jax
import jax.numpy as jnp
from jax import lax
from jax.experimental import pallas as pl
from jax.experimental.pallas import tpu as pltpu
from jax.sharding import PartitionSpec as P

F32 = jnp.float32
BF16 = jnp.bfloat16

ROWS = 64
PITCH = 72
BLOCK = 8
DEPTH = 512
SPAN = (BLOCK + 2) * 16
VMEM = pl.BlockSpec(memory_space=pltpu.VMEM)
HBM = pl.BlockSpec(memory_space=pltpu.HBM)
LIMIT = 40 * 2**20


def lanes():
    return lax.broadcasted_iota(jnp.int32, (8, 128), 1)


def turn(x, by):
    if isinstance(by, int):
        by = by % 128
        if by == 0:
            return x
    return pltpu.roll(x, by, x.ndim - 1)


def silu(v):
    half = 0.5 * v
    return half + half * jnp.tanh(half)


def dot(weights, x):
    return jnp.dot(weights, x, preferred_element_type=F32)


def even_place(axis):
    return lax.rem(lax.axis_index(axis), 2) == 0


def sides(inner, outer):
    even = even_place("lon")
    return (
        [jnp.where(even, inner[i], outer[i]) for i in range(4)],
        [jnp.where(even, outer[i], inner[i]) for i in range(4)],
    )


def tendency(q, north, south, east, west):
    sub = lax.broadcasted_iota(jnp.int32, (8, 128), 0)
    swapped = pltpu.roll(q[0], 4, 0)
    u = jnp.where(sub < 4, q[0], swapped)
    v = jnp.where(sub < 4, swapped, q[0])
    result = []
    for e, w, n, s, x in zip(east, west, north, south, q):
        total = -0.5 * (u * (e - w) + v * (n - s))
        result.append(total + 0.2 * (e + w + n + s - 4.0 * x))
    return result


def beside(e, e_at, w, w_at):
    return jnp.where(lanes() < 64, turn(e, -e_at), turn(w, 125 - w_at))


def turn_wide(x, c):
    return pltpu.roll(x, (1 - c) % 256, 1) if c != 1 else x


def spread(rows, width):
    blank = jnp.zeros((16, 2 * width), BF16)
    result = []
    for c in range(3):
        for row in rows:
            parts = [turn_wide(row[:, at : at + 256], c)[:, 0:width] for at in (0, 256)]
            result.append(jnp.concatenate(parts, axis=1))
        result.extend([blank] * ((BLOCK + 2 if c < 2 else BLOCK + 4) - len(rows)))
    return jnp.concatenate(result, axis=0)


def prepare_kernel(
    state_ref, b_one_ref, b_two_ref, b_three_ref,
    rows_ref, strip_ref, outer_ref, inner_ref, h_one_ref, h_two_ref, h_three_ref, cells_ref, sems,
):
    fetches = []
    for half in range(2):
        span = pl.ds(8 * half, 8)
        target = cells_ref.at[span, pl.ds(0, ROWS), :]
        fetches.append(pltpu.make_async_copy(state_ref.at[span], target, sems.at[half]))
    biases = ((b_one_ref, h_one_ref), (b_two_ref, h_two_ref), (b_three_ref, h_three_ref))
    for source, target in biases:
        fetches.append(pltpu.make_async_copy(source, target, sems.at[len(fetches)]))
    for fetch in fetches:
        fetch.start()

    flat = cells_ref.reshape(16 * PITCH, 128)
    group = lanes() // 16
    part = (lanes() % 16) // 4
    even = even_place("lon")
    shifts = [
        [jnp.where(even, (4 * s - a) % 128, (4 * s - b) % 128) for s in range(4)]
        for a, b in ((6, 3), (3, 6))
    ]
    for fetch in fetches[0:2]:
        fetch.wait()
    strip = [[jnp.zeros((8, 128), F32)] * 8 for half in range(2)]
    for b in range(8):
        for half in range(2):
            for r in range(8):
                x = flat[pl.ds(8 * PITCH * half + 8 * b + r, 8, stride=PITCH), :]
                rows_ref[8 * b + r, half] = x
                strip[half][r] = jnp.where(group == b, turn(x, 6 + 16 * b), strip[half][r])
    for target, shift in zip((outer_ref, inner_ref), shifts):
        for q in range(2):
            for half in range(2):
                value = jnp.zeros((8, 128), F32)
                for s in range(4):
                    value = jnp.where(part == s, turn(strip[half][4 * q + s], shift[s]), value)
                target[2 * q + half] = value
    for half in range(2):
        for r in range(8):
            strip_ref[r, half] = strip[half][r]
    for fetch in fetches[2:]:
        fetch.wait()


def prepare(state, biases):
    block = jax.ShapeDtypeStruct
    arrays = [pltpu.with_memory_space_constraint(x, pltpu.HBM) for x in (state, *biases)]
    return pl.pallas_call(
        prepare_kernel,
        out_shape=[
            block((ROWS, 2, 8, 128), F32),
            block((8, 2, 8, 128), F32),
            block((4, 8, 128), F32),
            block((4, 8, 128), F32),
            *[block(x.shape, F32) for x in biases],
        ],
        in_specs=[HBM] * 4,
        out_specs=[VMEM] * 7,
        scratch_shapes=[pltpu.VMEM((16, PITCH, 128), F32), pltpu.SemaphoreType.DMA((5,))],
        compiler_params=pltpu.CompilerParams(vmem_limit_bytes=LIMIT),
        cost_estimate=pl.CostEstimate(flops=400000, bytes_accessed=1200000, transcendentals=0),
        name="rows_edges",
    )(*arrays)


def corners_kernel(size, rows_ref, outer_ref, inner_ref, north_ref, first_ref, second_ref):
    lat = lax.axis_index("lat")
    even = lax.rem(lat, 2) == 0
    for t in range(3):
        for half in range(2):
            at = 2 * t + half
            low = rows_ref[t, half]
            first_ref[at] = jnp.where(even, north_ref[at], low)
            second_ref[at] = jnp.where(even, low, north_ref[at])
    top = lat == size - 1
    col = lanes()
    part = col // 16
    straight = even_place("lon")
    mirrored = straight != top
    index = jnp.where(top, 112 + 4 * (3 - col // 4 % 4) + 2 - col % 4, 112 + col % 16)
    low = high = jnp.zeros((8, 128), F32)
    for i in range(4):
        half = i // 2
        pair = (inner_ref, outer_ref) if i % 2 == 0 else (outer_ref, inner_ref)
        x = jnp.where(straight, pair[0][half], pair[1][half])
        low = jnp.where(part == i, turn(x, 16 * i), low)
        x = jnp.where(mirrored, pair[0][2 + half], pair[1][2 + half])
        high = jnp.where(part == i, jnp.take_along_axis(x, index, axis=1), high)
    high = jnp.where(top & (col < 32), -high, high)
    first_ref[6] = jnp.where(even, high, low)
    second_ref[6] = jnp.where(even, low, high)


def corners(size, rows, inner, outer, north):
    return pl.pallas_call(
        functools.partial(corners_kernel, size),
        out_shape=[jax.ShapeDtypeStruct((7, 8, 128), F32)] * 2,
        in_specs=[VMEM] * 4,
        out_specs=[VMEM] * 2,
        compiler_params=pltpu.CompilerParams(vmem_limit_bytes=LIMIT),
        cost_estimate=pl.CostEstimate(flops=1000, bytes_accessed=100000, transcendentals=0),
        name="add_corners",
    )(rows, outer, inner, north)


def band(kernel_ref, wide_ref, target_ref):
    n = kernel_ref.shape[2]
    wide_ref[...] = jnp.zeros_like(wide_ref)
    tiles = [None] * (DEPTH // 128)
    for c in range(3):
        for a in range(3):
            wide_ref[3 * c + a, :, 0:16] = kernel_ref[a, c].astype(wide_ref.dtype)
            tile, off = divmod(SPAN * c + 16 * a, 128)
            x = turn(wide_ref[3 * c + a], off)
            tiles[tile] = x if tiles[tile] is None else tiles[tile] + x
    blank = jnp.zeros((n, 128), wide_ref.dtype)
    first = jnp.concatenate([blank if x is None else x for x in tiles], axis=1)
    rows = [first] + [pltpu.roll(first, 16 * r, 1) for r in range(1, BLOCK)]
    for r in range(0, BLOCK, 16 // n):
        target_ref[n * r : n * r + 16, :] = jnp.concatenate(rows[r : r + 16 // n], axis=0).astype(BF16)


def band_compact(wide_ref, target_ref, slots, outs):
    n = wide_ref.shape[1]
    tiles = [jnp.zeros((n, 128), wide_ref.dtype)] * (target_ref.shape[1] // 128)
    for c in range(3):
        for a in range(3):
            tile, off = divmod(16 * slots * c + 16 * a, 128)
            tiles[tile] = tiles[tile] + turn(wide_ref[3 * c + a], off)
    first = jnp.concatenate(tiles, axis=1)
    rows = [pltpu.roll(first, 16 * r, 1) if r else first for r in range(outs)]
    rows = rows + [jnp.zeros_like(first)] * (target_ref.shape[0] // n - outs)
    for r in range(0, len(rows), 16 // n):
        target_ref[n * r : n * r + 16, :] = jnp.concatenate(rows[r : r + 16 // n], axis=0).astype(BF16)


def main_kernel(
    size, rows_ref, mask_ref, k_one_ref, k_two_ref, k_three_ref, b_one_ref, b_two_ref, b_three_ref,
    out_ref, north_ref, ocean_ref, one_ref, two_ref, three_ref,
    late_one_ref, late_two_ref, late_three_ref, bias_ref,
    wide_ref, narrow_ref, first_ref, second_ref, third_ref,
):
    top = lax.axis_index("lat") == size - 1
    col = lanes()
    for t in range(3):
        for half in range(2):
            folded = jnp.take_along_axis(rows_ref[ROWS - 1 - t, half], 127 - col, axis=1)
            folded = -folded if half == 0 else folded
            north_ref[2 * t + half] = jnp.where(top, folded, rows_ref[ROWS - 3 + t, half])
    ocean = jnp.zeros((8, 128), F32)
    for b in range(8):
        x = 0.1 * mask_ref[8 * b : 8 * b + 8, :].astype(F32)
        ocean = jnp.where(col // 16 == b, turn(x, 6 + 16 * b), ocean)
    ocean_ref[...] = ocean

    biases = []
    at = 0
    for ref in (b_one_ref, b_two_ref, b_three_ref):
        n = ref.shape[1]
        same = lax.broadcasted_iota(jnp.int32, (n, n), 0) == lax.broadcasted_iota(jnp.int32, (n, n), 1)
        column = jnp.sum(jnp.where(same, ref[...], 0.0), axis=1, keepdims=True)
        biases.append(jnp.broadcast_to(column, (n, 128)))
        bias_ref[at : at + n, :] = biases[-1]
        at += n
    band(k_one_ref, wide_ref.at[0], one_ref)
    band(k_two_ref, wide_ref.at[1], two_ref)
    band(k_three_ref, narrow_ref, three_ref)
    band_compact(wide_ref.at[0], late_one_ref, 5, 3)
    band_compact(wide_ref.at[1], late_two_ref, 5, 3)
    band_compact(narrow_ref, late_three_ref, 5, 3)
    for ref in (first_ref, second_ref, third_ref):
        for c in range(3):
            for row in (0, ROWS + 1, ROWS + 2, ROWS + 3):
                ref[c, row] = jnp.zeros((16, 128), BF16)

    for row in range(ROWS):
        x = jnp.concatenate([rows_ref[row, 0], rows_ref[row, 1]], axis=0).astype(BF16)
        for c in range(3):
            first_ref[c, row + 1] = turn(x, 1 - c)

    def layer(source, weights, at):
        parts = []
        for start in (at, at + ROWS // 2):
            for c in range(3):
                count = BLOCK + 2 if c < 2 else BLOCK + 4
                parts.append(source[c, start : start + count].reshape(16 * count, 128))
        x = jnp.concatenate(
            [jnp.concatenate(parts[0:3], axis=0), jnp.concatenate(parts[3:6], axis=0)], axis=1
        )
        return dot(weights[...], x)

    for source, weights, bias, target in (
        (first_ref, one_ref, biases[0], second_ref),
        (second_ref, two_ref, biases[1], third_ref),
    ):
        bias = jnp.concatenate([bias, bias], axis=1)
        ahead = layer(source, weights, 0)
        for at in range(0, ROWS // 2, BLOCK):
            total = ahead.reshape(BLOCK, 16, 256)
            if at + BLOCK < ROWS // 2:
                ahead = layer(source, weights, at + BLOCK)
            value = silu(total + bias[None]).astype(BF16).reshape(16 * BLOCK, 256)
            for part in range(2):
                start = at + ROWS // 2 * part + 1
                x = value[:, 128 * part : 128 * part + 128]
                for c in range(3):
                    target[c, start : start + BLOCK] = turn(x, 1 - c).reshape(BLOCK, 16, 128)

    bias = jnp.concatenate([biases[2], biases[2]], axis=1)
    ahead = layer(third_ref, three_ref, 0)
    for at in range(0, ROWS // 2, BLOCK):
        forcing = ahead.reshape(BLOCK, 8, 256) + bias[None]
        if at + BLOCK < ROWS // 2:
            ahead = layer(third_ref, three_ref, at + BLOCK)
        for part in range(2):
            for r in range(BLOCK):
                row = at + ROWS // 2 * part + r
                near = [min(max(row + d, 0), ROWS - 1) for d in (0, 1, -1)]
                q, north, south = [[rows_ref[i, half] for half in range(2)] for i in near]
                east = [turn(x, -1) for x in q]
                west = [turn(x, 1) for x in q]
                new = tendency(q, north, south, east, west)
                new[0] = new[0] + forcing[r, :, 128 * part : 128 * part + 128]
                ocean = 0.1 * mask_ref[row : row + 1, :].astype(F32)
                for half in range(2):
                    out_ref[row, half] = q[half] + ocean * new[half]


def main_pass(size, rows, mask, parameters):
    taps = pltpu.VMEM((3, ROWS + 4, 16, 128), BF16)
    block = jax.ShapeDtypeStruct
    return pl.pallas_call(
        functools.partial(main_kernel, size),
        out_shape=[
            block(rows.shape, F32),
            block((6, 8, 128), F32),
            block((8, 128), F32),
            *[block((n, DEPTH), BF16) for n in (128, 128, 64)],
            *[block(shape, BF16) for shape in ((48, 256), (48, 256), (32, 256))],
            block((40, 128), F32),
        ],
        in_specs=[VMEM] * 8,
        out_specs=[VMEM] * 10,
        scratch_shapes=[
            pltpu.VMEM((2, 9, 16, 128), BF16),
            pltpu.VMEM((9, 8, 128), F32),
            *[taps] * 3,
        ],
        compiler_params=pltpu.CompilerParams(vmem_limit_bytes=LIMIT),
        cost_estimate=pl.CostEstimate(
            flops=150000000, bytes_accessed=1500000, transcendentals=300000
        ),
        name="main_pass",
    )(rows, mask, *parameters)


def taps(rows, count):
    blank = jnp.zeros_like(rows[0])
    result = []
    for c in range(3):
        for row in rows:
            width = row.shape[1] // 128
            parts = [turn(row[:, 128 * i : 128 * i + 128], 1 - c) for i in range(width)]
            result.append(jnp.concatenate(parts, axis=1) if width > 1 else parts[0])
        result.extend([blank] * ((BLOCK + 2 if c < 2 else BLOCK + 4) - len(rows)))
    return jnp.concatenate(result, axis=0)


def strip_kernel(
    rows_ref, strip_ref, outer_ref, inner_ref, main_ref, ocean_ref, one_ref, two_ref, three_ref,
    bias_ref, cells_ref, low_ref, high_ref, side_ref, pre_one_ref, pre_two_ref, pre_three_ref,
):
    east, west = sides(inner_ref, outer_ref)
    col = lanes()
    at = col % 16
    cells = []
    for r in range(8):
        pair = [[], []]
        for half in range(2):
            block = 2 * (r // 4) + half
            own = strip_ref[r, half]
            pair[0].append(jnp.where(at < 6, own, turn(east[block], 6 - 4 * (r % 4))))
            pair[1].append(jnp.where(at < 3, turn(west[block], -4 * (r % 4)), turn(own, -3)))
        cells.append(pair)

    def own(row):
        start = 16 * (row // 8) + 4 * (row % 4)
        block = 2 * (row % 8 // 4)
        return [beside(east[block + h], start, west[block + h], start) for h in range(2)]

    low, high = [], []
    for row in list(range(6)) + list(range(ROWS - 6, ROWS)):
        side = own(row)
        slot = row if row < 3 else row - ROWS + 6
        if row < 3 or row >= ROWS - 3:
            for half in range(2):
                side_ref[slot, half] = side[half]
        parts = [
            jnp.concatenate([rows_ref[row, 0], rows_ref[row, 1]], axis=0),
            jnp.concatenate(side, axis=0),
        ]
        (low if row < 6 else high).append(jnp.concatenate(parts, axis=1).astype(BF16))
    def moved(pair, by):
        return [[turn(x, by) for x in part] for part in pair]

    cells = [moved(x, 16) for x in cells[5:8]] + cells + [moved(x, -16) for x in cells[0:3]]
    rows = []
    for pair in cells:
        parts = [jnp.concatenate(part, axis=0) for part in pair]
        rows.append(jnp.concatenate(parts, axis=1).astype(BF16))

    blank = jnp.zeros((16, 256), BF16)
    for weights, count, bias_at, pre_ref, width in (
        (one_ref, 7, 0, pre_one_ref, 256),
        (two_ref, 5, 16, pre_two_ref, 256),
        (three_ref, 3, 32, pre_three_ref, 128),
    ):
        n = weights.shape[0] // BLOCK
        more = len(rows) - 2 - BLOCK
        first = dot(weights[...], taps(rows[0:10], 256)).reshape(BLOCK, n, 256)
        if more > 0:
            second = dot(weights[0 : n * more, :], taps(rows[BLOCK:], 256)).reshape(more, n, 256)
        pairs = zip([blank] * 3 + low, high + [blank] * 3)
        operand = spread([jnp.concatenate(pair, axis=1) for pair in pairs], width)
        total = dot(weights[0 : (count + count % 2) * n, :], operand).reshape(-1, n, 2 * width)
        bias = bias_ref[bias_at : bias_at + n, :]
        first = first + jnp.concatenate([bias] * 2, axis=1)[None]
        if more > 0:
            second = second + jnp.concatenate([bias] * 2, axis=1)[None]
            rows = [silu(first[i]).astype(BF16) for i in range(BLOCK)]
            rows = rows + [silu(second[i]).astype(BF16) for i in range(more)]
        total = total + jnp.concatenate([bias] * (width // 64), axis=1)[None]
        for r in range(3):
            parts = [total[r, :, 0:width], total[count - 3 + r, :, width : 2 * width]]
            pre_ref[r] = jnp.concatenate(parts, axis=1)
        low = [silu(total[r, :, 0:width]).astype(BF16) for r in range(3, count)]
        high = [silu(total[r, :, width : 2 * width]).astype(BF16) for r in range(count - 3)]
    forcing = first

    both = []
    for r in range(8):
        new = []
        for part in range(2):
            q, north, south = [cells[i][part] for i in (r + 3, r + 4, r + 2)]
            value = tendency(
                q, north, south, [turn(x, -1) for x in q], [turn(x, 1) for x in q]
            )
            value[0] = value[0] + forcing[r, :, 128 * part : 128 * part + 128]
            new.append(value)
        ocean = ocean_ref[r : r + 1, :]
        value = [jnp.where(at < 6, new[0][half], turn(new[1][half], 3)) for half in range(2)]
        both.append([strip_ref[r, half] + ocean * value[half] for half in range(2)])

    edge = (col < 3) | (col >= 125)
    for b in range(8):
        ref, start = (low_ref, 0) if b == 0 else (high_ref, 0) if b == 7 else (cells_ref, 8 * b - 8)
        pitch = ref.shape[1]
        flat = ref.reshape(16 * pitch, 128)
        for r in range(8):
            for half in range(2):
                value = turn(both[r][half], -(16 * b + 6))
                value = jnp.where(edge, value, main_ref[8 * b + r, half])
                flat[pl.ds(8 * pitch * half + start + r, 8, stride=pitch), :] = value


def strip_pass(rows, strip, inner, outer, main, ocean, weights, bias):
    block = jax.ShapeDtypeStruct
    return pl.pallas_call(
        strip_kernel,
        out_shape=[
            block((16, ROWS - 8, 128), F32),
            *[block((16, 8, 128), F32)] * 2,
            block((6, 2, 8, 128), F32),
            *[block(shape, F32) for shape in ((3, 16, 512), (3, 16, 512), (3, 8, 256))],
        ],
        in_specs=[VMEM] * 10,
        out_specs=[VMEM] * 7,
        compiler_params=pltpu.CompilerParams(vmem_limit_bytes=LIMIT),
        cost_estimate=pl.CostEstimate(
            flops=150000000, bytes_accessed=2000000, transcendentals=100000
        ),
        name="strip_pass",
    )(rows, strip, outer, inner, main, ocean, *weights, bias)


def north_early(lat, size):
    return (lat == size - 2) & (lat % 2 == 0)


def join(parts):
    return jnp.concatenate(parts, axis=-1) if len(parts) > 1 else parts[0]


def received(strip, near_ref, far_ref, near, lat):
    halves, wide = [], []
    for t in range(3):
        main, side = [], []
        for half in range(2):
            at = 2 * t + half
            x, corner = near_ref[at], near_ref[6]
            if far_ref is not None:
                x = jnp.where(near, x, far_ref[at])
                corner = jnp.where(near, corner, far_ref[6])
            y = beside(corner, 32 * half + 4 * t + 4 * (1 - strip), corner, 32 * half + 16 + 4 * t + 4 * (1 - strip))
            if strip == 0:
                x, y = jnp.where(lat == 0, 0.0, x), jnp.where(lat == 0, 0.0, y)
            main.append(x)
            side.append(y)
        halves.append(main)
        parts = [jnp.concatenate(main, axis=0), jnp.concatenate(side, axis=0)]
        wide.append(jnp.concatenate(parts, axis=1).astype(BF16))
    return halves, wide


def complete(strips, rows, rows_ref, mask_ref, side_ref, pre, weights, blocks, out_ref, sems):
    def late(weights, wide, width):
        blank = [jnp.zeros((16, width), BF16)] * 2
        operand = []
        for c in range(3):
            columns = []
            for strip in strips:
                x = [turn_wide(row, c)[:, 0:width] for row in wide[strip]]
                columns.append(x + blank if strip == 0 else blank + x)
            operand.extend(join(parts) for parts in zip(*columns))
        operand.append(jnp.zeros((16, width * len(strips)), BF16))
        return dot(weights[...], jnp.concatenate(operand, axis=0))

    def shares(pre_ref, width):
        return join([pre_ref[:, :, width * strip : width * strip + width] for strip in strips])

    total = late(weights[0], {strip: rows[strip][1] for strip in strips}, 256)

    col = lanes()
    ready = {}
    for strip in strips:
        source, target = blocks[strip]
        target[...] = source[...]
        for t in range(3):
            row = t if strip == 0 else ROWS - 3 + t
            near = {i: [rows_ref[i, half] for half in range(2)] for i in (row - 1, row, row + 1) if 0 <= i < ROWS}
            near[-1], near[ROWS] = rows[strip][0][2], rows[strip][0][0]
            q = near[row]
            side = [side_ref[3 * strip + t, half] for half in range(2)]
            e = [turn(jnp.where(col == 0, y, x), -1) for x, y in zip(q, side)]
            w = [turn(jnp.where(col == 127, y, x), 1) for x, y in zip(q, side)]
            new = tendency(q, near[row + 1], near[row - 1], e, w)
            ocean = 0.1 * mask_ref[row : row + 1, :].astype(F32)
            ready[strip, t] = (q[0] + ocean * new[0], q[1] + ocean * new[1], ocean)

    for layer_at, width in ((0, 256), (1, 128)):
        value = total.reshape(3, 16, 256 * len(strips)) + shares(pre[layer_at], 256)
        value = silu(value).astype(BF16)
        wide = {
            strip: [value[r, :, 256 * i : 256 * i + 256] for r in range(3)]
            for i, strip in enumerate(strips)
        }
        total = late(weights[layer_at + 1], wide, width)
    total = total.reshape(4, 8, 128 * len(strips))[0:3] + shares(pre[2], 128)

    stores = []
    for i, strip in enumerate(strips):
        ref, at, start = (blocks[strip][1], 0, 0) if strip == 0 else (blocks[strip][1], ROWS - 8, 5)
        flat = ref.reshape(128, 128)
        for t in range(3):
            first, second, ocean = ready[strip, t]
            new = (first + ocean * total[t, :, 128 * i : 128 * i + 128], second)
            row = start + t
            for half in range(2):
                flat[pl.ds(64 * half + row, 8, stride=8), :] = new[half]
        store = pltpu.make_async_copy(ref, out_ref.at[:, pl.ds(at, 8), :], sems.at[1 + strip])
        store.start()
        stores.append(store)
    return stores


def copy_middle(cells_ref, out_ref, sem):
    source = cells_ref.at[:, pl.ds(0, ROWS - 16), :]
    return pltpu.make_async_copy(source, out_ref.at[:, pl.ds(8, ROWS - 16), :], sem)


def border_kernel(size, last, *refs):
    rows_ref, mask_ref, first_ref, *refs = refs
    if last:
        second_ref, *refs = refs
    side_ref, *refs = refs
    pre, weights, refs = refs[0:3], refs[3:6], refs[6:]
    cells_ref, low_in_ref, high_in_ref, *refs = refs
    out_ref, low_ref, high_ref, sems = refs[1:] if last else refs
    lat = lax.axis_index("lat")
    even = lat % 2 == 0
    early = north_early(lat, size)
    blocks = ((low_in_ref, low_ref), (high_in_ref, high_ref))

    def run(strips, middle, rows):
        stores = []
        if middle:
            stores.append(copy_middle(cells_ref, out_ref, sems.at[0]))
            stores[0].start()
        stores += complete(
            strips, rows, rows_ref, mask_ref, side_ref, pre, weights, blocks, out_ref, sems
        )
        for store in stores:
            store.wait()

    if not last:

        @pl.when(early)
        def _():
            run((1,), True, {1: received(1, first_ref, None, even, lat)})

        return

    @pl.when(early)
    def _():
        run((0,), False, {0: received(0, second_ref, None, even, lat)})

    @pl.when(jnp.logical_not(early))
    def _():
        low = received(0, second_ref, first_ref, even, lat)
        run((0, 1), True, {0: low, 1: received(1, first_ref, second_ref, even, lat)})


def border_pass(size, rows, mask, messages, side, pre, late, cells, low, high, out=()):
    last = len(out) > 0
    operands = (rows, mask, *messages, side, *pre, *late, cells, low, high)
    return pl.pallas_call(
        functools.partial(border_kernel, size, last),
        out_shape=jax.ShapeDtypeStruct((16, ROWS, 128), F32),
        in_specs=[VMEM] * len(operands) + [HBM] * len(out),
        out_specs=HBM,
        input_output_aliases={len(operands): 0} if last else {},
        scratch_shapes=[
            pltpu.VMEM(low.shape, F32),
            pltpu.VMEM(high.shape, F32),
            pltpu.SemaphoreType.DMA((3,)),
        ],
        compiler_params=pltpu.CompilerParams(vmem_limit_bytes=LIMIT),
        cost_estimate=pl.CostEstimate(flops=60000000, bytes_accessed=1000000, transcendentals=60000),
        name="border_pass" if last else "north_strip",
    )(*operands, *out)


def shards(state, land_mask, kernel_one, bias_one, kernel_two, bias_two, kernel_three, bias_three):
    lon, lat = (lax.axis_size("lon"), lax.axis_size("lat"))
    biases = [x.reshape(1, x.shape[0]) for x in (bias_one, bias_two, bias_three)]
    rows, strip, outer, inner, *biases = prepare(state, biases)
    parameters = (kernel_one, kernel_two, kernel_three, *biases)

    inner = lax.ppermute(inner, "lon", [(i, i + 1 - 2 * (i % 2)) for i in range(lon)])
    outer = lax.ppermute(outer, "lon", [(i, (i + 1 if i % 2 else i - 1) % lon) for i in range(lon)])
    main, north, ocean, *weights, bias = main_pass(lat, rows, land_mask, parameters)
    weights, late = weights[0:3], weights[3:6]

    def pairs(parity):
        result = []
        for i in range(lon):
            for j in range(parity, lat - 1, 2):
                result += [(i * lat + j, i * lat + j + 1), (i * lat + j + 1, i * lat + j)]
            if parity == 1:
                result.append((i * lat, (i + 1 - 2 * (i % 2)) * lat))
            if (lat - 1) % 2 == parity:
                result.append((i * lat + lat - 1, (lon - 1 - i) * lat + lat - 1))
        return result

    first, second = corners(lat, rows, inner, outer, north)
    first = lax.ppermute(first, ("lon", "lat"), pairs(0))
    second = lax.ppermute(second, ("lon", "lat"), pairs(1))
    cells, low, high, side, *pre = strip_pass(
        rows, strip, inner, outer, main, ocean, weights, bias
    )
    held = (side, pre, late, cells, low, high)
    out = border_pass(lat, rows, land_mask, (first,), *held)
    return border_pass(lat, rows, land_mask, (first, second), *held, (out,))


def solution(mesh):
    return jax.shard_map(
        shards,
        mesh=mesh,
        in_specs=(P(None, "lat", "lon"), P("lat", "lon"), P(), P(), P(), P(), P(), P()),
        out_specs=P(None, "lat", "lon"),
        check_vma=False,
    )
```

```python
import functools

import jax
import jax.numpy as jnp
from jax import lax
from jax.experimental import pallas as pl
from jax.experimental.pallas import tpu as pltpu
from jax.sharding import PartitionSpec as P

F32 = jnp.float32
BF16 = jnp.bfloat16

ROWS = 64
PITCH = 72
BLOCK = 8
DEPTH = 512
SPAN = (BLOCK + 2) * 16
VMEM = pl.BlockSpec(memory_space=pltpu.VMEM)
HBM = pl.BlockSpec(memory_space=pltpu.HBM)
LIMIT = 40 * 2**20


def lanes():
    return lax.broadcasted_iota(jnp.int32, (8, 128), 1)


def turn(x, by):
    if isinstance(by, int):
        by = by % 128
        if by == 0:
            return x
    return pltpu.roll(x, by, x.ndim - 1)


def silu(v):
    half = 0.5 * v
    return half + half * jnp.tanh(half)


def dot(weights, x):
    return jnp.dot(weights, x, preferred_element_type=F32)


def even_place(axis):
    return lax.rem(lax.axis_index(axis), 2) == 0


def sides(inner, outer):
    even = even_place("lon")
    return (
        [jnp.where(even, inner[i], outer[i]) for i in range(4)],
        [jnp.where(even, outer[i], inner[i]) for i in range(4)],
    )


def tendency(q, north, south, east, west):
    sub = lax.broadcasted_iota(jnp.int32, (8, 128), 0)
    swapped = pltpu.roll(q[0], 4, 0)
    u = jnp.where(sub < 4, q[0], swapped)
    v = jnp.where(sub < 4, swapped, q[0])
    result = []
    for e, w, n, s, x in zip(east, west, north, south, q):
        total = -0.5 * (u * (e - w) + v * (n - s))
        result.append(total + 0.2 * (e + w + n + s - 4.0 * x))
    return result


def beside(e, e_at, w, w_at):
    return jnp.where(lanes() < 64, turn(e, -e_at), turn(w, 125 - w_at))


def turn_wide(x, c):
    return pltpu.roll(x, (1 - c) % 256, 1) if c != 1 else x


def spread(rows, width):
    blank = jnp.zeros((16, 2 * width), BF16)
    result = []
    for c in range(3):
        for row in rows:
            parts = [turn_wide(row[:, at : at + 256], c)[:, 0:width] for at in (0, 256)]
            result.append(jnp.concatenate(parts, axis=1))
        result.extend([blank] * ((BLOCK + 2 if c < 2 else BLOCK + 4) - len(rows)))
    return jnp.concatenate(result, axis=0)


def prepare_kernel(
    state_ref, b_one_ref, b_two_ref, b_three_ref,
    cells_ref, strip_ref, outer_ref, inner_ref, h_one_ref, h_two_ref, h_three_ref, sems,
):
    fetches = []
    for half in range(2):
        span = pl.ds(8 * half, 8)
        target = cells_ref.at[span, pl.ds(0, ROWS), :]
        fetches.append(pltpu.make_async_copy(state_ref.at[span], target, sems.at[half]))
    biases = ((b_one_ref, h_one_ref), (b_two_ref, h_two_ref), (b_three_ref, h_three_ref))
    for source, target in biases:
        fetches.append(pltpu.make_async_copy(source, target, sems.at[len(fetches)]))
    for fetch in fetches:
        fetch.start()

    flat = cells_ref.reshape(16 * PITCH, 128)
    group = lanes() // 16
    part = (lanes() % 16) // 4
    even = even_place("lon")
    shifts = [
        [jnp.where(even, (4 * s - a) % 128, (4 * s - b) % 128) for s in range(4)]
        for a, b in ((6, 3), (3, 6))
    ]
    for fetch in fetches[0:2]:
        fetch.wait()
    strip = [[jnp.zeros((8, 128), F32)] * 8 for half in range(2)]
    for b in range(8):
        for half in range(2):
            for r in range(8):
                x = flat[pl.ds(8 * PITCH * half + 8 * b + r, 8, stride=PITCH), :]
                strip[half][r] = jnp.where(group == b, turn(x, 6 + 16 * b), strip[half][r])
    for target, shift in zip((outer_ref, inner_ref), shifts):
        for q in range(2):
            for half in range(2):
                value = jnp.zeros((8, 128), F32)
                for s in range(4):
                    value = jnp.where(part == s, turn(strip[half][4 * q + s], shift[s]), value)
                target[2 * q + half] = value
    for half in range(2):
        for r in range(8):
            strip_ref[r, half] = strip[half][r]
    for fetch in fetches[2:]:
        fetch.wait()


def prepare(state, biases):
    block = jax.ShapeDtypeStruct
    arrays = [pltpu.with_memory_space_constraint(x, pltpu.HBM) for x in (state, *biases)]
    return pl.pallas_call(
        prepare_kernel,
        out_shape=[
            block((16, PITCH, 128), F32),
            block((8, 2, 8, 128), F32),
            block((4, 8, 128), F32),
            block((4, 8, 128), F32),
            *[block(x.shape, F32) for x in biases],
        ],
        in_specs=[HBM] * 4,
        out_specs=[VMEM] * 7,
        scratch_shapes=[pltpu.SemaphoreType.DMA((5,))],
        compiler_params=pltpu.CompilerParams(vmem_limit_bytes=LIMIT),
        cost_estimate=pl.CostEstimate(flops=400000, bytes_accessed=1200000, transcendentals=0),
        name="rows_edges",
    )(*arrays)


def corners_kernel(size, rows_ref, outer_ref, inner_ref, north_ref, first_ref, second_ref):
    lat = lax.axis_index("lat")
    even = lax.rem(lat, 2) == 0
    for t in range(3):
        for half in range(2):
            at = 2 * t + half
            low = rows_ref[t, half]
            first_ref[at] = jnp.where(even, north_ref[at], low)
            second_ref[at] = jnp.where(even, low, north_ref[at])
    top = lat == size - 1
    col = lanes()
    part = col // 16
    straight = even_place("lon")
    mirrored = straight != top
    index = jnp.where(top, 112 + 4 * (3 - col // 4 % 4) + 2 - col % 4, 112 + col % 16)
    low = high = jnp.zeros((8, 128), F32)
    for i in range(4):
        half = i // 2
        pair = (inner_ref, outer_ref) if i % 2 == 0 else (outer_ref, inner_ref)
        x = jnp.where(straight, pair[0][half], pair[1][half])
        low = jnp.where(part == i, turn(x, 16 * i), low)
        x = jnp.where(mirrored, pair[0][2 + half], pair[1][2 + half])
        high = jnp.where(part == i, jnp.take_along_axis(x, index, axis=1), high)
    high = jnp.where(top & (col < 32), -high, high)
    first_ref[6] = jnp.where(even, high, low)
    second_ref[6] = jnp.where(even, low, high)


def corners(size, rows, inner, outer, north):
    return pl.pallas_call(
        functools.partial(corners_kernel, size),
        out_shape=[jax.ShapeDtypeStruct((7, 8, 128), F32)] * 2,
        in_specs=[VMEM] * 4,
        out_specs=[VMEM] * 2,
        compiler_params=pltpu.CompilerParams(vmem_limit_bytes=LIMIT),
        cost_estimate=pl.CostEstimate(flops=1000, bytes_accessed=100000, transcendentals=0),
        name="add_corners",
    )(rows, outer, inner, north)


def band(kernel_ref, wide_ref, target_ref):
    n = kernel_ref.shape[2]
    wide_ref[...] = jnp.zeros_like(wide_ref)
    tiles = [None] * (DEPTH // 128)
    for c in range(3):
        for a in range(3):
            wide_ref[3 * c + a, :, 0:16] = kernel_ref[a, c].astype(wide_ref.dtype)
            tile, off = divmod(SPAN * c + 16 * a, 128)
            x = turn(wide_ref[3 * c + a], off)
            tiles[tile] = x if tiles[tile] is None else tiles[tile] + x
    blank = jnp.zeros((n, 128), wide_ref.dtype)
    first = jnp.concatenate([blank if x is None else x for x in tiles], axis=1)
    rows = [first] + [pltpu.roll(first, 16 * r, 1) for r in range(1, BLOCK)]
    for r in range(0, BLOCK, 16 // n):
        target_ref[n * r : n * r + 16, :] = jnp.concatenate(rows[r : r + 16 // n], axis=0).astype(BF16)


def band_compact(wide_ref, target_ref, slots, outs):
    n = wide_ref.shape[1]
    tiles = [jnp.zeros((n, 128), wide_ref.dtype)] * (target_ref.shape[1] // 128)
    for c in range(3):
        for a in range(3):
            tile, off = divmod(16 * slots * c + 16 * a, 128)
            tiles[tile] = tiles[tile] + turn(wide_ref[3 * c + a], off)
    first = jnp.concatenate(tiles, axis=1)
    rows = [pltpu.roll(first, 16 * r, 1) if r else first for r in range(outs)]
    rows = rows + [jnp.zeros_like(first)] * (target_ref.shape[0] // n - outs)
    for r in range(0, len(rows), 16 // n):
        target_ref[n * r : n * r + 16, :] = jnp.concatenate(rows[r : r + 16 // n], axis=0).astype(BF16)


def main_kernel(
    size, cells_ref, mask_ref, k_one_ref, k_two_ref, k_three_ref, b_one_ref, b_two_ref, b_three_ref,
    rows_ref, out_ref, north_ref, ocean_ref, one_ref, two_ref, three_ref,
    late_one_ref, late_two_ref, late_three_ref, bias_ref,
    wide_ref, narrow_ref, first_ref, second_ref, third_ref,
):
    flat = cells_ref.reshape(16 * PITCH, 128)

    def load(row, half):
        return flat[pl.ds(8 * PITCH * half + row, 8, stride=PITCH), :]

    top = lax.axis_index("lat") == size - 1
    col = lanes()
    for t in range(3):
        for half in range(2):
            folded = jnp.take_along_axis(load(ROWS - 1 - t, half), 127 - col, axis=1)
            folded = -folded if half == 0 else folded
            north_ref[2 * t + half] = jnp.where(top, folded, load(ROWS - 3 + t, half))
    ocean = jnp.zeros((8, 128), F32)
    for b in range(8):
        x = 0.1 * mask_ref[8 * b : 8 * b + 8, :].astype(F32)
        ocean = jnp.where(col // 16 == b, turn(x, 6 + 16 * b), ocean)
    ocean_ref[...] = ocean

    biases = []
    at = 0
    for ref in (b_one_ref, b_two_ref, b_three_ref):
        n = ref.shape[1]
        same = lax.broadcasted_iota(jnp.int32, (n, n), 0) == lax.broadcasted_iota(jnp.int32, (n, n), 1)
        column = jnp.sum(jnp.where(same, ref[...], 0.0), axis=1, keepdims=True)
        biases.append(jnp.broadcast_to(column, (n, 128)))
        bias_ref[at : at + n, :] = biases[-1]
        at += n
    band(k_one_ref, wide_ref.at[0], one_ref)
    band(k_two_ref, wide_ref.at[1], two_ref)
    band(k_three_ref, narrow_ref, three_ref)
    band_compact(wide_ref.at[0], late_one_ref, 5, 3)
    band_compact(wide_ref.at[1], late_two_ref, 5, 3)
    band_compact(narrow_ref, late_three_ref, 5, 3)
    for ref in (first_ref, second_ref, third_ref):
        for c in range(3):
            for row in (0, ROWS + 1, ROWS + 2, ROWS + 3):
                ref[c, row] = jnp.zeros((16, 128), BF16)

    for row in range(ROWS):
        x = [load(row, half) for half in range(2)]
        for half in range(2):
            rows_ref[row, half] = x[half]
        x = jnp.concatenate(x, axis=0).astype(BF16)
        for c in range(3):
            first_ref[c, row + 1] = turn(x, 1 - c)

    def layer(source, weights, at):
        parts = []
        for start in (at, at + ROWS // 2):
            for c in range(3):
                count = BLOCK + 2 if c < 2 else BLOCK + 4
                parts.append(source[c, start : start + count].reshape(16 * count, 128))
        x = jnp.concatenate(
            [jnp.concatenate(parts[0:3], axis=0), jnp.concatenate(parts[3:6], axis=0)], axis=1
        )
        return dot(weights[...], x)

    for source, weights, bias, target in (
        (first_ref, one_ref, biases[0], second_ref),
        (second_ref, two_ref, biases[1], third_ref),
    ):
        bias = jnp.concatenate([bias, bias], axis=1)
        ahead = layer(source, weights, 0)
        for at in range(0, ROWS // 2, BLOCK):
            total = ahead.reshape(BLOCK, 16, 256)
            if at + BLOCK < ROWS // 2:
                ahead = layer(source, weights, at + BLOCK)
            value = silu(total + bias[None]).astype(BF16).reshape(16 * BLOCK, 256)
            for part in range(2):
                start = at + ROWS // 2 * part + 1
                x = value[:, 128 * part : 128 * part + 128]
                for c in range(3):
                    target[c, start : start + BLOCK] = turn(x, 1 - c).reshape(BLOCK, 16, 128)

    bias = jnp.concatenate([biases[2], biases[2]], axis=1)
    ahead = layer(third_ref, three_ref, 0)
    for at in range(0, ROWS // 2, BLOCK):
        forcing = ahead.reshape(BLOCK, 8, 256) + bias[None]
        if at + BLOCK < ROWS // 2:
            ahead = layer(third_ref, three_ref, at + BLOCK)
        for part in range(2):
            for r in range(BLOCK):
                row = at + ROWS // 2 * part + r
                near = [min(max(row + d, 0), ROWS - 1) for d in (0, 1, -1)]
                q, north, south = [[rows_ref[i, half] for half in range(2)] for i in near]
                east = [turn(x, -1) for x in q]
                west = [turn(x, 1) for x in q]
                new = tendency(q, north, south, east, west)
                new[0] = new[0] + forcing[r, :, 128 * part : 128 * part + 128]
                ocean = 0.1 * mask_ref[row : row + 1, :].astype(F32)
                for half in range(2):
                    out_ref[row, half] = q[half] + ocean * new[half]


def main_pass(size, cells, mask, parameters):
    taps = pltpu.VMEM((3, ROWS + 4, 16, 128), BF16)
    block = jax.ShapeDtypeStruct
    return pl.pallas_call(
        functools.partial(main_kernel, size),
        out_shape=[
            *[block((ROWS, 2, 8, 128), F32)] * 2,
            block((6, 8, 128), F32),
            block((8, 128), F32),
            *[block((n, DEPTH), BF16) for n in (128, 128, 64)],
            *[block(shape, BF16) for shape in ((48, 256), (48, 256), (32, 256))],
            block((40, 128), F32),
        ],
        in_specs=[VMEM] * 8,
        out_specs=[VMEM] * 11,
        scratch_shapes=[
            pltpu.VMEM((2, 9, 16, 128), BF16),
            pltpu.VMEM((9, 8, 128), F32),
            *[taps] * 3,
        ],
        compiler_params=pltpu.CompilerParams(vmem_limit_bytes=LIMIT),
        cost_estimate=pl.CostEstimate(
            flops=150000000, bytes_accessed=1500000, transcendentals=300000
        ),
        name="main_pass",
    )(cells, mask, *parameters)


def taps(rows, count):
    blank = jnp.zeros_like(rows[0])
    result = []
    for c in range(3):
        for row in rows:
            width = row.shape[1] // 128
            parts = [turn(row[:, 128 * i : 128 * i + 128], 1 - c) for i in range(width)]
            result.append(jnp.concatenate(parts, axis=1) if width > 1 else parts[0])
        result.extend([blank] * ((BLOCK + 2 if c < 2 else BLOCK + 4) - len(rows)))
    return jnp.concatenate(result, axis=0)


def strip_kernel(
    rows_ref, strip_ref, outer_ref, inner_ref, main_ref, ocean_ref, one_ref, two_ref, three_ref,
    bias_ref, cells_ref, low_ref, high_ref, side_ref, pre_one_ref, pre_two_ref, pre_three_ref,
):
    east, west = sides(inner_ref, outer_ref)
    col = lanes()
    at = col % 16
    cells = []
    for r in range(8):
        pair = [[], []]
        for half in range(2):
            block = 2 * (r // 4) + half
            own = strip_ref[r, half]
            pair[0].append(jnp.where(at < 6, own, turn(east[block], 6 - 4 * (r % 4))))
            pair[1].append(jnp.where(at < 3, turn(west[block], -4 * (r % 4)), turn(own, -3)))
        cells.append(pair)

    def own(row):
        start = 16 * (row // 8) + 4 * (row % 4)
        block = 2 * (row % 8 // 4)
        return [beside(east[block + h], start, west[block + h], start) for h in range(2)]

    low, high = [], []
    for row in list(range(6)) + list(range(ROWS - 6, ROWS)):
        side = own(row)
        slot = row if row < 3 else row - ROWS + 6
        if row < 3 or row >= ROWS - 3:
            for half in range(2):
                side_ref[slot, half] = side[half]
        parts = [
            jnp.concatenate([rows_ref[row, 0], rows_ref[row, 1]], axis=0),
            jnp.concatenate(side, axis=0),
        ]
        (low if row < 6 else high).append(jnp.concatenate(parts, axis=1).astype(BF16))
    def moved(pair, by):
        return [[turn(x, by) for x in part] for part in pair]

    cells = [moved(x, 16) for x in cells[5:8]] + cells + [moved(x, -16) for x in cells[0:3]]
    rows = []
    for pair in cells:
        parts = [jnp.concatenate(part, axis=0) for part in pair]
        rows.append(jnp.concatenate(parts, axis=1).astype(BF16))

    blank = jnp.zeros((16, 256), BF16)
    for weights, count, bias_at, pre_ref, width in (
        (one_ref, 7, 0, pre_one_ref, 256),
        (two_ref, 5, 16, pre_two_ref, 256),
        (three_ref, 3, 32, pre_three_ref, 128),
    ):
        n = weights.shape[0] // BLOCK
        more = len(rows) - 2 - BLOCK
        first = dot(weights[...], taps(rows[0:10], 256)).reshape(BLOCK, n, 256)
        if more > 0:
            second = dot(weights[0 : n * more, :], taps(rows[BLOCK:], 256)).reshape(more, n, 256)
        pairs = zip([blank] * 3 + low, high + [blank] * 3)
        operand = spread([jnp.concatenate(pair, axis=1) for pair in pairs], width)
        total = dot(weights[0 : (count + count % 2) * n, :], operand).reshape(-1, n, 2 * width)
        bias = bias_ref[bias_at : bias_at + n, :]
        first = first + jnp.concatenate([bias] * 2, axis=1)[None]
        if more > 0:
            second = second + jnp.concatenate([bias] * 2, axis=1)[None]
            rows = [silu(first[i]).astype(BF16) for i in range(BLOCK)]
            rows = rows + [silu(second[i]).astype(BF16) for i in range(more)]
        total = total + jnp.concatenate([bias] * (width // 64), axis=1)[None]
        for r in range(3):
            parts = [total[r, :, 0:width], total[count - 3 + r, :, width : 2 * width]]
            pre_ref[r] = jnp.concatenate(parts, axis=1)
        low = [silu(total[r, :, 0:width]).astype(BF16) for r in range(3, count)]
        high = [silu(total[r, :, width : 2 * width]).astype(BF16) for r in range(count - 3)]
    forcing = first

    both = []
    for r in range(8):
        new = []
        for part in range(2):
            q, north, south = [cells[i][part] for i in (r + 3, r + 4, r + 2)]
            value = tendency(
                q, north, south, [turn(x, -1) for x in q], [turn(x, 1) for x in q]
            )
            value[0] = value[0] + forcing[r, :, 128 * part : 128 * part + 128]
            new.append(value)
        ocean = ocean_ref[r : r + 1, :]
        value = [jnp.where(at < 6, new[0][half], turn(new[1][half], 3)) for half in range(2)]
        both.append([strip_ref[r, half] + ocean * value[half] for half in range(2)])

    edge = (col < 3) | (col >= 125)
    for b in range(8):
        ref, start = (low_ref, 0) if b == 0 else (high_ref, 0) if b == 7 else (cells_ref, 8 * b - 8)
        pitch = ref.shape[1]
        flat = ref.reshape(16 * pitch, 128)
        for r in range(8):
            for half in range(2):
                value = turn(both[r][half], -(16 * b + 6))
                value = jnp.where(edge, value, main_ref[8 * b + r, half])
                flat[pl.ds(8 * pitch * half + start + r, 8, stride=pitch), :] = value


def strip_pass(rows, strip, inner, outer, main, ocean, weights, bias):
    block = jax.ShapeDtypeStruct
    return pl.pallas_call(
        strip_kernel,
        out_shape=[
            block((16, ROWS - 8, 128), F32),
            *[block((16, 8, 128), F32)] * 2,
            block((6, 2, 8, 128), F32),
            *[block(shape, F32) for shape in ((3, 16, 512), (3, 16, 512), (3, 8, 256))],
        ],
        in_specs=[VMEM] * 10,
        out_specs=[VMEM] * 7,
        compiler_params=pltpu.CompilerParams(vmem_limit_bytes=LIMIT),
        cost_estimate=pl.CostEstimate(
            flops=150000000, bytes_accessed=2000000, transcendentals=100000
        ),
        name="strip_pass",
    )(rows, strip, outer, inner, main, ocean, *weights, bias)


def north_early(lat, size):
    return (lat == size - 2) & (lat % 2 == 0)


def join(parts):
    return jnp.concatenate(parts, axis=-1) if len(parts) > 1 else parts[0]


def received(strip, near_ref, far_ref, near, lat):
    halves, wide = [], []
    for t in range(3):
        main, side = [], []
        for half in range(2):
            at = 2 * t + half
            x, corner = near_ref[at], near_ref[6]
            if far_ref is not None:
                x = jnp.where(near, x, far_ref[at])
                corner = jnp.where(near, corner, far_ref[6])
            y = beside(corner, 32 * half + 4 * t + 4 * (1 - strip), corner, 32 * half + 16 + 4 * t + 4 * (1 - strip))
            if strip == 0:
                x, y = jnp.where(lat == 0, 0.0, x), jnp.where(lat == 0, 0.0, y)
            main.append(x)
            side.append(y)
        halves.append(main)
        parts = [jnp.concatenate(main, axis=0), jnp.concatenate(side, axis=0)]
        wide.append(jnp.concatenate(parts, axis=1).astype(BF16))
    return halves, wide


def complete(strips, rows, rows_ref, mask_ref, side_ref, pre, weights, blocks, out_ref, sems):
    def late(weights, wide, width):
        blank = [jnp.zeros((16, width), BF16)] * 2
        operand = []
        for c in range(3):
            columns = []
            for strip in strips:
                x = [turn_wide(row, c)[:, 0:width] for row in wide[strip]]
                columns.append(x + blank if strip == 0 else blank + x)
            operand.extend(join(parts) for parts in zip(*columns))
        operand.append(jnp.zeros((16, width * len(strips)), BF16))
        return dot(weights[...], jnp.concatenate(operand, axis=0))

    def shares(pre_ref, width):
        return join([pre_ref[:, :, width * strip : width * strip + width] for strip in strips])

    total = late(weights[0], {strip: rows[strip][1] for strip in strips}, 256)

    col = lanes()
    ready = {}
    for strip in strips:
        source, target = blocks[strip]
        target[...] = source[...]
        for t in range(3):
            row = t if strip == 0 else ROWS - 3 + t
            near = {i: [rows_ref[i, half] for half in range(2)] for i in (row - 1, row, row + 1) if 0 <= i < ROWS}
            near[-1], near[ROWS] = rows[strip][0][2], rows[strip][0][0]
            q = near[row]
            side = [side_ref[3 * strip + t, half] for half in range(2)]
            e = [turn(jnp.where(col == 0, y, x), -1) for x, y in zip(q, side)]
            w = [turn(jnp.where(col == 127, y, x), 1) for x, y in zip(q, side)]
            new = tendency(q, near[row + 1], near[row - 1], e, w)
            ocean = 0.1 * mask_ref[row : row + 1, :].astype(F32)
            ready[strip, t] = (q[0] + ocean * new[0], q[1] + ocean * new[1], ocean)

    for layer_at, width in ((0, 256), (1, 128)):
        value = total.reshape(3, 16, 256 * len(strips)) + shares(pre[layer_at], 256)
        value = silu(value).astype(BF16)
        wide = {
            strip: [value[r, :, 256 * i : 256 * i + 256] for r in range(3)]
            for i, strip in enumerate(strips)
        }
        total = late(weights[layer_at + 1], wide, width)
    total = total.reshape(4, 8, 128 * len(strips))[0:3] + shares(pre[2], 128)

    stores = []
    for i, strip in enumerate(strips):
        ref, at, start = (blocks[strip][1], 0, 0) if strip == 0 else (blocks[strip][1], ROWS - 8, 5)
        flat = ref.reshape(128, 128)
        for t in range(3):
            first, second, ocean = ready[strip, t]
            new = (first + ocean * total[t, :, 128 * i : 128 * i + 128], second)
            row = start + t
            for half in range(2):
                flat[pl.ds(64 * half + row, 8, stride=8), :] = new[half]
        store = pltpu.make_async_copy(ref, out_ref.at[:, pl.ds(at, 8), :], sems.at[1 + strip])
        store.start()
        stores.append(store)
    return stores


def copy_middle(cells_ref, out_ref, sem):
    source = cells_ref.at[:, pl.ds(0, ROWS - 16), :]
    return pltpu.make_async_copy(source, out_ref.at[:, pl.ds(8, ROWS - 16), :], sem)


def border_kernel(size, last, *refs):
    rows_ref, mask_ref, first_ref, *refs = refs
    if last:
        second_ref, *refs = refs
    side_ref, *refs = refs
    pre, weights, refs = refs[0:3], refs[3:6], refs[6:]
    cells_ref, low_in_ref, high_in_ref, *refs = refs
    out_ref, low_ref, high_ref, sems = refs[1:] if last else refs
    lat = lax.axis_index("lat")
    even = lat % 2 == 0
    early = north_early(lat, size)
    blocks = ((low_in_ref, low_ref), (high_in_ref, high_ref))

    def run(strips, middle, rows):
        stores = []
        if middle:
            stores.append(copy_middle(cells_ref, out_ref, sems.at[0]))
            stores[0].start()
        stores += complete(
            strips, rows, rows_ref, mask_ref, side_ref, pre, weights, blocks, out_ref, sems
        )
        for store in stores:
            store.wait()

    if not last:

        @pl.when(early)
        def _():
            run((1,), True, {1: received(1, first_ref, None, even, lat)})

        return

    @pl.when(early)
    def _():
        run((0,), False, {0: received(0, second_ref, None, even, lat)})

    @pl.when(jnp.logical_not(early))
    def _():
        low = received(0, second_ref, first_ref, even, lat)
        run((0, 1), True, {0: low, 1: received(1, first_ref, second_ref, even, lat)})


def border_pass(size, rows, mask, messages, side, pre, late, cells, low, high, out=()):
    last = len(out) > 0
    operands = (rows, mask, *messages, side, *pre, *late, cells, low, high)
    return pl.pallas_call(
        functools.partial(border_kernel, size, last),
        out_shape=jax.ShapeDtypeStruct((16, ROWS, 128), F32),
        in_specs=[VMEM] * len(operands) + [HBM] * len(out),
        out_specs=HBM,
        input_output_aliases={len(operands): 0} if last else {},
        scratch_shapes=[
            pltpu.VMEM(low.shape, F32),
            pltpu.VMEM(high.shape, F32),
            pltpu.SemaphoreType.DMA((3,)),
        ],
        compiler_params=pltpu.CompilerParams(vmem_limit_bytes=LIMIT),
        cost_estimate=pl.CostEstimate(flops=60000000, bytes_accessed=1000000, transcendentals=60000),
        name="border_pass" if last else "north_strip",
    )(*operands, *out)


def shards(state, land_mask, kernel_one, bias_one, kernel_two, bias_two, kernel_three, bias_three):
    lon, lat = (lax.axis_size("lon"), lax.axis_size("lat"))
    biases = [x.reshape(1, x.shape[0]) for x in (bias_one, bias_two, bias_three)]
    cells, strip, outer, inner, *biases = prepare(state, biases)
    parameters = (kernel_one, kernel_two, kernel_three, *biases)

    inner = lax.ppermute(inner, "lon", [(i, i + 1 - 2 * (i % 2)) for i in range(lon)])
    outer = lax.ppermute(outer, "lon", [(i, (i + 1 if i % 2 else i - 1) % lon) for i in range(lon)])
    rows, main, north, ocean, *weights, bias = main_pass(lat, cells, land_mask, parameters)
    weights, late = weights[0:3], weights[3:6]

    def pairs(parity):
        result = []
        for i in range(lon):
            for j in range(parity, lat - 1, 2):
                result += [(i * lat + j, i * lat + j + 1), (i * lat + j + 1, i * lat + j)]
            if parity == 1:
                result.append((i * lat, (i + 1 - 2 * (i % 2)) * lat))
            if (lat - 1) % 2 == parity:
                result.append((i * lat + lat - 1, (lon - 1 - i) * lat + lat - 1))
        return result

    first, second = corners(lat, rows, inner, outer, north)
    first = lax.ppermute(first, ("lon", "lat"), pairs(0))
    second = lax.ppermute(second, ("lon", "lat"), pairs(1))
    cells, low, high, side, *pre = strip_pass(
        rows, strip, inner, outer, main, ocean, weights, bias
    )
    held = (side, pre, late, cells, low, high)
    out = border_pass(lat, rows, land_mask, (first,), *held)
    return border_pass(lat, rows, land_mask, (first, second), *held, (out,))


def solution(mesh):
    return jax.shard_map(
        shards,
        mesh=mesh,
        in_specs=(P(None, "lat", "lon"), P("lat", "lon"), P(), P(), P(), P(), P(), P()),
        out_specs=P(None, "lat", "lon"),
        check_vma=False,
    )
```

```python
import functools

import jax
import jax.numpy as jnp
from jax import lax
from jax.experimental import pallas as pl
from jax.experimental.pallas import tpu as pltpu
from jax.sharding import PartitionSpec as P

F32 = jnp.float32
BF16 = jnp.bfloat16

ROWS = 64
PITCH = 72
BLOCK = 8
DEPTH = 512
SPAN = (BLOCK + 2) * 16
VMEM = pl.BlockSpec(memory_space=pltpu.VMEM)
HBM = pl.BlockSpec(memory_space=pltpu.HBM)
LIMIT = 40 * 2**20


def lanes():
    return lax.broadcasted_iota(jnp.int32, (8, 128), 1)


def turn(x, by):
    if isinstance(by, int):
        by = by % 128
        if by == 0:
            return x
    return pltpu.roll(x, by, x.ndim - 1)


def silu(v):
    half = 0.5 * v
    return half + half * jnp.tanh(half)


def dot(weights, x):
    return jnp.dot(weights, x, preferred_element_type=F32)


def even_place(axis):
    return lax.rem(lax.axis_index(axis), 2) == 0


def sides(inner, outer):
    even = even_place("lon")
    return (
        [jnp.where(even, inner[i], outer[i]) for i in range(4)],
        [jnp.where(even, outer[i], inner[i]) for i in range(4)],
    )


def tendency(q, north, south, east, west):
    sub = lax.broadcasted_iota(jnp.int32, (8, 128), 0)
    swapped = pltpu.roll(q[0], 4, 0)
    u = jnp.where(sub < 4, q[0], swapped)
    v = jnp.where(sub < 4, swapped, q[0])
    result = []
    for e, w, n, s, x in zip(east, west, north, south, q):
        total = -0.5 * (u * (e - w) + v * (n - s))
        result.append(total + 0.2 * (e + w + n + s - 4.0 * x))
    return result


def beside(e, e_at, w, w_at):
    return jnp.where(lanes() < 64, turn(e, -e_at), turn(w, 125 - w_at))


def turn_wide(x, c):
    return pltpu.roll(x, (1 - c) % 256, 1) if c != 1 else x


def spread(rows, width):
    blank = jnp.zeros((16, 2 * width), BF16)
    result = []
    for c in range(3):
        for row in rows:
            parts = [turn_wide(row[:, at : at + 256], c)[:, 0:width] for at in (0, 256)]
            result.append(jnp.concatenate(parts, axis=1))
        result.extend([blank] * ((BLOCK + 2 if c < 2 else BLOCK + 4) - len(rows)))
    return jnp.concatenate(result, axis=0)


def prepare_kernel(
    state_ref, b_one_ref, b_two_ref, b_three_ref,
    cells_ref, strip_ref, outer_ref, inner_ref, h_one_ref, h_two_ref, h_three_ref, sems,
):
    fetches = []
    for half in range(2):
        span = pl.ds(8 * half, 8)
        target = cells_ref.at[span, pl.ds(0, ROWS), :]
        fetches.append(pltpu.make_async_copy(state_ref.at[span], target, sems.at[half]))
    biases = ((b_one_ref, h_one_ref), (b_two_ref, h_two_ref), (b_three_ref, h_three_ref))
    for source, target in biases:
        fetches.append(pltpu.make_async_copy(source, target, sems.at[len(fetches)]))
    for fetch in fetches:
        fetch.start()

    flat = cells_ref.reshape(16 * PITCH, 128)
    group = lanes() // 16
    part = (lanes() % 16) // 4
    even = even_place("lon")
    shifts = [
        [jnp.where(even, (4 * s - a) % 128, (4 * s - b) % 128) for s in range(4)]
        for a, b in ((6, 3), (3, 6))
    ]
    for fetch in fetches[0:2]:
        fetch.wait()
    def make(half, q):
        rows = []
        for r in range(4 * q, 4 * q + 4):
            value = jnp.zeros((8, 128), F32)
            for b in range(8):
                x = flat[pl.ds(8 * PITCH * half + 8 * b + r, 8, stride=PITCH), :]
                value = jnp.where(group == b, turn(x, 6 + 16 * b), value)
            rows.append(value)
        return rows

    order = [(half, q) for half in range(2) for q in range(2)]
    ahead = make(*order[0])
    for i, (half, q) in enumerate(order):
        strip = ahead
        if i + 1 < len(order):
            ahead = make(*order[i + 1])
        for target, shift in zip((outer_ref, inner_ref), shifts):
            value = jnp.zeros((8, 128), F32)
            for s in range(4):
                value = jnp.where(part == s, turn(strip[s], shift[s]), value)
            target[2 * q + half] = value
        for s in range(4):
            strip_ref[4 * q + s, half] = strip[s]
    for fetch in fetches[2:]:
        fetch.wait()


def prepare(state, biases):
    block = jax.ShapeDtypeStruct
    arrays = [pltpu.with_memory_space_constraint(x, pltpu.HBM) for x in (state, *biases)]
    return pl.pallas_call(
        prepare_kernel,
        out_shape=[
            block((16, PITCH, 128), F32),
            block((8, 2, 8, 128), F32),
            block((4, 8, 128), F32),
            block((4, 8, 128), F32),
            *[block(x.shape, F32) for x in biases],
        ],
        in_specs=[HBM] * 4,
        out_specs=[VMEM] * 7,
        scratch_shapes=[pltpu.SemaphoreType.DMA((5,))],
        compiler_params=pltpu.CompilerParams(vmem_limit_bytes=LIMIT),
        cost_estimate=pl.CostEstimate(flops=400000, bytes_accessed=1200000, transcendentals=0),
        name="rows_edges",
    )(*arrays)


def corners_kernel(size, rows_ref, outer_ref, inner_ref, north_ref, first_ref, second_ref):
    lat = lax.axis_index("lat")
    even = lax.rem(lat, 2) == 0
    for t in range(3):
        for half in range(2):
            at = 2 * t + half
            low = rows_ref[t, half]
            first_ref[at] = jnp.where(even, north_ref[at], low)
            second_ref[at] = jnp.where(even, low, north_ref[at])
    top = lat == size - 1
    col = lanes()
    part = col // 16
    straight = even_place("lon")
    mirrored = straight != top
    index = jnp.where(top, 112 + 4 * (3 - col // 4 % 4) + 2 - col % 4, 112 + col % 16)
    low = high = jnp.zeros((8, 128), F32)
    for i in range(4):
        half = i // 2
        pair = (inner_ref, outer_ref) if i % 2 == 0 else (outer_ref, inner_ref)
        x = jnp.where(straight, pair[0][half], pair[1][half])
        low = jnp.where(part == i, turn(x, 16 * i), low)
        x = jnp.where(mirrored, pair[0][2 + half], pair[1][2 + half])
        high = jnp.where(part == i, jnp.take_along_axis(x, index, axis=1), high)
    high = jnp.where(top & (col < 32), -high, high)
    first_ref[6] = jnp.where(even, high, low)
    second_ref[6] = jnp.where(even, low, high)


def corners(size, rows, inner, outer, north):
    return pl.pallas_call(
        functools.partial(corners_kernel, size),
        out_shape=[jax.ShapeDtypeStruct((7, 8, 128), F32)] * 2,
        in_specs=[VMEM] * 4,
        out_specs=[VMEM] * 2,
        compiler_params=pltpu.CompilerParams(vmem_limit_bytes=LIMIT),
        cost_estimate=pl.CostEstimate(flops=1000, bytes_accessed=100000, transcendentals=0),
        name="add_corners",
    )(rows, outer, inner, north)


def band(kernel_ref, wide_ref, target_ref):
    n = kernel_ref.shape[2]
    wide_ref[...] = jnp.zeros_like(wide_ref)
    tiles = [None] * (DEPTH // 128)
    for c in range(3):
        for a in range(3):
            wide_ref[3 * c + a, :, 0:16] = kernel_ref[a, c].astype(wide_ref.dtype)
            tile, off = divmod(SPAN * c + 16 * a, 128)
            x = turn(wide_ref[3 * c + a], off)
            tiles[tile] = x if tiles[tile] is None else tiles[tile] + x
    blank = jnp.zeros((n, 128), wide_ref.dtype)
    first = jnp.concatenate([blank if x is None else x for x in tiles], axis=1)
    rows = [first] + [pltpu.roll(first, 16 * r, 1) for r in range(1, BLOCK)]
    for r in range(0, BLOCK, 16 // n):
        target_ref[n * r : n * r + 16, :] = jnp.concatenate(rows[r : r + 16 // n], axis=0).astype(BF16)


def band_compact(wide_ref, target_ref, slots, outs):
    n = wide_ref.shape[1]
    tiles = [jnp.zeros((n, 128), wide_ref.dtype)] * (target_ref.shape[1] // 128)
    for c in range(3):
        for a in range(3):
            tile, off = divmod(16 * slots * c + 16 * a, 128)
            tiles[tile] = tiles[tile] + turn(wide_ref[3 * c + a], off)
    first = jnp.concatenate(tiles, axis=1)
    rows = [pltpu.roll(first, 16 * r, 1) if r else first for r in range(outs)]
    rows = rows + [jnp.zeros_like(first)] * (target_ref.shape[0] // n - outs)
    for r in range(0, len(rows), 16 // n):
        target_ref[n * r : n * r + 16, :] = jnp.concatenate(rows[r : r + 16 // n], axis=0).astype(BF16)


def main_kernel(
    size, cells_ref, mask_ref, k_one_ref, k_two_ref, k_three_ref, b_one_ref, b_two_ref, b_three_ref,
    rows_ref, out_ref, north_ref, ocean_ref, one_ref, two_ref, three_ref,
    late_one_ref, late_two_ref, late_three_ref, bias_ref,
    wide_ref, narrow_ref, first_ref, second_ref, third_ref,
):
    flat = cells_ref.reshape(16 * PITCH, 128)

    def load(row, half):
        return flat[pl.ds(8 * PITCH * half + row, 8, stride=PITCH), :]

    top = lax.axis_index("lat") == size - 1
    col = lanes()
    for t in range(3):
        for half in range(2):
            folded = jnp.take_along_axis(load(ROWS - 1 - t, half), 127 - col, axis=1)
            folded = -folded if half == 0 else folded
            north_ref[2 * t + half] = jnp.where(top, folded, load(ROWS - 3 + t, half))
    ocean = jnp.zeros((8, 128), F32)
    for b in range(8):
        x = 0.1 * mask_ref[8 * b : 8 * b + 8, :].astype(F32)
        ocean = jnp.where(col // 16 == b, turn(x, 6 + 16 * b), ocean)
    ocean_ref[...] = ocean

    biases = []
    at = 0
    for ref in (b_one_ref, b_two_ref, b_three_ref):
        n = ref.shape[1]
        same = lax.broadcasted_iota(jnp.int32, (n, n), 0) == lax.broadcasted_iota(jnp.int32, (n, n), 1)
        column = jnp.sum(jnp.where(same, ref[...], 0.0), axis=1, keepdims=True)
        biases.append(jnp.broadcast_to(column, (n, 128)))
        bias_ref[at : at + n, :] = biases[-1]
        at += n
    band(k_one_ref, wide_ref.at[0], one_ref)
    band(k_two_ref, wide_ref.at[1], two_ref)
    band(k_three_ref, narrow_ref, three_ref)
    band_compact(wide_ref.at[0], late_one_ref, 5, 3)
    band_compact(wide_ref.at[1], late_two_ref, 5, 3)
    band_compact(narrow_ref, late_three_ref, 5, 3)
    for ref in (first_ref, second_ref, third_ref):
        for c in range(3):
            for row in (0, ROWS + 1, ROWS + 2, ROWS + 3):
                ref[c, row] = jnp.zeros((16, 128), BF16)

    for row in range(ROWS):
        x = [load(row, half) for half in range(2)]
        for half in range(2):
            rows_ref[row, half] = x[half]
        x = jnp.concatenate(x, axis=0).astype(BF16)
        for c in range(3):
            first_ref[c, row + 1] = turn(x, 1 - c)

    def layer(source, weights, at):
        parts = []
        for start in (at, at + ROWS // 2):
            for c in range(3):
                count = BLOCK + 2 if c < 2 else BLOCK + 4
                parts.append(source[c, start : start + count].reshape(16 * count, 128))
        x = jnp.concatenate(
            [jnp.concatenate(parts[0:3], axis=0), jnp.concatenate(parts[3:6], axis=0)], axis=1
        )
        return dot(weights[...], x)

    for source, weights, bias, target in (
        (first_ref, one_ref, biases[0], second_ref),
        (second_ref, two_ref, biases[1], third_ref),
    ):
        bias = jnp.concatenate([bias, bias], axis=1)
        ahead = layer(source, weights, 0)
        for at in range(0, ROWS // 2, BLOCK):
            total = ahead.reshape(BLOCK, 16, 256)
            if at + BLOCK < ROWS // 2:
                ahead = layer(source, weights, at + BLOCK)
            value = silu(total + bias[None]).astype(BF16).reshape(16 * BLOCK, 256)
            for part in range(2):
                start = at + ROWS // 2 * part + 1
                x = value[:, 128 * part : 128 * part + 128]
                for c in range(3):
                    target[c, start : start + BLOCK] = turn(x, 1 - c).reshape(BLOCK, 16, 128)

    bias = jnp.concatenate([biases[2], biases[2]], axis=1)
    ahead = layer(third_ref, three_ref, 0)
    for at in range(0, ROWS // 2, BLOCK):
        forcing = ahead.reshape(BLOCK, 8, 256) + bias[None]
        if at + BLOCK < ROWS // 2:
            ahead = layer(third_ref, three_ref, at + BLOCK)
        for part in range(2):
            for r in range(BLOCK):
                row = at + ROWS // 2 * part + r
                near = [min(max(row + d, 0), ROWS - 1) for d in (0, 1, -1)]
                q, north, south = [[rows_ref[i, half] for half in range(2)] for i in near]
                east = [turn(x, -1) for x in q]
                west = [turn(x, 1) for x in q]
                new = tendency(q, north, south, east, west)
                new[0] = new[0] + forcing[r, :, 128 * part : 128 * part + 128]
                ocean = 0.1 * mask_ref[row : row + 1, :].astype(F32)
                for half in range(2):
                    out_ref[row, half] = q[half] + ocean * new[half]


def main_pass(size, cells, mask, parameters):
    taps = pltpu.VMEM((3, ROWS + 4, 16, 128), BF16)
    block = jax.ShapeDtypeStruct
    return pl.pallas_call(
        functools.partial(main_kernel, size),
        out_shape=[
            *[block((ROWS, 2, 8, 128), F32)] * 2,
            block((6, 8, 128), F32),
            block((8, 128), F32),
            *[block((n, DEPTH), BF16) for n in (128, 128, 64)],
            *[block(shape, BF16) for shape in ((48, 256), (48, 256), (32, 256))],
            block((40, 128), F32),
        ],
        in_specs=[VMEM] * 8,
        out_specs=[VMEM] * 11,
        scratch_shapes=[
            pltpu.VMEM((2, 9, 16, 128), BF16),
            pltpu.VMEM((9, 8, 128), F32),
            *[taps] * 3,
        ],
        compiler_params=pltpu.CompilerParams(vmem_limit_bytes=LIMIT),
        cost_estimate=pl.CostEstimate(
            flops=150000000, bytes_accessed=1500000, transcendentals=300000
        ),
        name="main_pass",
    )(cells, mask, *parameters)


def taps(rows, count):
    blank = jnp.zeros_like(rows[0])
    result = []
    for c in range(3):
        for row in rows:
            width = row.shape[1] // 128
            parts = [turn(row[:, 128 * i : 128 * i + 128], 1 - c) for i in range(width)]
            result.append(jnp.concatenate(parts, axis=1) if width > 1 else parts[0])
        result.extend([blank] * ((BLOCK + 2 if c < 2 else BLOCK + 4) - len(rows)))
    return jnp.concatenate(result, axis=0)


def strip_kernel(
    rows_ref, strip_ref, outer_ref, inner_ref, main_ref, ocean_ref, one_ref, two_ref, three_ref,
    bias_ref, cells_ref, low_ref, high_ref, side_ref, pre_one_ref, pre_two_ref, pre_three_ref,
):
    east, west = sides(inner_ref, outer_ref)
    col = lanes()
    at = col % 16
    cells = []
    for r in range(8):
        pair = [[], []]
        for half in range(2):
            block = 2 * (r // 4) + half
            own = strip_ref[r, half]
            pair[0].append(jnp.where(at < 6, own, turn(east[block], 6 - 4 * (r % 4))))
            pair[1].append(jnp.where(at < 3, turn(west[block], -4 * (r % 4)), turn(own, -3)))
        cells.append(pair)

    def own(row):
        start = 16 * (row // 8) + 4 * (row % 4)
        block = 2 * (row % 8 // 4)
        return [beside(east[block + h], start, west[block + h], start) for h in range(2)]

    low, high = [], []
    for row in list(range(6)) + list(range(ROWS - 6, ROWS)):
        side = own(row)
        slot = row if row < 3 else row - ROWS + 6
        if row < 3 or row >= ROWS - 3:
            for half in range(2):
                side_ref[slot, half] = side[half]
        parts = [
            jnp.concatenate([rows_ref[row, 0], rows_ref[row, 1]], axis=0),
            jnp.concatenate(side, axis=0),
        ]
        (low if row < 6 else high).append(jnp.concatenate(parts, axis=1).astype(BF16))
    def moved(pair, by):
        return [[turn(x, by) for x in part] for part in pair]

    cells = [moved(x, 16) for x in cells[5:8]] + cells + [moved(x, -16) for x in cells[0:3]]
    rows = []
    for pair in cells:
        parts = [jnp.concatenate(part, axis=0) for part in pair]
        rows.append(jnp.concatenate(parts, axis=1).astype(BF16))

    blank = jnp.zeros((16, 256), BF16)
    for weights, count, bias_at, pre_ref, width in (
        (one_ref, 7, 0, pre_one_ref, 256),
        (two_ref, 5, 16, pre_two_ref, 256),
        (three_ref, 3, 32, pre_three_ref, 128),
    ):
        n = weights.shape[0] // BLOCK
        more = len(rows) - 2 - BLOCK
        first = dot(weights[...], taps(rows[0:10], 256)).reshape(BLOCK, n, 256)
        if more > 0:
            second = dot(weights[0 : n * more, :], taps(rows[BLOCK:], 256)).reshape(more, n, 256)
        pairs = zip([blank] * 3 + low, high + [blank] * 3)
        operand = spread([jnp.concatenate(pair, axis=1) for pair in pairs], width)
        total = dot(weights[0 : (count + count % 2) * n, :], operand).reshape(-1, n, 2 * width)
        bias = bias_ref[bias_at : bias_at + n, :]
        first = first + jnp.concatenate([bias] * 2, axis=1)[None]
        if more > 0:
            second = second + jnp.concatenate([bias] * 2, axis=1)[None]
            rows = [silu(first[i]).astype(BF16) for i in range(BLOCK)]
            rows = rows + [silu(second[i]).astype(BF16) for i in range(more)]
        total = total + jnp.concatenate([bias] * (width // 64), axis=1)[None]
        for r in range(3):
            parts = [total[r, :, 0:width], total[count - 3 + r, :, width : 2 * width]]
            pre_ref[r] = jnp.concatenate(parts, axis=1)
        low = [silu(total[r, :, 0:width]).astype(BF16) for r in range(3, count)]
        high = [silu(total[r, :, width : 2 * width]).astype(BF16) for r in range(count - 3)]
    forcing = first

    both = []
    for r in range(8):
        new = []
        for part in range(2):
            q, north, south = [cells[i][part] for i in (r + 3, r + 4, r + 2)]
            value = tendency(
                q, north, south, [turn(x, -1) for x in q], [turn(x, 1) for x in q]
            )
            value[0] = value[0] + forcing[r, :, 128 * part : 128 * part + 128]
            new.append(value)
        ocean = ocean_ref[r : r + 1, :]
        value = [jnp.where(at < 6, new[0][half], turn(new[1][half], 3)) for half in range(2)]
        both.append([strip_ref[r, half] + ocean * value[half] for half in range(2)])

    edge = (col < 3) | (col >= 125)
    for b in range(8):
        ref, start = (low_ref, 0) if b == 0 else (high_ref, 0) if b == 7 else (cells_ref, 8 * b - 8)
        pitch = ref.shape[1]
        flat = ref.reshape(16 * pitch, 128)
        for r in range(8):
            for half in range(2):
                value = turn(both[r][half], -(16 * b + 6))
                value = jnp.where(edge, value, main_ref[8 * b + r, half])
                flat[pl.ds(8 * pitch * half + start + r, 8, stride=pitch), :] = value


def strip_pass(rows, strip, inner, outer, main, ocean, weights, bias):
    block = jax.ShapeDtypeStruct
    return pl.pallas_call(
        strip_kernel,
        out_shape=[
            block((16, ROWS - 8, 128), F32),
            *[block((16, 8, 128), F32)] * 2,
            block((6, 2, 8, 128), F32),
            *[block(shape, F32) for shape in ((3, 16, 512), (3, 16, 512), (3, 8, 256))],
        ],
        in_specs=[VMEM] * 10,
        out_specs=[VMEM] * 7,
        compiler_params=pltpu.CompilerParams(vmem_limit_bytes=LIMIT),
        cost_estimate=pl.CostEstimate(
            flops=150000000, bytes_accessed=2000000, transcendentals=100000
        ),
        name="strip_pass",
    )(rows, strip, outer, inner, main, ocean, *weights, bias)


def north_early(lat, size):
    return (lat == size - 2) & (lat % 2 == 0)


def join(parts):
    return jnp.concatenate(parts, axis=-1) if len(parts) > 1 else parts[0]


def received(strip, near_ref, far_ref, near, lat):
    halves, wide = [], []
    for t in range(3):
        main, side = [], []
        for half in range(2):
            at = 2 * t + half
            x, corner = near_ref[at], near_ref[6]
            if far_ref is not None:
                x = jnp.where(near, x, far_ref[at])
                corner = jnp.where(near, corner, far_ref[6])
            y = beside(corner, 32 * half + 4 * t + 4 * (1 - strip), corner, 32 * half + 16 + 4 * t + 4 * (1 - strip))
            if strip == 0:
                x, y = jnp.where(lat == 0, 0.0, x), jnp.where(lat == 0, 0.0, y)
            main.append(x)
            side.append(y)
        halves.append(main)
        parts = [jnp.concatenate(main, axis=0), jnp.concatenate(side, axis=0)]
        wide.append(jnp.concatenate(parts, axis=1).astype(BF16))
    return halves, wide


def complete(strips, rows, rows_ref, mask_ref, side_ref, pre, weights, blocks, out_ref, sems):
    def late(weights, wide, width):
        blank = [jnp.zeros((16, width), BF16)] * 2
        operand = []
        for c in range(3):
            columns = []
            for strip in strips:
                x = [turn_wide(row, c)[:, 0:width] for row in wide[strip]]
                columns.append(x + blank if strip == 0 else blank + x)
            operand.extend(join(parts) for parts in zip(*columns))
        operand.append(jnp.zeros((16, width * len(strips)), BF16))
        return dot(weights[...], jnp.concatenate(operand, axis=0))

    def shares(pre_ref, width):
        return join([pre_ref[:, :, width * strip : width * strip + width] for strip in strips])

    total = late(weights[0], {strip: rows[strip][1] for strip in strips}, 256)

    col = lanes()
    ready = {}
    for strip in strips:
        source, target = blocks[strip]
        target[...] = source[...]
        for t in range(3):
            row = t if strip == 0 else ROWS - 3 + t
            near = {i: [rows_ref[i, half] for half in range(2)] for i in (row - 1, row, row + 1) if 0 <= i < ROWS}
            near[-1], near[ROWS] = rows[strip][0][2], rows[strip][0][0]
            q = near[row]
            side = [side_ref[3 * strip + t, half] for half in range(2)]
            e = [turn(jnp.where(col == 0, y, x), -1) for x, y in zip(q, side)]
            w = [turn(jnp.where(col == 127, y, x), 1) for x, y in zip(q, side)]
            new = tendency(q, near[row + 1], near[row - 1], e, w)
            ocean = 0.1 * mask_ref[row : row + 1, :].astype(F32)
            ready[strip, t] = (q[0] + ocean * new[0], q[1] + ocean * new[1], ocean)

    for layer_at, width in ((0, 256), (1, 128)):
        value = total.reshape(3, 16, 256 * len(strips)) + shares(pre[layer_at], 256)
        value = silu(value).astype(BF16)
        wide = {
            strip: [value[r, :, 256 * i : 256 * i + 256] for r in range(3)]
            for i, strip in enumerate(strips)
        }
        total = late(weights[layer_at + 1], wide, width)
    total = total.reshape(4, 8, 128 * len(strips))[0:3] + shares(pre[2], 128)

    stores = []
    for i, strip in enumerate(strips):
        ref, at, start = (blocks[strip][1], 0, 0) if strip == 0 else (blocks[strip][1], ROWS - 8, 5)
        flat = ref.reshape(128, 128)
        for t in range(3):
            first, second, ocean = ready[strip, t]
            new = (first + ocean * total[t, :, 128 * i : 128 * i + 128], second)
            row = start + t
            for half in range(2):
                flat[pl.ds(64 * half + row, 8, stride=8), :] = new[half]
        store = pltpu.make_async_copy(ref, out_ref.at[:, pl.ds(at, 8), :], sems.at[1 + strip])
        store.start()
        stores.append(store)
    return stores


def copy_middle(cells_ref, out_ref, sem):
    source = cells_ref.at[:, pl.ds(0, ROWS - 16), :]
    return pltpu.make_async_copy(source, out_ref.at[:, pl.ds(8, ROWS - 16), :], sem)


def border_kernel(size, last, *refs):
    rows_ref, mask_ref, first_ref, *refs = refs
    if last:
        second_ref, *refs = refs
    side_ref, *refs = refs
    pre, weights, refs = refs[0:3], refs[3:6], refs[6:]
    cells_ref, low_in_ref, high_in_ref, *refs = refs
    out_ref, low_ref, high_ref, sems = refs[1:] if last else refs
    lat = lax.axis_index("lat")
    even = lat % 2 == 0
    early = north_early(lat, size)
    blocks = ((low_in_ref, low_ref), (high_in_ref, high_ref))

    def run(strips, middle, rows):
        stores = []
        if middle:
            stores.append(copy_middle(cells_ref, out_ref, sems.at[0]))
            stores[0].start()
        stores += complete(
            strips, rows, rows_ref, mask_ref, side_ref, pre, weights, blocks, out_ref, sems
        )
        for store in stores:
            store.wait()

    if not last:

        @pl.when(early)
        def _():
            run((1,), True, {1: received(1, first_ref, None, even, lat)})

        return

    @pl.when(early)
    def _():
        run((0,), False, {0: received(0, second_ref, None, even, lat)})

    @pl.when(jnp.logical_not(early))
    def _():
        low = received(0, second_ref, first_ref, even, lat)
        run((0, 1), True, {0: low, 1: received(1, first_ref, second_ref, even, lat)})


def border_pass(size, rows, mask, messages, side, pre, late, cells, low, high, out=()):
    last = len(out) > 0
    operands = (rows, mask, *messages, side, *pre, *late, cells, low, high)
    return pl.pallas_call(
        functools.partial(border_kernel, size, last),
        out_shape=jax.ShapeDtypeStruct((16, ROWS, 128), F32),
        in_specs=[VMEM] * len(operands) + [HBM] * len(out),
        out_specs=HBM,
        input_output_aliases={len(operands): 0} if last else {},
        scratch_shapes=[
            pltpu.VMEM(low.shape, F32),
            pltpu.VMEM(high.shape, F32),
            pltpu.SemaphoreType.DMA((3,)),
        ],
        compiler_params=pltpu.CompilerParams(vmem_limit_bytes=LIMIT),
        cost_estimate=pl.CostEstimate(flops=60000000, bytes_accessed=1000000, transcendentals=60000),
        name="border_pass" if last else "north_strip",
    )(*operands, *out)


def shards(state, land_mask, kernel_one, bias_one, kernel_two, bias_two, kernel_three, bias_three):
    lon, lat = (lax.axis_size("lon"), lax.axis_size("lat"))
    biases = [x.reshape(1, x.shape[0]) for x in (bias_one, bias_two, bias_three)]
    cells, strip, outer, inner, *biases = prepare(state, biases)
    parameters = (kernel_one, kernel_two, kernel_three, *biases)

    inner = lax.ppermute(inner, "lon", [(i, i + 1 - 2 * (i % 2)) for i in range(lon)])
    outer = lax.ppermute(outer, "lon", [(i, (i + 1 if i % 2 else i - 1) % lon) for i in range(lon)])
    rows, main, north, ocean, *weights, bias = main_pass(lat, cells, land_mask, parameters)
    weights, late = weights[0:3], weights[3:6]

    def pairs(parity):
        result = []
        for i in range(lon):
            for j in range(parity, lat - 1, 2):
                result += [(i * lat + j, i * lat + j + 1), (i * lat + j + 1, i * lat + j)]
            if parity == 1:
                result.append((i * lat, (i + 1 - 2 * (i % 2)) * lat))
            if (lat - 1) % 2 == parity:
                result.append((i * lat + lat - 1, (lon - 1 - i) * lat + lat - 1))
        return result

    first, second = corners(lat, rows, inner, outer, north)
    first = lax.ppermute(first, ("lon", "lat"), pairs(0))
    second = lax.ppermute(second, ("lon", "lat"), pairs(1))
    cells, low, high, side, *pre = strip_pass(
        rows, strip, inner, outer, main, ocean, weights, bias
    )
    held = (side, pre, late, cells, low, high)
    out = border_pass(lat, rows, land_mask, (first,), *held)
    return border_pass(lat, rows, land_mask, (first, second), *held, (out,))


def solution(mesh):
    return jax.shard_map(
        shards,
        mesh=mesh,
        in_specs=(P(None, "lat", "lon"), P("lat", "lon"), P(), P(), P(), P(), P(), P()),
        out_specs=P(None, "lat", "lon"),
        check_vma=False,
    )
```

```python
import functools

import jax
import jax.numpy as jnp
from jax import lax
from jax.experimental import pallas as pl
from jax.experimental.pallas import tpu as pltpu
from jax.sharding import PartitionSpec as P

F32 = jnp.float32
BF16 = jnp.bfloat16

ROWS = 64
PITCH = 72
BLOCK = 8
DEPTH = 512
SPAN = (BLOCK + 2) * 16
VMEM = pl.BlockSpec(memory_space=pltpu.VMEM)
HBM = pl.BlockSpec(memory_space=pltpu.HBM)
LIMIT = 40 * 2**20


def lanes():
    return lax.broadcasted_iota(jnp.int32, (8, 128), 1)


def turn(x, by):
    if isinstance(by, int):
        by = by % 128
        if by == 0:
            return x
    return pltpu.roll(x, by, x.ndim - 1)


def silu(v):
    half = 0.5 * v
    return half + half * jnp.tanh(half)


def dot(weights, x):
    return jnp.dot(weights, x, preferred_element_type=F32)


def even_place(axis):
    return lax.rem(lax.axis_index(axis), 2) == 0


def sides(inner, outer):
    even = even_place("lon")
    return (
        [jnp.where(even, inner[i], outer[i]) for i in range(4)],
        [jnp.where(even, outer[i], inner[i]) for i in range(4)],
    )


def tendency(q, north, south, east, west):
    sub = lax.broadcasted_iota(jnp.int32, (8, 128), 0)
    swapped = pltpu.roll(q[0], 4, 0)
    u = jnp.where(sub < 4, q[0], swapped)
    v = jnp.where(sub < 4, swapped, q[0])
    result = []
    for e, w, n, s, x in zip(east, west, north, south, q):
        total = -0.5 * (u * (e - w) + v * (n - s))
        result.append(total + 0.2 * (e + w + n + s - 4.0 * x))
    return result


def beside(e, e_at, w, w_at):
    return jnp.where(lanes() < 64, turn(e, -e_at), turn(w, 125 - w_at))


def turn_wide(x, c):
    return pltpu.roll(x, (1 - c) % 256, 1) if c != 1 else x


def spread(rows, width):
    blank = jnp.zeros((16, 2 * width), BF16)
    result = []
    for c in range(3):
        for row in rows:
            parts = [turn_wide(row[:, at : at + 256], c)[:, 0:width] for at in (0, 256)]
            result.append(jnp.concatenate(parts, axis=1))
        result.extend([blank] * ((BLOCK + 2 if c < 2 else BLOCK + 4) - len(rows)))
    return jnp.concatenate(result, axis=0)


def prepare_kernel(
    state_ref, b_one_ref, b_two_ref, b_three_ref,
    cells_ref, strip_ref, outer_ref, inner_ref, h_one_ref, h_two_ref, h_three_ref, sems,
):
    image = cells_ref.at[:, pl.ds(0, ROWS), :]
    fetches = [pltpu.make_async_copy(state_ref, image, sems.at[0])]
    biases = ((b_one_ref, h_one_ref), (b_two_ref, h_two_ref), (b_three_ref, h_three_ref))
    for source, target in biases:
        fetches.append(pltpu.make_async_copy(source, target, sems.at[len(fetches)]))
    for fetch in fetches:
        fetch.start()

    flat = cells_ref.reshape(16 * PITCH, 128)
    group = lanes() // 16
    part = (lanes() % 16) // 4
    even = even_place("lon")
    shifts = [
        [jnp.where(even, (4 * s - a) % 128, (4 * s - b) % 128) for s in range(4)]
        for a, b in ((6, 3), (3, 6))
    ]
    fetches[0].wait()
    strip = [[jnp.zeros((8, 128), F32)] * 8 for half in range(2)]
    for b in range(8):
        for half in range(2):
            for r in range(8):
                x = flat[pl.ds(8 * PITCH * half + 8 * b + r, 8, stride=PITCH), :]
                strip[half][r] = jnp.where(group == b, turn(x, 6 + 16 * b), strip[half][r])
    for target, shift in zip((outer_ref, inner_ref), shifts):
        for q in range(2):
            for half in range(2):
                value = jnp.zeros((8, 128), F32)
                for s in range(4):
                    value = jnp.where(part == s, turn(strip[half][4 * q + s], shift[s]), value)
                target[2 * q + half] = value
    for half in range(2):
        for r in range(8):
            strip_ref[r, half] = strip[half][r]
    for fetch in fetches[1:]:
        fetch.wait()


def prepare(state, biases):
    block = jax.ShapeDtypeStruct
    arrays = [pltpu.with_memory_space_constraint(x, pltpu.HBM) for x in (state, *biases)]
    return pl.pallas_call(
        prepare_kernel,
        out_shape=[
            block((16, PITCH, 128), F32),
            block((8, 2, 8, 128), F32),
            block((4, 8, 128), F32),
            block((4, 8, 128), F32),
            *[block(x.shape, F32) for x in biases],
        ],
        in_specs=[HBM] * 4,
        out_specs=[VMEM] * 7,
        scratch_shapes=[pltpu.SemaphoreType.DMA((4,))],
        compiler_params=pltpu.CompilerParams(vmem_limit_bytes=LIMIT),
        cost_estimate=pl.CostEstimate(flops=400000, bytes_accessed=1200000, transcendentals=0),
        name="rows_edges",
    )(*arrays)


def corners_kernel(size, rows_ref, outer_ref, inner_ref, north_ref, first_ref, second_ref):
    lat = lax.axis_index("lat")
    even = lax.rem(lat, 2) == 0
    for t in range(3):
        for half in range(2):
            at = 2 * t + half
            low = rows_ref[t, half]
            first_ref[at] = jnp.where(even, north_ref[at], low)
            second_ref[at] = jnp.where(even, low, north_ref[at])
    top = lat == size - 1
    col = lanes()
    part = col // 16
    straight = even_place("lon")
    mirrored = straight != top
    index = jnp.where(top, 112 + 4 * (3 - col // 4 % 4) + 2 - col % 4, 112 + col % 16)
    low = high = jnp.zeros((8, 128), F32)
    for i in range(4):
        half = i // 2
        pair = (inner_ref, outer_ref) if i % 2 == 0 else (outer_ref, inner_ref)
        x = jnp.where(straight, pair[0][half], pair[1][half])
        low = jnp.where(part == i, turn(x, 16 * i), low)
        x = jnp.where(mirrored, pair[0][2 + half], pair[1][2 + half])
        high = jnp.where(part == i, jnp.take_along_axis(x, index, axis=1), high)
    high = jnp.where(top & (col < 32), -high, high)
    first_ref[6] = jnp.where(even, high, low)
    second_ref[6] = jnp.where(even, low, high)


def corners(size, rows, inner, outer, north):
    return pl.pallas_call(
        functools.partial(corners_kernel, size),
        out_shape=[jax.ShapeDtypeStruct((7, 8, 128), F32)] * 2,
        in_specs=[VMEM] * 4,
        out_specs=[VMEM] * 2,
        compiler_params=pltpu.CompilerParams(vmem_limit_bytes=LIMIT),
        cost_estimate=pl.CostEstimate(flops=1000, bytes_accessed=100000, transcendentals=0),
        name="add_corners",
    )(rows, outer, inner, north)


def band(kernel_ref, wide_ref, target_ref):
    n = kernel_ref.shape[2]
    wide_ref[...] = jnp.zeros_like(wide_ref)
    tiles = [None] * (DEPTH // 128)
    for c in range(3):
        for a in range(3):
            wide_ref[3 * c + a, :, 0:16] = kernel_ref[a, c].astype(wide_ref.dtype)
            tile, off = divmod(SPAN * c + 16 * a, 128)
            x = turn(wide_ref[3 * c + a], off)
            tiles[tile] = x if tiles[tile] is None else tiles[tile] + x
    blank = jnp.zeros((n, 128), wide_ref.dtype)
    first = jnp.concatenate([blank if x is None else x for x in tiles], axis=1)
    rows = [first] + [pltpu.roll(first, 16 * r, 1) for r in range(1, BLOCK)]
    for r in range(0, BLOCK, 16 // n):
        target_ref[n * r : n * r + 16, :] = jnp.concatenate(rows[r : r + 16 // n], axis=0).astype(BF16)


def band_compact(wide_ref, target_ref, slots, outs):
    n = wide_ref.shape[1]
    tiles = [jnp.zeros((n, 128), wide_ref.dtype)] * (target_ref.shape[1] // 128)
    for c in range(3):
        for a in range(3):
            tile, off = divmod(16 * slots * c + 16 * a, 128)
            tiles[tile] = tiles[tile] + turn(wide_ref[3 * c + a], off)
    first = jnp.concatenate(tiles, axis=1)
    rows = [pltpu.roll(first, 16 * r, 1) if r else first for r in range(outs)]
    rows = rows + [jnp.zeros_like(first)] * (target_ref.shape[0] // n - outs)
    for r in range(0, len(rows), 16 // n):
        target_ref[n * r : n * r + 16, :] = jnp.concatenate(rows[r : r + 16 // n], axis=0).astype(BF16)


def main_kernel(
    size, cells_ref, mask_ref, k_one_ref, k_two_ref, k_three_ref, b_one_ref, b_two_ref, b_three_ref,
    rows_ref, out_ref, north_ref, ocean_ref, one_ref, two_ref, three_ref,
    late_one_ref, late_two_ref, late_three_ref, bias_ref,
    wide_ref, narrow_ref, first_ref, second_ref, third_ref,
):
    flat = cells_ref.reshape(16 * PITCH, 128)

    def load(row, half):
        return flat[pl.ds(8 * PITCH * half + row, 8, stride=PITCH), :]

    top = lax.axis_index("lat") == size - 1
    col = lanes()
    for t in range(3):
        for half in range(2):
            folded = jnp.take_along_axis(load(ROWS - 1 - t, half), 127 - col, axis=1)
            folded = -folded if half == 0 else folded
            north_ref[2 * t + half] = jnp.where(top, folded, load(ROWS - 3 + t, half))
    ocean = jnp.zeros((8, 128), F32)
    for b in range(8):
        x = 0.1 * mask_ref[8 * b : 8 * b + 8, :].astype(F32)
        ocean = jnp.where(col // 16 == b, turn(x, 6 + 16 * b), ocean)
    ocean_ref[...] = ocean

    biases = []
    at = 0
    for ref in (b_one_ref, b_two_ref, b_three_ref):
        n = ref.shape[1]
        same = lax.broadcasted_iota(jnp.int32, (n, n), 0) == lax.broadcasted_iota(jnp.int32, (n, n), 1)
        column = jnp.sum(jnp.where(same, ref[...], 0.0), axis=1, keepdims=True)
        biases.append(jnp.broadcast_to(column, (n, 128)))
        bias_ref[at : at + n, :] = biases[-1]
        at += n
    band(k_one_ref, wide_ref.at[0], one_ref)
    band(k_two_ref, wide_ref.at[1], two_ref)
    band(k_three_ref, narrow_ref, three_ref)
    band_compact(wide_ref.at[0], late_one_ref, 5, 3)
    band_compact(wide_ref.at[1], late_two_ref, 5, 3)
    band_compact(narrow_ref, late_three_ref, 5, 3)
    for ref in (first_ref, second_ref, third_ref):
        for c in range(3):
            for row in (0, ROWS + 1, ROWS + 2, ROWS + 3):
                ref[c, row] = jnp.zeros((16, 128), BF16)

    for row in range(ROWS):
        x = [load(row, half) for half in range(2)]
        for half in range(2):
            rows_ref[row, half] = x[half]
        x = jnp.concatenate(x, axis=0).astype(BF16)
        for c in range(3):
            first_ref[c, row + 1] = turn(x, 1 - c)

    def layer(source, weights, at):
        parts = []
        for start in (at, at + ROWS // 2):
            for c in range(3):
                count = BLOCK + 2 if c < 2 else BLOCK + 4
                parts.append(source[c, start : start + count].reshape(16 * count, 128))
        x = jnp.concatenate(
            [jnp.concatenate(parts[0:3], axis=0), jnp.concatenate(parts[3:6], axis=0)], axis=1
        )
        return dot(weights[...], x)

    for source, weights, bias, target in (
        (first_ref, one_ref, biases[0], second_ref),
        (second_ref, two_ref, biases[1], third_ref),
    ):
        bias = jnp.concatenate([bias, bias], axis=1)
        ahead = layer(source, weights, 0)
        for at in range(0, ROWS // 2, BLOCK):
            total = ahead.reshape(BLOCK, 16, 256)
            if at + BLOCK < ROWS // 2:
                ahead = layer(source, weights, at + BLOCK)
            value = silu(total + bias[None]).astype(BF16).reshape(16 * BLOCK, 256)
            for part in range(2):
                start = at + ROWS // 2 * part + 1
                x = value[:, 128 * part : 128 * part + 128]
                for c in range(3):
                    target[c, start : start + BLOCK] = turn(x, 1 - c).reshape(BLOCK, 16, 128)

    bias = jnp.concatenate([biases[2], biases[2]], axis=1)
    ahead = layer(third_ref, three_ref, 0)
    for at in range(0, ROWS // 2, BLOCK):
        forcing = ahead.reshape(BLOCK, 8, 256) + bias[None]
        if at + BLOCK < ROWS // 2:
            ahead = layer(third_ref, three_ref, at + BLOCK)
        for part in range(2):
            for r in range(BLOCK):
                row = at + ROWS // 2 * part + r
                near = [min(max(row + d, 0), ROWS - 1) for d in (0, 1, -1)]
                q, north, south = [[rows_ref[i, half] for half in range(2)] for i in near]
                east = [turn(x, -1) for x in q]
                west = [turn(x, 1) for x in q]
                new = tendency(q, north, south, east, west)
                new[0] = new[0] + forcing[r, :, 128 * part : 128 * part + 128]
                ocean = 0.1 * mask_ref[row : row + 1, :].astype(F32)
                for half in range(2):
                    out_ref[row, half] = q[half] + ocean * new[half]


def main_pass(size, cells, mask, parameters):
    taps = pltpu.VMEM((3, ROWS + 4, 16, 128), BF16)
    block = jax.ShapeDtypeStruct
    return pl.pallas_call(
        functools.partial(main_kernel, size),
        out_shape=[
            *[block((ROWS, 2, 8, 128), F32)] * 2,
            block((6, 8, 128), F32),
            block((8, 128), F32),
            *[block((n, DEPTH), BF16) for n in (128, 128, 64)],
            *[block(shape, BF16) for shape in ((48, 256), (48, 256), (32, 256))],
            block((40, 128), F32),
        ],
        in_specs=[VMEM] * 8,
        out_specs=[VMEM] * 11,
        scratch_shapes=[
            pltpu.VMEM((2, 9, 16, 128), BF16),
            pltpu.VMEM((9, 8, 128), F32),
            *[taps] * 3,
        ],
        compiler_params=pltpu.CompilerParams(vmem_limit_bytes=LIMIT),
        cost_estimate=pl.CostEstimate(
            flops=150000000, bytes_accessed=1500000, transcendentals=300000
        ),
        name="main_pass",
    )(cells, mask, *parameters)


def taps(rows, count):
    blank = jnp.zeros_like(rows[0])
    result = []
    for c in range(3):
        for row in rows:
            width = row.shape[1] // 128
            parts = [turn(row[:, 128 * i : 128 * i + 128], 1 - c) for i in range(width)]
            result.append(jnp.concatenate(parts, axis=1) if width > 1 else parts[0])
        result.extend([blank] * ((BLOCK + 2 if c < 2 else BLOCK + 4) - len(rows)))
    return jnp.concatenate(result, axis=0)


def strip_kernel(
    rows_ref, strip_ref, outer_ref, inner_ref, main_ref, ocean_ref, one_ref, two_ref, three_ref,
    bias_ref, cells_ref, low_ref, high_ref, side_ref, pre_one_ref, pre_two_ref, pre_three_ref,
):
    east, west = sides(inner_ref, outer_ref)
    col = lanes()
    at = col % 16
    cells = []
    for r in range(8):
        pair = [[], []]
        for half in range(2):
            block = 2 * (r // 4) + half
            own = strip_ref[r, half]
            pair[0].append(jnp.where(at < 6, own, turn(east[block], 6 - 4 * (r % 4))))
            pair[1].append(jnp.where(at < 3, turn(west[block], -4 * (r % 4)), turn(own, -3)))
        cells.append(pair)

    def own(row):
        start = 16 * (row // 8) + 4 * (row % 4)
        block = 2 * (row % 8 // 4)
        return [beside(east[block + h], start, west[block + h], start) for h in range(2)]

    low, high = [], []
    for row in list(range(6)) + list(range(ROWS - 6, ROWS)):
        side = own(row)
        slot = row if row < 3 else row - ROWS + 6
        if row < 3 or row >= ROWS - 3:
            for half in range(2):
                side_ref[slot, half] = side[half]
        parts = [
            jnp.concatenate([rows_ref[row, 0], rows_ref[row, 1]], axis=0),
            jnp.concatenate(side, axis=0),
        ]
        (low if row < 6 else high).append(jnp.concatenate(parts, axis=1).astype(BF16))
    def moved(pair, by):
        return [[turn(x, by) for x in part] for part in pair]

    cells = [moved(x, 16) for x in cells[5:8]] + cells + [moved(x, -16) for x in cells[0:3]]
    rows = []
    for pair in cells:
        parts = [jnp.concatenate(part, axis=0) for part in pair]
        rows.append(jnp.concatenate(parts, axis=1).astype(BF16))

    blank = jnp.zeros((16, 256), BF16)
    for weights, count, bias_at, pre_ref, width in (
        (one_ref, 7, 0, pre_one_ref, 256),
        (two_ref, 5, 16, pre_two_ref, 256),
        (three_ref, 3, 32, pre_three_ref, 128),
    ):
        n = weights.shape[0] // BLOCK
        more = len(rows) - 2 - BLOCK
        first = dot(weights[...], taps(rows[0:10], 256)).reshape(BLOCK, n, 256)
        if more > 0:
            second = dot(weights[0 : n * more, :], taps(rows[BLOCK:], 256)).reshape(more, n, 256)
        pairs = zip([blank] * 3 + low, high + [blank] * 3)
        operand = spread([jnp.concatenate(pair, axis=1) for pair in pairs], width)
        total = dot(weights[0 : (count + count % 2) * n, :], operand).reshape(-1, n, 2 * width)
        bias = bias_ref[bias_at : bias_at + n, :]
        first = first + jnp.concatenate([bias] * 2, axis=1)[None]
        if more > 0:
            second = second + jnp.concatenate([bias] * 2, axis=1)[None]
            rows = [silu(first[i]).astype(BF16) for i in range(BLOCK)]
            rows = rows + [silu(second[i]).astype(BF16) for i in range(more)]
        total = total + jnp.concatenate([bias] * (width // 64), axis=1)[None]
        for r in range(3):
            parts = [total[r, :, 0:width], total[count - 3 + r, :, width : 2 * width]]
            pre_ref[r] = jnp.concatenate(parts, axis=1)
        low = [silu(total[r, :, 0:width]).astype(BF16) for r in range(3, count)]
        high = [silu(total[r, :, width : 2 * width]).astype(BF16) for r in range(count - 3)]
    forcing = first

    both = []
    for r in range(8):
        new = []
        for part in range(2):
            q, north, south = [cells[i][part] for i in (r + 3, r + 4, r + 2)]
            value = tendency(
                q, north, south, [turn(x, -1) for x in q], [turn(x, 1) for x in q]
            )
            value[0] = value[0] + forcing[r, :, 128 * part : 128 * part + 128]
            new.append(value)
        ocean = ocean_ref[r : r + 1, :]
        value = [jnp.where(at < 6, new[0][half], turn(new[1][half], 3)) for half in range(2)]
        both.append([strip_ref[r, half] + ocean * value[half] for half in range(2)])

    edge = (col < 3) | (col >= 125)
    for b in range(8):
        ref, start = (low_ref, 0) if b == 0 else (high_ref, 0) if b == 7 else (cells_ref, 8 * b - 8)
        pitch = ref.shape[1]
        flat = ref.reshape(16 * pitch, 128)
        for r in range(8):
            for half in range(2):
                value = turn(both[r][half], -(16 * b + 6))
                value = jnp.where(edge, value, main_ref[8 * b + r, half])
                flat[pl.ds(8 * pitch * half + start + r, 8, stride=pitch), :] = value


def strip_pass(rows, strip, inner, outer, main, ocean, weights, bias):
    block = jax.ShapeDtypeStruct
    return pl.pallas_call(
        strip_kernel,
        out_shape=[
            block((16, ROWS - 8, 128), F32),
            *[block((16, 8, 128), F32)] * 2,
            block((6, 2, 8, 128), F32),
            *[block(shape, F32) for shape in ((3, 16, 512), (3, 16, 512), (3, 8, 256))],
        ],
        in_specs=[VMEM] * 10,
        out_specs=[VMEM] * 7,
        compiler_params=pltpu.CompilerParams(vmem_limit_bytes=LIMIT),
        cost_estimate=pl.CostEstimate(
            flops=150000000, bytes_accessed=2000000, transcendentals=100000
        ),
        name="strip_pass",
    )(rows, strip, outer, inner, main, ocean, *weights, bias)


def north_early(lat, size):
    return (lat == size - 2) & (lat % 2 == 0)


def join(parts):
    return jnp.concatenate(parts, axis=-1) if len(parts) > 1 else parts[0]


def received(strip, near_ref, far_ref, near, lat):
    halves, wide = [], []
    for t in range(3):
        main, side = [], []
        for half in range(2):
            at = 2 * t + half
            x, corner = near_ref[at], near_ref[6]
            if far_ref is not None:
                x = jnp.where(near, x, far_ref[at])
                corner = jnp.where(near, corner, far_ref[6])
            y = beside(corner, 32 * half + 4 * t + 4 * (1 - strip), corner, 32 * half + 16 + 4 * t + 4 * (1 - strip))
            if strip == 0:
                x, y = jnp.where(lat == 0, 0.0, x), jnp.where(lat == 0, 0.0, y)
            main.append(x)
            side.append(y)
        halves.append(main)
        parts = [jnp.concatenate(main, axis=0), jnp.concatenate(side, axis=0)]
        wide.append(jnp.concatenate(parts, axis=1).astype(BF16))
    return halves, wide


def complete(strips, rows, rows_ref, mask_ref, side_ref, pre, weights, blocks, out_ref, sems):
    def late(weights, wide, width):
        blank = [jnp.zeros((16, width), BF16)] * 2
        operand = []
        for c in range(3):
            columns = []
            for strip in strips:
                x = [turn_wide(row, c)[:, 0:width] for row in wide[strip]]
                columns.append(x + blank if strip == 0 else blank + x)
            operand.extend(join(parts) for parts in zip(*columns))
        operand.append(jnp.zeros((16, width * len(strips)), BF16))
        return dot(weights[...], jnp.concatenate(operand, axis=0))

    def shares(pre_ref, width):
        return join([pre_ref[:, :, width * strip : width * strip + width] for strip in strips])

    total = late(weights[0], {strip: rows[strip][1] for strip in strips}, 256)

    col = lanes()
    ready = {}
    for strip in strips:
        source, target = blocks[strip]
        target[...] = source[...]
        for t in range(3):
            row = t if strip == 0 else ROWS - 3 + t
            near = {i: [rows_ref[i, half] for half in range(2)] for i in (row - 1, row, row + 1) if 0 <= i < ROWS}
            near[-1], near[ROWS] = rows[strip][0][2], rows[strip][0][0]
            q = near[row]
            side = [side_ref[3 * strip + t, half] for half in range(2)]
            e = [turn(jnp.where(col == 0, y, x), -1) for x, y in zip(q, side)]
            w = [turn(jnp.where(col == 127, y, x), 1) for x, y in zip(q, side)]
            new = tendency(q, near[row + 1], near[row - 1], e, w)
            ocean = 0.1 * mask_ref[row : row + 1, :].astype(F32)
            ready[strip, t] = (q[0] + ocean * new[0], q[1] + ocean * new[1], ocean)

    for layer_at, width in ((0, 256), (1, 128)):
        value = total.reshape(3, 16, 256 * len(strips)) + shares(pre[layer_at], 256)
        value = silu(value).astype(BF16)
        wide = {
            strip: [value[r, :, 256 * i : 256 * i + 256] for r in range(3)]
            for i, strip in enumerate(strips)
        }
        total = late(weights[layer_at + 1], wide, width)
    total = total.reshape(4, 8, 128 * len(strips))[0:3] + shares(pre[2], 128)

    stores = []
    for i, strip in enumerate(strips):
        ref, at, start = (blocks[strip][1], 0, 0) if strip == 0 else (blocks[strip][1], ROWS - 8, 5)
        flat = ref.reshape(128, 128)
        for t in range(3):
            first, second, ocean = ready[strip, t]
            new = (first + ocean * total[t, :, 128 * i : 128 * i + 128], second)
            row = start + t
            for half in range(2):
                flat[pl.ds(64 * half + row, 8, stride=8), :] = new[half]
        store = pltpu.make_async_copy(ref, out_ref.at[:, pl.ds(at, 8), :], sems.at[1 + strip])
        store.start()
        stores.append(store)
    return stores


def copy_middle(cells_ref, out_ref, sem):
    source = cells_ref.at[:, pl.ds(0, ROWS - 16), :]
    return pltpu.make_async_copy(source, out_ref.at[:, pl.ds(8, ROWS - 16), :], sem)


def border_kernel(size, last, *refs):
    rows_ref, mask_ref, first_ref, *refs = refs
    if last:
        second_ref, *refs = refs
    side_ref, *refs = refs
    pre, weights, refs = refs[0:3], refs[3:6], refs[6:]
    cells_ref, low_in_ref, high_in_ref, *refs = refs
    out_ref, low_ref, high_ref, sems = refs[1:] if last else refs
    lat = lax.axis_index("lat")
    even = lat % 2 == 0
    early = north_early(lat, size)
    blocks = ((low_in_ref, low_ref), (high_in_ref, high_ref))

    def run(strips, middle, rows):
        stores = []
        if middle:
            stores.append(copy_middle(cells_ref, out_ref, sems.at[0]))
            stores[0].start()
        stores += complete(
            strips, rows, rows_ref, mask_ref, side_ref, pre, weights, blocks, out_ref, sems
        )
        for store in stores:
            store.wait()

    if not last:

        @pl.when(early)
        def _():
            run((1,), True, {1: received(1, first_ref, None, even, lat)})

        return

    @pl.when(early)
    def _():
        run((0,), False, {0: received(0, second_ref, None, even, lat)})

    @pl.when(jnp.logical_not(early))
    def _():
        low = received(0, second_ref, first_ref, even, lat)
        run((0, 1), True, {0: low, 1: received(1, first_ref, second_ref, even, lat)})


def border_pass(size, rows, mask, messages, side, pre, late, cells, low, high, out=()):
    last = len(out) > 0
    operands = (rows, mask, *messages, side, *pre, *late, cells, low, high)
    return pl.pallas_call(
        functools.partial(border_kernel, size, last),
        out_shape=jax.ShapeDtypeStruct((16, ROWS, 128), F32),
        in_specs=[VMEM] * len(operands) + [HBM] * len(out),
        out_specs=HBM,
        input_output_aliases={len(operands): 0} if last else {},
        scratch_shapes=[
            pltpu.VMEM(low.shape, F32),
            pltpu.VMEM(high.shape, F32),
            pltpu.SemaphoreType.DMA((3,)),
        ],
        compiler_params=pltpu.CompilerParams(vmem_limit_bytes=LIMIT),
        cost_estimate=pl.CostEstimate(flops=60000000, bytes_accessed=1000000, transcendentals=60000),
        name="border_pass" if last else "north_strip",
    )(*operands, *out)


def shards(state, land_mask, kernel_one, bias_one, kernel_two, bias_two, kernel_three, bias_three):
    lon, lat = (lax.axis_size("lon"), lax.axis_size("lat"))
    biases = [x.reshape(1, x.shape[0]) for x in (bias_one, bias_two, bias_three)]
    cells, strip, outer, inner, *biases = prepare(state, biases)
    parameters = (kernel_one, kernel_two, kernel_three, *biases)

    inner = lax.ppermute(inner, "lon", [(i, i + 1 - 2 * (i % 2)) for i in range(lon)])
    outer = lax.ppermute(outer, "lon", [(i, (i + 1 if i % 2 else i - 1) % lon) for i in range(lon)])
    rows, main, north, ocean, *weights, bias = main_pass(lat, cells, land_mask, parameters)
    weights, late = weights[0:3], weights[3:6]

    def pairs(parity):
        result = []
        for i in range(lon):
            for j in range(parity, lat - 1, 2):
                result += [(i * lat + j, i * lat + j + 1), (i * lat + j + 1, i * lat + j)]
            if parity == 1:
                result.append((i * lat, (i + 1 - 2 * (i % 2)) * lat))
            if (lat - 1) % 2 == parity:
                result.append((i * lat + lat - 1, (lon - 1 - i) * lat + lat - 1))
        return result

    first, second = corners(lat, rows, inner, outer, north)
    first = lax.ppermute(first, ("lon", "lat"), pairs(0))
    second = lax.ppermute(second, ("lon", "lat"), pairs(1))
    cells, low, high, side, *pre = strip_pass(
        rows, strip, inner, outer, main, ocean, weights, bias
    )
    held = (side, pre, late, cells, low, high)
    out = border_pass(lat, rows, land_mask, (first,), *held)
    return border_pass(lat, rows, land_mask, (first, second), *held, (out,))


def solution(mesh):
    return jax.shard_map(
        shards,
        mesh=mesh,
        in_specs=(P(None, "lat", "lon"), P("lat", "lon"), P(), P(), P(), P(), P(), P()),
        out_specs=P(None, "lat", "lon"),
        check_vma=False,
    )
```
